32 devices in a mesh: inst: 4 (over x, core), zone: 8 (over z, y).
Axes of the slice: x: 2, y: 2, z: 4, core: 2. Of those that a mesh axis runs over, the one named last changes fastest.
Arguments:
- state: float32 [4, 1024, 320], P('inst', 'zone'), may hold values from -6 to 6
- source: float32 [4, 1024, 320], P('inst', 'zone'), may hold values from -6 to 6
- jac_table: bfloat16 [64, 320, 320], P('zone'), may hold values from -0.3125 to 0.3125
- pattern_col: int32 [1024, 4], P('zone'), may hold values from 0 to 127
- pattern_type: int32 [1024, 4], P('zone'), may hold values from 0 to 7
- pseudo_step: float32 [4, 1024], P('inst', 'zone'), may hold values from 0.05 to 0.4
- zone_count: int32 [8], P('zone'), may hold values from 64 to 128, as said below
- link_src: int32 [4, 256], P('inst', 'zone'), may hold values from 0 to 127
- link_owner: int32 [4, 256, 1], P('inst', 'zone'), may hold values from 0 to 7; in each aligned block of 32 rows (0 to 31, 32 to 63, ..., all dimensions but the last counted through in order) at most 8 rows name the same one
- link_dest: int32 [4, 256], P('inst', 'zone'), may hold values from 0 to 127
- link_weight: int32 [4, 256], P('inst', 'zone'), may hold values from 0 to 15
- iface_table: float32 [16, 320], replicated, may hold values from 0.5 to 1.5
Outputs:
- updated: float32 [4, 1024, 320], P('inst', 'zone')
- residual: float32 [4, 1024, 320], P('inst', 'zone')
The draws below stay inside these ranges and needn't reach their ends.
Inputs may be any that keep to these rules, and one draw needn't show every extreme that they name: `link_owner`: among the 32 links of one zone at one instance, no owner zone is named more than 8 times; in some of them one zone is named exactly 8 times. `zone_count`: some zone uses all 128 clusters.
All inputs are finite; a program needn't handle non-finite values.
Results may differ from the reference program's by a relative error of at most 0.0014.
Values sent between devices are 32-bit elements; how exact they have to be, the bound alone decides.
No kernel may reach another device: no remote copies, remote signals or barrier semaphores. Data moves between devices by JAX's collectives and lax.ppermute only.
A program may use at most 64 MiB of HBM per device.

```python
import math
import jax
import jax.numpy as jnp
import numpy as np
from jax import lax

W = 320
NB = 8
K = 4
NWT = 16
CLZ = 128
NL = 32
NT = 4
ZC = 1024
CAP = 8
NLT = 256
N_ZONE = 8


def draw_zone_count(key, part):
    counts = jax.random.randint(key, (N_ZONE,), CLZ // 2, CLZ + 1)
    chosen = jax.random.randint(jax.random.fold_in(key, 7), (), 0, N_ZONE)
    return jnp.where(jnp.arange(N_ZONE) == chosen, CLZ, counts).astype(jnp.int32)


def with_ends(entries, rng, low, top_value):
    longest = entries.shape.index(max(entries.shape))
    spots = []
    for shift in (0, 1):
        where = [jax.random.randint(jax.random.fold_in(rng, axis), (), 0, length) for axis, length in enumerate(entries.shape)]
        where[longest] = (where[longest] + shift) % entries.shape[longest]
        spots.append(tuple(where))
    return entries.at[spots[0]].set(low).at[spots[1]].set(top_value)


def levels(own_key, extent, shards, low, largest):
    level, own = 1.0, jax.random.fold_in(own_key, 6)
    for position, parts in shards:
        draws = jnp.exp(jax.random.uniform(jax.random.fold_in(own, position), (parts,), jnp.float32, low / len(shards), largest / len(shards)))
        level = level * jnp.repeat(draws, extent[position] // parts).reshape([-1 if axis == position else 1 for axis in range(len(extent))])
    return level


def assign_block(key, own, number, rows, number_of, top, most, lean):
    order = jax.random.permutation(key, number_of)
    packed, common = shares(number_of, rows * top, most, lean, True), shares(number_of, rows * top, most, lean, False)
    places = jnp.arange(number_of)

    def named(tallies, rotation):
        used = int((tallies > 0).sum())
        fixed = max(1, used // 4)
        shifted = fixed + (places - fixed + rotation * (used - fixed)) % max(1, number_of - fixed)
        return jnp.zeros((number_of,), jnp.int32).at[order[jnp.where(places < fixed, places, shifted)]].set(jnp.asarray(tallies, jnp.int32))

    tallies = jnp.where(number % 4 == 0, named(packed, number // 4), named(common, number - number // 4 - 1))
    mixed = jax.random.permutation(jax.random.fold_in(own, 3), number_of)
    donor, taker = mixed[0:number_of // 2 * 2:2], mixed[1:number_of // 2 * 2:2]
    slack = jnp.minimum(tallies[donor] - 1, most - tallies[taker]) // 2
    slack = jnp.where((donor == order[0]) | (taker == order[0]) | (tallies[taker] == 0), 0, jnp.maximum(slack, 0))
    shifted = jax.random.randint(jax.random.fold_in(own, 4), (number_of // 2,), 0, 1 << 20) % (slack + 1)
    tallies = tallies.at[donor].add(-shifted).at[taker].add(shifted)
    members = jnp.searchsorted(jnp.cumsum(tallies), jnp.arange(rows * top), side="right").astype(jnp.int32)
    table = members.reshape(top, rows).T
    table = table[jax.random.permutation(jax.random.fold_in(own, 1), rows)]
    rotation = jax.random.randint(jax.random.fold_in(own, 2), (rows, 1), 0, top)
    return jnp.take_along_axis(table, (jnp.arange(top)[None, :] + rotation) % top, axis=1)


def shares(number_of, total, reach, lean, full):
    weights = [(1 << 20) // math.isqrt(rank ** lean) + 1 for rank in range(1, number_of + 1)]
    largest = reach if full else min(reach, max(-(-total // number_of), total * weights[0] // sum(weights)))
    least = 1 if total - largest >= number_of - 1 else 0
    holding, spare = [largest] + [least] * (number_of - 1), total - largest - least * (number_of - 1)
    while spare > 0:
        free = [i for i in range(1, number_of) if holding[i] < largest] or [i for i in range(1, number_of) if holding[i] < reach]
        mass, budget = sum([weights[i] for i in free]), spare
        for i in free:
            extra = min(reach - holding[i], max(1, budget * weights[i] // mass), spare)
            holding[i] = holding[i] + extra
            spare = spare - extra
    return np.array(holding)


def bell_draw(rng, extent, spread, most, pieces=(), held_as=jnp.bfloat16):
    drawn = spread * jax.random.normal(rng, extent, jnp.float32)
    if pieces:
        drawn = drawn * levels(rng, extent, pieces, -0.22, 0.18)
    return jnp.clip(drawn, -most, most).astype(held_as)


def setup_inputs(seed: int = 0) -> dict:
    arg_keys = jax.random.split(jax.random.key(seed), 13)
    state = bell_draw(arg_keys[0], (NT, ZC, W), 1.0, 6.0, ((0, 4), (1, 8)), jnp.float32)
    source = bell_draw(arg_keys[1], (NT, ZC, W), 1.0, 6.0, ((0, 4), (1, 8)), jnp.float32)
    jac_table = bell_draw(arg_keys[2], (N_ZONE * NB, W, W), W ** -0.5, 0.3125, ((0, 8),))
    pattern_col = with_ends(jax.random.randint(arg_keys[3], (ZC, K), 0, CLZ), jax.random.fold_in(arg_keys[3], 1), 0, CLZ - 1).astype(jnp.int32)
    pattern_type = with_ends(jax.random.randint(arg_keys[4], (ZC, K), 0, NB), jax.random.fold_in(arg_keys[4], 1), 0, NB - 1).astype(jnp.int32)
    pseudo_step = jnp.clip(jnp.exp(math.log(0.4) - 2.0794415 * jax.random.uniform(arg_keys[5], (NT, ZC), jnp.float32) ** levels(arg_keys[5], (NT, ZC), ((0, 4), (1, 8)), -0.2, 0.2)), 0.05, 0.4)
    zone_count = draw_zone_count(jax.random.fold_in(arg_keys[12], 71), 0)
    link_src = with_ends(jax.random.randint(arg_keys[7], (NT, NLT), 0, CLZ), jax.random.fold_in(arg_keys[7], 1), 0, CLZ - 1).astype(jnp.int32)
    link_owner_keys = jax.random.split(jax.random.fold_in(arg_keys[8], 1), NT * NLT // NL)
    link_owner_turns = jax.random.permutation(jax.random.fold_in(arg_keys[8], 3), NT * NLT // NL)
    link_owner = jax.vmap(lambda own, number: assign_block(jax.random.fold_in(arg_keys[8], 2), own, number, NL, N_ZONE, 1, CAP, 2))(link_owner_keys, link_owner_turns).reshape((NT, NLT, 1))
    link_dest = with_ends(jax.random.randint(arg_keys[9], (NT, NLT), 0, CLZ), jax.random.fold_in(arg_keys[9], 1), 0, CLZ - 1).astype(jnp.int32)
    link_weight = with_ends(jax.random.randint(arg_keys[10], (NT, NLT), 0, NWT), jax.random.fold_in(arg_keys[10], 1), 0, NWT - 1).astype(jnp.int32)
    iface_table = jnp.clip(jax.random.uniform(arg_keys[11], (NWT, W), jnp.float32, 0.5, 1.5), 0.5, 1.5)
    return dict(state=state, source=source, jac_table=jac_table, pattern_col=pattern_col, pattern_type=pattern_type, pseudo_step=pseudo_step, zone_count=zone_count, link_src=link_src, link_owner=link_owner, link_dest=link_dest, link_weight=link_weight, iface_table=iface_table)


OMEGA = 0.25
NU = 0.1


def coefficient(shift_steps, period):
    steps_f = shift_steps.astype(jnp.float32)
    parity = 1.0 - 2.0 * (shift_steps % 2).astype(jnp.float32)
    phase = math.pi * steps_f / period
    sine_safe = jnp.where(shift_steps == 0, 1.0, jnp.sin(phase))
    derive = OMEGA * parity * jnp.cos(phase) / sine_safe
    damping = NU * parity / (2.0 * sine_safe * sine_safe)
    centre = NU * (period * period + 2) / 12.0
    return jnp.where(shift_steps == 0, centre, derive + damping).astype(jnp.float32)


def reference(state, source, jac_table, pattern_col, pattern_type, pseudo_step, zone_count, link_src, link_owner, link_dest, link_weight, iface_table):
    instance_ids = jnp.arange(NT).astype(jnp.int32)
    steps_grid = (instance_ids[:, None] - instance_ids[None, :]) % NT
    spectral = coefficient(steps_grid, NT)
    time_term = jnp.einsum("nm,mcw->ncw", spectral, state, precision=lax.Precision.HIGHEST)
    state_half = state.astype(jnp.bfloat16)
    by_zone = state_half.reshape(NT, N_ZONE, CLZ, W).transpose(1, 0, 2, 3)
    tables = jac_table.reshape(N_ZONE, NB * W, W)
    columns = pattern_col.reshape(N_ZONE, CLZ, K)
    kinds = pattern_type.reshape(N_ZONE, CLZ, K)

    def zone_product(inputs):
        block_states, table, col_zone, kind_zone = inputs
        products = lax.dot_general(block_states.reshape(NT * CLZ, W), table, (((1,), (1,)), ((), ())), preferred_element_type=jnp.float32)
        products = products.reshape(NT, CLZ * NB, W)
        entry_rows = (col_zone * NB + kind_zone).astype(jnp.int32)
        return jnp.sum(products[:, entry_rows], axis=2)

    jac_term = lax.map(zone_product, (by_zone, tables, columns, kinds)).transpose(1, 0, 2, 3).reshape(NT, ZC, W)
    link_zone = (jnp.arange(NLT) // NL).astype(jnp.int32)
    source_rows = (link_zone[None, :] * CLZ + link_src).astype(jnp.int32)
    scales = iface_table[link_weight]
    picked = jax.vmap(lambda rows_all, which: rows_all[which])(state, source_rows)
    blocks = picked * scales
    target_rows = (link_owner[:, :, 0] * CLZ + link_dest).astype(jnp.int32)
    iface = jax.vmap(lambda values, targets: jax.ops.segment_sum(values, targets, num_segments=ZC))(blocks, target_rows)
    cluster_ids = jnp.arange(ZC).astype(jnp.int32)
    limit = zone_count[cluster_ids // CLZ]
    active = (cluster_ids % CLZ) < limit
    residual = jnp.where(active[None, :, None], source + jac_term + time_term - iface, jnp.float32(0.0))
    updated = state - pseudo_step[:, :, None] * residual
    return updated, residual
```

```python
import functools
import math

import jax
import jax.numpy as jnp
import numpy as np
from jax import lax
from jax.experimental import pallas as pl
from jax.experimental.pallas import tpu as pltpu
from jax.sharding import PartitionSpec as P

OMEGA = 0.25
NU = 0.1
LANES = 128
VMEM = pl.BlockSpec(memory_space=pltpu.VMEM)
SMEM = pl.BlockSpec(memory_space=pltpu.SMEM)


def coefficients(period):
    table = [NU * (period * period + 2) / 12.0]
    for shift in range(1, period):
        phase = math.pi * shift / period
        sign = -1.0 if shift % 2 else 1.0
        sine = math.sin(phase)
        table.append(OMEGA * sign * math.cos(phase) / sine + NU * sign / (2.0 * sine * sine))
    return [float(np.float32(entry)) for entry in table]


def chosen(table, index):
    value = jnp.float32(table[0])
    for position in range(1, len(table)):
        value = jnp.where(index == position, jnp.float32(table[position]), value)
    return value


def parts_of(value):
    high = value.astype(jnp.bfloat16)
    rest = value - high.astype(jnp.float32)
    middle = rest.astype(jnp.bfloat16)
    low = (rest - middle.astype(jnp.float32)).astype(jnp.bfloat16)
    return high, middle, low


def power_of_two(count):
    return count & (count - 1) == 0


def radices_of(zones):
    radices = []
    rest = zones
    while rest > 1:
        step = 2 if not radices or rest == 2 else 4
        radices.append(step)
        rest //= step
    return radices


def block_of(relative, radices):
    place = jnp.zeros_like(relative)
    shift = 0
    for radix in radices:
        bits = radix.bit_length() - 1
        place = place * radix + ((relative >> shift) & (radix - 1))
        shift += bits
    return place


def as_column(row):
    count = row.shape[1]
    lane = lax.broadcasted_iota(jnp.int32, (count, count), 1)
    sublane = lax.broadcasted_iota(jnp.int32, (count, count), 0)
    return jnp.sum(jnp.where(lane == sublane, row, jnp.zeros_like(row)), axis=1, keepdims=True)


def outgoing_kernel(radices, slots_per, state, source, owner, dest, weight, table, keep, send):
    width, clusters = state.shape
    links = owner.shape[1]
    sets = table.shape[0]
    slots = keep.shape[0] + send.shape[0]
    owners = owner[...].astype(jnp.float32)
    lane = lax.broadcasted_iota(jnp.int32, (links, links), 1)
    sublane = lax.broadcasted_iota(jnp.int32, (links, links), 0)
    earlier = (as_column(owners) == owners) & (sublane < lane)
    rank = jnp.sum(jnp.where(earlier, 1.0, 0.0), axis=0, keepdims=True).astype(jnp.int32)
    if radices:
        relative = owner[...] ^ lax.axis_index("zone")
        block = block_of(relative, radices)
    else:
        block = owner[...]
    slot = block * slots_per + rank
    placing = lax.broadcasted_iota(jnp.int32, (slots, links), 0) == slot

    def of_slot(row):
        return jnp.sum(
            jnp.where(placing, row[...].astype(jnp.float32) + 1.0, 0.0), axis=1, keepdims=True
        ) - 1.0

    from_cluster, to_cluster, by_set = of_slot(source), of_slot(dest), of_slot(weight)
    pick = lax.broadcasted_iota(jnp.int32, (slots, clusters), 1) == from_cluster.astype(jnp.int32)
    pick = jnp.where(pick, 1.0, 0.0).astype(jnp.bfloat16)
    parts = jnp.concatenate(parts_of(state[...]), axis=1)
    picked = lax.dot_general(
        jnp.concatenate([pick, pick, pick], axis=1),
        parts,
        (((1,), (1,)), ((), ())),
        preferred_element_type=jnp.float32,
    )
    pick = lax.broadcasted_iota(jnp.int32, (slots, sets), 1) == by_set.astype(jnp.int32)
    pick = jnp.where(pick, 1.0, 0.0).astype(jnp.bfloat16)
    scales = jnp.zeros((slots, width), jnp.float32)
    for part in parts_of(table[...]):
        scales = scales + jnp.dot(pick, part, preferred_element_type=jnp.float32)
    blocks = picked * scales
    marks = jnp.broadcast_to(to_cluster, (slots, keep.shape[1] - width))
    kept = keep.shape[0]
    keep[:, :width] = blocks[:kept]
    keep[:, width:] = marks[:kept]
    send[:, :width] = blocks[kept:]
    send[:, width:] = marks[kept:]


def jacobian_kernel(state, table, column, kind, product):
    width, clusters = state.shape
    kinds = table.shape[0]
    half = state[...].astype(jnp.bfloat16)
    codes = column[...] + clusters * kind[...]
    row = lax.broadcasted_iota(jnp.int32, (clusters, clusters), 0)
    total = jnp.zeros((width, clusters), jnp.float32)
    for which in range(kinds):
        full = jnp.dot(table[which], half, preferred_element_type=jnp.float32)
        high = full.astype(jnp.bfloat16)
        low = (full - high.astype(jnp.float32)).astype(jnp.bfloat16)
        count = jnp.zeros((clusters, clusters), jnp.float32)
        for entry in range(codes.shape[0]):
            hit = row == codes[entry : entry + 1, :] - which * clusters
            count = count + jnp.where(hit, 1.0, 0.0)
        count = count.astype(jnp.bfloat16)
        total = total + jnp.dot(
            jnp.concatenate([high, low], axis=1),
            jnp.concatenate([count, count], axis=0),
            preferred_element_type=jnp.float32,
        )
    product[...] = total


def combine_kernel(table, held_by, *refs):
    period = len(table)
    me = lax.axis_index("inst")
    *held, out = refs
    total = None
    for mask, ref in zip(held_by, held, strict=True):
        shift = ((me ^ 1) - (me ^ mask) + period) & (period - 1)
        term = chosen(table, shift) * ref[...]
        total = term if total is None else total + term
    out[...] = total


def final_kernel(table, held_by, pieces, count, step, source, product, *refs):
    period = len(table)
    held = refs[: len(held_by)]
    others = refs[len(held_by) : len(refs) - pieces - 2]
    incoming = refs[len(refs) - pieces - 2 : len(refs) - 2]
    updated, residual = refs[-2:]
    width, clusters = source.shape
    me = lax.axis_index("inst")
    total = source[...] + product[...]
    for mask, ref in zip(held_by, held, strict=True):
        shift = (me - (me ^ mask) + period) & (period - 1)
        total = total + chosen(table, shift) * ref[...]
    for ref in others:
        total = total + ref[...]
    arrived = jnp.concatenate([ref[...] for ref in incoming], axis=0)
    target = arrived[:, width : width + 1].astype(jnp.int32)
    landing = lax.broadcasted_iota(jnp.int32, (arrived.shape[0], clusters), 1) == target
    landing = jnp.where(landing, 1.0, 0.0).astype(jnp.bfloat16)
    parts = jnp.concatenate(parts_of(arrived), axis=0)
    iface = lax.dot_general(
        parts,
        jnp.concatenate([landing, landing, landing], axis=0),
        (((0,), (0,)), ((), ())),
        preferred_element_type=jnp.float32,
    )[:width]
    active = lax.broadcasted_iota(jnp.int32, (1, clusters), 1) < count[0]
    kept = jnp.where(active, total - iface, 0.0)
    residual[...] = kept
    updated[...] = held[0][...] - step[...] * kept


def moved(value, axis, mask):
    count = lax.axis_size(axis)
    return lax.ppermute(value, axis, [(place, place ^ mask) for place in range(count)])


def zone_exchange(keep, send, radices, slots_per):
    zones = math.prod(radices)
    lanes = keep.shape[-1]
    rest = zones // radices[0]
    held, shift = [], 0
    for stage, radix in enumerate(radices):
        if stage == 0:
            arrived = moved(send, "zone", 1).reshape(rest, slots_per, lanes)
            held = [keep.reshape(rest, slots_per, lanes), arrived]
            shift = 1
            continue
        bits = radix.bit_length() - 1
        rest //= radix
        cut = [piece.reshape(radix, -1, slots_per, lanes) for piece in held]
        after = [piece[0] for piece in cut]
        for digit in range(radix - 1, 0, -1):
            leaving = jnp.concatenate([piece[digit] for piece in cut], axis=0)
            leaving = leaving.reshape(-1, lanes)
            landed = moved(leaving, "zone", digit << shift)
            after.append(landed.reshape(-1, slots_per, lanes))
        if rest > 1:
            joined = []
            for piece in after:
                groups = piece.reshape(-1, rest, slots_per, lanes)
                joined.extend(groups[index] for index in range(groups.shape[0]))
            after = joined
        held = after
        shift += bits
    return [piece.reshape(-1, lanes) for piece in held]


def on_device(
    state,
    source,
    jac_table,
    pattern_col,
    pattern_type,
    pseudo_step,
    zone_count,
    link_src,
    link_owner,
    link_dest,
    link_weight,
    iface_table,
):
    instances = lax.axis_size("inst")
    zones = lax.axis_size("zone")
    state_t = state[0].T
    source_t = source[0].T
    width, clusters = state_t.shape
    links = link_src.shape[1]
    slots_per = 2 * links // zones
    slots = zones * slots_per
    padded = -(-(width + 1) // LANES) * LANES
    table = coefficients(instances)
    block = jax.ShapeDtypeStruct((width, clusters), jnp.float32)

    radices = radices_of(zones)
    half = jax.ShapeDtypeStruct((slots // 2, padded), jnp.float32)
    keep, send = pl.pallas_call(
        functools.partial(outgoing_kernel, radices, slots_per),
        out_shape=(half, half),
        in_specs=[VMEM] * 6,
        out_specs=(VMEM, VMEM),
    )(
        state_t,
        link_src,
        link_owner.reshape(1, links),
        link_dest,
        link_weight,
        iface_table,
    )
    incoming = zone_exchange(keep, send, radices, slots_per)

    held, held_by = [state_t], [0]
    mask = instances // 2
    while mask > 1:
        held = held + [moved(piece, "inst", mask) for piece in held]
        held_by = held_by + [by ^ mask for by in held_by]
        mask //= 2
    others = []
    if instances > 1:
        combined = pl.pallas_call(
            functools.partial(combine_kernel, table, held_by),
            out_shape=block,
            in_specs=[VMEM] * len(held),
            out_specs=VMEM,
        )(*held)
        others = [moved(combined, "inst", 1)]

    product = pl.pallas_call(
        jacobian_kernel,
        out_shape=block,
        in_specs=[VMEM] * 4,
        out_specs=VMEM,
    )(state_t, jac_table, pattern_col.T, pattern_type.T)

    updated, residual = pl.pallas_call(
        functools.partial(final_kernel, table, held_by, len(incoming)),
        out_shape=(block, block),
        in_specs=[SMEM] + [VMEM] * (3 + len(held) + len(others) + len(incoming)),
        out_specs=(VMEM, VMEM),
    )(zone_count, pseudo_step, source_t, product, *held, *others, *incoming)
    return updated.T[None], residual.T[None]


def solution(mesh):
    placed = (
        P("inst", "zone", None),
        P("inst", "zone", None),
        P("zone", None, None),
        P("zone", None),
        P("zone", None),
        P("inst", "zone"),
        P("zone"),
        P("inst", "zone"),
        P("inst", "zone", None),
        P("inst", "zone"),
        P("inst", "zone"),
        P(),
    )
    return jax.shard_map(
        on_device,
        mesh=mesh,
        in_specs=placed,
        out_specs=(P("inst", "zone", None), P("inst", "zone", None)),
        check_vma=False,
    )
```

```python
import functools
import math

import jax
import jax.numpy as jnp
import numpy as np
from jax import lax
from jax.experimental import pallas as pl
from jax.experimental.pallas import tpu as pltpu
from jax.sharding import PartitionSpec as P

OMEGA = 0.25
NU = 0.1
LANES = 128
VMEM = pl.BlockSpec(memory_space=pltpu.VMEM)
HBM = pl.BlockSpec(memory_space=pltpu.HBM)
ROOM = pltpu.CompilerParams(vmem_limit_bytes=6 << 20)


def in_hbm(value):
    return pltpu.with_memory_space_constraint(value, pltpu.HBM)


def coefficients(period):
    table = [NU * (period * period + 2) / 12.0]
    for shift in range(1, period):
        phase = math.pi * shift / period
        sign = -1.0 if shift % 2 else 1.0
        sine = math.sin(phase)
        table.append(OMEGA * sign * math.cos(phase) / sine + NU * sign / (2.0 * sine * sine))
    return [float(np.float32(entry)) for entry in table]


def chosen(table, index):
    value = jnp.float32(table[0])
    for position in range(1, len(table)):
        value = jnp.where(index == position, jnp.float32(table[position]), value)
    return value


def parts_of(value):
    high = value.astype(jnp.bfloat16)
    rest = value - high.astype(jnp.float32)
    middle = rest.astype(jnp.bfloat16)
    low = (rest - middle.astype(jnp.float32)).astype(jnp.bfloat16)
    return high, middle, low


def power_of_two(count):
    return count & (count - 1) == 0


def radices_of(zones):
    radices = []
    rest = zones
    while rest > 1:
        step = 2 if not radices or rest == 2 else 4
        radices.append(step)
        rest //= step
    return radices


def block_of(relative, radices):
    place = jnp.zeros_like(relative)
    shift = 0
    for radix in radices:
        bits = radix.bit_length() - 1
        place = place * radix + ((relative >> shift) & (radix - 1))
        shift += bits
    return place


def as_column(row):
    count = row.shape[1]
    lane = lax.broadcasted_iota(jnp.int32, (count, count), 1)
    sublane = lax.broadcasted_iota(jnp.int32, (count, count), 0)
    return jnp.sum(jnp.where(lane == sublane, row, jnp.zeros_like(row)), axis=1, keepdims=True)


def fetched(pairs, sems):
    copies = []
    for place, (origin, target) in enumerate(pairs):
        copy = pltpu.make_async_copy(origin, target, sems.at[place])
        copy.start()
        copies.append(copy)
    return copies


def outgoing_kernel(
    radices,
    slots_per,
    state_in,
    source_in,
    owner_in,
    dest_in,
    weight_in,
    table_in,
    state,
    keep,
    send,
    source,
    owner,
    dest,
    weight,
    table,
    sems,
):
    copies = fetched(
        (
            (owner_in, owner),
            (source_in, source),
            (weight_in, weight),
            (dest_in, dest),
            (state_in, state),
            (table_in, table),
        ),
        sems,
    )
    width, clusters = state.shape
    links = owner.shape[1]
    sets = table.shape[0]
    slots = keep.shape[0] + send.shape[0]
    for copy in copies[:4]:
        copy.wait()
    owners = owner[...].astype(jnp.float32)
    lane = lax.broadcasted_iota(jnp.int32, (links, links), 1)
    sublane = lax.broadcasted_iota(jnp.int32, (links, links), 0)
    earlier = (as_column(owners) == owners) & (sublane < lane)
    rank = jnp.sum(jnp.where(earlier, 1.0, 0.0), axis=0, keepdims=True).astype(jnp.int32)
    relative = owner[...] ^ lax.axis_index("zone")
    slot = block_of(relative, radices) * slots_per + rank
    placing = lax.broadcasted_iota(jnp.int32, (slots, links), 0) == slot

    def of_slot(row):
        return jnp.sum(
            jnp.where(placing, row[...].astype(jnp.float32) + 1.0, 0.0), axis=1, keepdims=True
        ) - 1.0

    from_cluster, to_cluster, by_set = of_slot(source), of_slot(dest), of_slot(weight)
    pick = lax.broadcasted_iota(jnp.int32, (slots, clusters), 1) == from_cluster.astype(jnp.int32)
    pick = jnp.where(pick, 1.0, 0.0).astype(jnp.bfloat16)
    choose = lax.broadcasted_iota(jnp.int32, (slots, sets), 1) == by_set.astype(jnp.int32)
    choose = jnp.where(choose, 1.0, 0.0).astype(jnp.bfloat16)
    copies[5].wait()
    scales = jnp.zeros((slots, width), jnp.float32)
    for part in parts_of(table[...]):
        scales = scales + jnp.dot(choose, part, preferred_element_type=jnp.float32)
    copies[4].wait()
    parts = jnp.concatenate(parts_of(state[...]), axis=1)
    picked = lax.dot_general(
        jnp.concatenate([pick, pick, pick], axis=1),
        parts,
        (((1,), (1,)), ((), ())),
        preferred_element_type=jnp.float32,
    )
    blocks = picked * scales
    marks = jnp.broadcast_to(to_cluster, (slots, keep.shape[1] - width))
    kept = keep.shape[0]
    keep[:, :width] = blocks[:kept]
    keep[:, width:] = marks[:kept]
    send[:, :width] = blocks[kept:]
    send[:, width:] = marks[kept:]


def put_products(blocks, place, half, high, low):
    clusters = half.shape[1]
    full = jnp.dot(blocks, half, preferred_element_type=jnp.float32)
    columns = slice(place * clusters, (place + 1) * clusters)
    upper = full.astype(jnp.bfloat16)
    high[:, columns] = upper
    low[:, columns] = (full - upper.astype(jnp.float32)).astype(jnp.bfloat16)


def products_kernel(blocks_in, state, high, low, blocks, sems):
    (copy,) = fetched([(blocks_in.at[pl.ds(0, blocks.shape[0])], blocks)], sems)
    half = state[...].astype(jnp.bfloat16)
    copy.wait()
    for which in range(blocks.shape[0]):
        put_products(blocks[which], which, half, high, low)


def local_kernel(
    table,
    blocks_in,
    column_in,
    kind_in,
    source_in,
    step_in,
    count,
    state,
    high,
    low,
    base,
    rows,
    blocks,
    column,
    kind,
    source,
    step,
    more_high,
    more_low,
    sems,
):
    clusters = state.shape[1]
    kinds = blocks_in.shape[0]
    ready = kinds - blocks.shape[0]
    copies = fetched(
        [
            (column_in, column),
            (kind_in, kind),
            (blocks_in.at[pl.ds(ready, kinds - ready)], blocks),
            (source_in, source),
            (step_in, step),
        ],
        sems,
    )
    half = state[...].astype(jnp.bfloat16)
    copies[0].wait()
    copies[1].wait()
    codes = column[...] + clusters * kind[...]
    row = lax.broadcasted_iota(jnp.int32, (clusters, clusters), 0)
    counts = []
    for which in range(kinds):
        count_of = jnp.zeros((clusters, clusters), jnp.float32)
        for entry in range(codes.shape[0]):
            hit = row == codes[entry : entry + 1, :] - which * clusters
            count_of = count_of + jnp.where(hit, 1.0, 0.0)
        counts.append(count_of.astype(jnp.bfloat16))
    counts = jnp.concatenate(counts, axis=0)
    total = chosen(table, 0) * state[...]
    for part in (high, low):
        total = total + jnp.dot(
            part[...], counts[: ready * clusters], preferred_element_type=jnp.float32
        )
    copies[2].wait()
    for which in range(kinds - ready):
        put_products(blocks[which], which, half, more_high, more_low)
    for part in (more_high, more_low):
        total = total + jnp.dot(
            part[...], counts[ready * clusters :], preferred_element_type=jnp.float32
        )
    copies[3].wait()
    base[...] = total + source[...]
    copies[4].wait()
    active = lax.broadcasted_iota(jnp.int32, (1, clusters), 1) < count[0]
    rows[0:1, :] = step[...]
    rows[1:2, :] = jnp.where(active, 1.0, 0.0)


def combine_kernel(table, held_by, mask, _, *refs):
    period = len(table)
    me = lax.axis_index("inst")
    *held, out = refs
    total = None
    for by, ref in zip(held_by, held, strict=True):
        shift = ((me ^ mask) - (me ^ by) + period) & (period - 1)
        term = chosen(table, shift) * ref[...]
        total = term if total is None else total + term
    out[...] = total


def final_kernel(table, held_by, pieces, base, rows, *refs):
    period = len(table)
    held = refs[: len(held_by)]
    others = refs[len(held_by) : len(refs) - pieces - 2]
    incoming = refs[len(refs) - pieces - 2 : len(refs) - 2]
    updated, residual = refs[-2:]
    width, clusters = base.shape
    me = lax.axis_index("inst")
    total = base[...]
    for mask, ref in zip(held_by[1:], held[1:], strict=True):
        shift = (me - (me ^ mask) + period) & (period - 1)
        total = total + chosen(table, shift) * ref[...]
    for ref in others:
        total = total + ref[...]
    arrived = jnp.concatenate([ref[...] for ref in incoming], axis=0)
    target = arrived[:, width : width + 1].astype(jnp.int32)
    landing = lax.broadcasted_iota(jnp.int32, (arrived.shape[0], clusters), 1) == target
    landing = jnp.where(landing, 1.0, 0.0).astype(jnp.bfloat16)
    parts = jnp.concatenate(parts_of(arrived), axis=0)
    iface = lax.dot_general(
        parts,
        jnp.concatenate([landing, landing, landing], axis=0),
        (((0,), (0,)), ((), ())),
        preferred_element_type=jnp.float32,
    )[:width]
    kept = jnp.where(rows[1:2, :] > 0.0, total - iface, 0.0)
    residual[...] = kept
    updated[...] = held[0][...] - rows[0:1, :] * kept


def ordered_kernel(_, *refs):
    half = len(refs) // 2
    for origin, target in zip(refs[:half], refs[half:], strict=True):
        target[...] = origin[...]


def ordered(after, *values):
    return pl.pallas_call(
        ordered_kernel,
        out_shape=tuple(jax.ShapeDtypeStruct(value.shape, value.dtype) for value in values),
        in_specs=[VMEM] * (1 + len(values)),
        out_specs=(VMEM,) * len(values),
        compiler_params=ROOM,
    )(after, *values)


def moved(value, axis, mask):
    count = lax.axis_size(axis)
    return lax.ppermute(value, axis, [(place, place ^ mask) for place in range(count)])


def zone_exchange(keep, send, radices, slots_per, after):
    zones = math.prod(radices)
    lanes = keep.shape[-1]
    rest = zones // radices[0]
    held, shift = [], 0
    for stage, radix in enumerate(radices):
        if stage == 0:
            pieces = ordered(after, keep, moved(send, "zone", 1))
            held = [piece.reshape(rest, slots_per, lanes) for piece in pieces]
            shift = 1
            continue
        bits = radix.bit_length() - 1
        rest //= radix
        cut = [piece.reshape(radix, -1, slots_per, lanes) for piece in held]
        after = [piece[0] for piece in cut]
        for digit in range(radix - 1, 0, -1):
            leaving = jnp.concatenate([piece[digit] for piece in cut], axis=0)
            leaving = leaving.reshape(-1, lanes)
            landed = moved(leaving, "zone", digit << shift)
            after.append(landed.reshape(-1, slots_per, lanes))
        if rest > 1:
            joined = []
            for piece in after:
                groups = piece.reshape(-1, rest, slots_per, lanes)
                joined.extend(groups[index] for index in range(groups.shape[0]))
            after = joined
        held = after
        shift += bits
    return [piece.reshape(-1, lanes) for piece in held]


def on_device(
    state,
    source,
    jac_table,
    pattern_col,
    pattern_type,
    pseudo_step,
    zone_count,
    link_src,
    link_owner,
    link_dest,
    link_weight,
    iface_table,
):
    instances = lax.axis_size("inst")
    zones = lax.axis_size("zone")
    state_t = state[0].T
    source_t = source[0].T
    width, clusters = state_t.shape
    links = link_src.shape[1]
    slots_per = 2 * links // zones
    slots = zones * slots_per
    padded = -(-(width + 1) // LANES) * LANES
    table = coefficients(instances)
    block = jax.ShapeDtypeStruct((width, clusters), jnp.float32)

    radices = radices_of(zones)
    half = jax.ShapeDtypeStruct((slots // 2, padded), jnp.float32)
    state_t, keep, send = pl.pallas_call(
        functools.partial(outgoing_kernel, radices, slots_per),
        out_shape=(block, half, half),
        in_specs=[HBM] * 6,
        out_specs=(VMEM, VMEM, VMEM),
        scratch_shapes=[pltpu.VMEM((1, links), jnp.int32)] * 4
        + [pltpu.VMEM(iface_table.shape, jnp.float32), pltpu.SemaphoreType.DMA((6,))],
        compiler_params=ROOM,
    )(
        in_hbm(state_t),
        in_hbm(link_src),
        in_hbm(link_owner.reshape(1, links)),
        in_hbm(link_dest),
        in_hbm(link_weight),
        in_hbm(iface_table),
    )
    kinds = jac_table.shape[0]
    first = kinds // 2
    blocks_hbm = in_hbm(jac_table)
    parts = jax.ShapeDtypeStruct((width, first * clusters), jnp.bfloat16)
    high, low = pl.pallas_call(
        products_kernel,
        out_shape=(parts, parts),
        in_specs=[HBM, VMEM],
        out_specs=(VMEM, VMEM),
        scratch_shapes=[
            pltpu.VMEM((first, *jac_table.shape[1:]), jac_table.dtype),
            pltpu.SemaphoreType.DMA((1,)),
        ],
        compiler_params=ROOM,
        cost_estimate=pl.CostEstimate(
            flops=2 * first * width * clusters * width,
            bytes_accessed=2 * first * width * width + 4 * parts.size,
            transcendentals=0,
        ),
    )(blocks_hbm, state_t)

    held, held_by = [state_t], [0]
    mask = 1
    while mask < instances // 2:
        held = held + [moved(piece, "inst", mask) for piece in held]
        held_by = held_by + [by ^ mask for by in held_by]
        mask *= 2
    others = []
    if instances > 1:
        combined = pl.pallas_call(
            functools.partial(combine_kernel, table, held_by, mask),
            out_shape=block,
            in_specs=[VMEM] * (1 + len(held)),
            out_specs=VMEM,
            compiler_params=ROOM,
        )(high, *held)
        others = [moved(combined, "inst", mask)]
    incoming = zone_exchange(keep, send, radices, slots_per, combined)

    column, kind = pattern_col.T, pattern_type.T
    base, rows = pl.pallas_call(
        functools.partial(local_kernel, table),
        out_shape=(block, jax.ShapeDtypeStruct((8, clusters), jnp.float32)),
        in_specs=[HBM] * 5 + [VMEM] * 4,
        out_specs=(VMEM, VMEM),
        scratch_shapes=[
            pltpu.VMEM((kinds - first, *jac_table.shape[1:]), jac_table.dtype),
            pltpu.VMEM(column.shape, jnp.int32),
            pltpu.VMEM(kind.shape, jnp.int32),
            pltpu.VMEM((width, clusters), jnp.float32),
            pltpu.VMEM((1, clusters), jnp.float32),
            pltpu.VMEM((width, (kinds - first) * clusters), jnp.bfloat16),
            pltpu.VMEM((width, (kinds - first) * clusters), jnp.bfloat16),
            pltpu.SemaphoreType.DMA((5,)),
        ],
        compiler_params=ROOM,
        cost_estimate=pl.CostEstimate(
            flops=4 * kinds * width * clusters * clusters,
            bytes_accessed=4 * parts.size + 8 * width * clusters,
            transcendentals=0,
        ),
    )(
        blocks_hbm,
        in_hbm(column),
        in_hbm(kind),
        in_hbm(source_t),
        in_hbm(pseudo_step),
        zone_count,
        state_t,
        high,
        low,
    )

    updated, residual = pl.pallas_call(
        functools.partial(final_kernel, table, held_by, len(incoming)),
        out_shape=(block, block),
        in_specs=[VMEM] * (2 + len(held) + len(others) + len(incoming)),
        out_specs=(VMEM, VMEM),
        compiler_params=ROOM,
    )(base, rows, *held, *others, *incoming)
    return updated.T[None], residual.T[None]


def solution(mesh):
    placed = (
        P("inst", "zone", None),
        P("inst", "zone", None),
        P("zone", None, None),
        P("zone", None),
        P("zone", None),
        P("inst", "zone"),
        P("zone"),
        P("inst", "zone"),
        P("inst", "zone", None),
        P("inst", "zone"),
        P("inst", "zone"),
        P(),
    )
    return jax.shard_map(
        on_device,
        mesh=mesh,
        in_specs=placed,
        out_specs=(P("inst", "zone", None), P("inst", "zone", None)),
        check_vma=False,
    )
```

```python
import functools
import math

import jax
import jax.numpy as jnp
import numpy as np
from jax import lax
from jax.experimental import pallas as pl
from jax.experimental.pallas import tpu as pltpu
from jax.sharding import PartitionSpec as P

OMEGA = 0.25
NU = 0.1
LANES = 128
VMEM = pl.BlockSpec(memory_space=pltpu.VMEM)
SMEM = pl.BlockSpec(memory_space=pltpu.SMEM)
HBM = pl.BlockSpec(memory_space=pltpu.HBM)
FREE = pl.CostEstimate(flops=1, bytes_accessed=1, transcendentals=0)
ROOM = pltpu.CompilerParams(vmem_limit_bytes=6 << 20)


def in_hbm(value):
    return pltpu.with_memory_space_constraint(value, pltpu.HBM)


def coefficients(period):
    table = [NU * (period * period + 2) / 12.0]
    for shift in range(1, period):
        phase = math.pi * shift / period
        sign = -1.0 if shift % 2 else 1.0
        sine = math.sin(phase)
        table.append(OMEGA * sign * math.cos(phase) / sine + NU * sign / (2.0 * sine * sine))
    return [float(np.float32(entry)) for entry in table]


def chosen(table, index, dtype=jnp.float32):
    value = jnp.asarray(table[0], dtype)
    for position in range(1, len(table)):
        value = jnp.where(index == position, jnp.asarray(table[position], dtype), value)
    return value


def parts_of(value):
    high = value.astype(jnp.bfloat16)
    rest = value - high.astype(jnp.float32)
    middle = rest.astype(jnp.bfloat16)
    low = (rest - middle.astype(jnp.float32)).astype(jnp.bfloat16)
    return high, middle, low


def power_of_two(count):
    return count & (count - 1) == 0


def stages_of(zones):
    stages = []
    shift = zones.bit_length() - 1
    while shift:
        bits = 2 if shift > 1 else 1
        shift -= bits
        stages.append((1 << bits, shift))
    return stages


def turns_of(radix):
    if radix == 4:
        return ((0, 1, 2, 3), (2, 3, 1, 0), (3, 2, 0, 1), (1, 0, 3, 2))
    return tuple(tuple(digit ^ turn for digit in range(radix)) for turn in range(radix))


def block_of(owner, me, stages):
    place = jnp.zeros_like(owner)
    for radix, shift in stages:
        turns = turns_of(radix)
        mine = (me >> shift) & (radix - 1)
        theirs = (owner >> shift) & (radix - 1)
        turn = jnp.zeros_like(owner)
        for which in range(1, radix):
            target = chosen(turns[which], mine, jnp.int32)
            turn = jnp.where(theirs == target, which, turn)
        place = place * radix + turn
    return place


def as_column(row):
    count = row.shape[1]
    lane = lax.broadcasted_iota(jnp.int32, (count, count), 1)
    sublane = lax.broadcasted_iota(jnp.int32, (count, count), 0)
    return jnp.sum(jnp.where(lane == sublane, row, jnp.zeros_like(row)), axis=1, keepdims=True)


def fetched(pairs, sems):
    copies = []
    for place, (origin, target) in enumerate(pairs):
        copy = pltpu.make_async_copy(origin, target, sems.at[place])
        copy.start()
        copies.append(copy)
    return copies


def outgoing_kernel(
    stages,
    slots_per,
    state_in,
    source_in,
    owner_in,
    dest_in,
    weight_in,
    table_in,
    state,
    *refs,
):
    *sends, source, owner, dest, weight, table, sems = refs
    copies = fetched(
        (
            (owner_in, owner),
            (source_in, source),
            (weight_in, weight),
            (dest_in, dest),
            (state_in, state),
            (table_in, table),
        ),
        sems,
    )
    width, clusters = state.shape
    links = owner.shape[1]
    sets = table.shape[0]
    share, lanes = sends[0].shape
    slots = share * len(sends)
    for copy in copies[:4]:
        copy.wait()
    owners = owner[...].astype(jnp.float32)
    lane = lax.broadcasted_iota(jnp.int32, (links, links), 1)
    sublane = lax.broadcasted_iota(jnp.int32, (links, links), 0)
    earlier = (as_column(owners) == owners) & (sublane < lane)
    rank = jnp.sum(jnp.where(earlier, 1.0, 0.0), axis=0, keepdims=True).astype(jnp.int32)
    slot = block_of(owner[...], lax.axis_index("zone"), stages) * slots_per + rank
    placing = lax.broadcasted_iota(jnp.int32, (slots, links), 0) == slot

    def of_slot(row):
        return jnp.sum(
            jnp.where(placing, row[...].astype(jnp.float32) + 1.0, 0.0), axis=1, keepdims=True
        ) - 1.0

    from_cluster, to_cluster, by_set = of_slot(source), of_slot(dest), of_slot(weight)
    pick = lax.broadcasted_iota(jnp.int32, (slots, clusters), 1) == from_cluster.astype(jnp.int32)
    pick = jnp.where(pick, 1.0, 0.0).astype(jnp.bfloat16)
    choose = lax.broadcasted_iota(jnp.int32, (slots, sets), 1) == by_set.astype(jnp.int32)
    choose = jnp.where(choose, 1.0, 0.0).astype(jnp.bfloat16)
    copies[5].wait()
    scales = jnp.zeros((slots, width), jnp.float32)
    for part in parts_of(table[...]):
        scales = scales + jnp.dot(choose, part, preferred_element_type=jnp.float32)
    copies[4].wait()
    parts = jnp.concatenate(parts_of(state[...]), axis=1)
    picked = lax.dot_general(
        jnp.concatenate([pick, pick, pick], axis=1),
        parts,
        (((1,), (1,)), ((), ())),
        preferred_element_type=jnp.float32,
    )
    blocks = picked * scales
    marks = jnp.broadcast_to(to_cluster, (slots, lanes - width))
    for place, send in enumerate(sends):
        rows = slice(place * share, (place + 1) * share)
        send[:, :width] = blocks[rows]
        send[:, width:] = marks[rows]


def half_kernel(state, _, half):
    half[...] = state[...].astype(jnp.bfloat16)


def landed(pieces, width, clusters):
    arrived = jnp.concatenate([piece[...] for piece in pieces], axis=0)
    target = arrived[:, width : width + 1].astype(jnp.int32)
    landing = lax.broadcasted_iota(jnp.int32, (arrived.shape[0], clusters), 1) == target
    landing = jnp.where(landing, 1.0, 0.0).astype(jnp.bfloat16)
    return lax.dot_general(
        jnp.concatenate(parts_of(arrived), axis=0),
        jnp.concatenate([landing, landing, landing], axis=0),
        (((0,), (0,)), ((), ())),
        preferred_element_type=jnp.float32,
    )[:width]


def local_kernel(
    table,
    column_in,
    kind_in,
    source_in,
    step_in,
    count,
    state,
    products,
    staying,
    base,
    rows,
    column,
    kind,
    source,
    sems,
):
    width, clusters = state.shape
    kinds = products.shape[0] // width
    step = rows.at[pl.ds(0, 1), :]
    copies = fetched(
        [(column_in, column), (kind_in, kind), (source_in, source), (step_in, step)], sems
    )
    total = chosen(table, 0) * state[...] - landed([staying], width, clusters)
    high, low = [], []
    for which in range(kinds):
        full = products[pl.ds(which * width, width), :]
        upper = full.astype(jnp.bfloat16)
        high.append(upper)
        low.append((full - upper.astype(jnp.float32)).astype(jnp.bfloat16))
    copies[0].wait()
    copies[1].wait()
    codes = column[...] + clusters * kind[...]
    row = lax.broadcasted_iota(jnp.int32, (clusters, clusters), 0)
    counts = []
    for which in range(kinds):
        count_of = jnp.zeros((clusters, clusters), jnp.float32)
        for entry in range(codes.shape[0]):
            hit = row == codes[entry : entry + 1, :] - which * clusters
            count_of = count_of + jnp.where(hit, 1.0, 0.0)
        counts.append(count_of.astype(jnp.bfloat16))
    counts = jnp.concatenate(counts, axis=0)
    for part in (high, low):
        total = total + jnp.dot(
            jnp.concatenate(part, axis=1), counts, preferred_element_type=jnp.float32
        )
    copies[2].wait()
    copies[3].wait()
    base[...] = total + source[...]
    active = lax.broadcasted_iota(jnp.int32, (1, clusters), 1) < count[0]
    rows[1:2, :] = jnp.where(active, 1.0, 0.0)


def combine_kernel(table, held_by, mask, *refs):
    period = len(table)
    me = lax.axis_index("inst")
    held, rest = refs[: len(held_by)], refs[len(held_by) :]
    passing = len(rest) // 2
    out = rest[passing]
    for origin, target in zip(rest[:passing], rest[passing + 1 :], strict=True):
        target[...] = origin[...]
    total = None
    for by, ref in zip(held_by, held, strict=True):
        shift = ((me ^ mask) - (me ^ by) + period) & (period - 1)
        term = chosen(table, shift) * ref[...]
        total = term if total is None else total + term
    out[...] = total


def final_kernel(table, held_by, pieces, base, rows, *refs):
    period = len(table)
    held = refs[: len(held_by)]
    others = refs[len(held_by) : len(refs) - pieces - 2]
    incoming = refs[len(refs) - pieces - 2 : len(refs) - 2]
    updated, residual = refs[-2:]
    width, clusters = base.shape
    me = lax.axis_index("inst")
    total = base[...]
    for mask, ref in zip(held_by[1:], held[1:], strict=True):
        shift = (me - (me ^ mask) + period) & (period - 1)
        total = total + chosen(table, shift) * ref[...]
    for ref in others:
        total = total + ref[...]
    total = total - landed(incoming, width, clusters)
    kept = jnp.where(rows[1:2, :] > 0.0, total, 0.0)
    residual[...] = kept
    updated[...] = held[0][...] - rows[0:1, :] * kept


def ordered_kernel(_, *refs):
    half = len(refs) // 2
    for origin, target in zip(refs[:half], refs[half:], strict=True):
        target[...] = origin[...]


def ordered(after, *values):
    return pl.pallas_call(
        ordered_kernel,
        out_shape=tuple(jax.ShapeDtypeStruct(value.shape, value.dtype) for value in values),
        in_specs=[VMEM] * (1 + len(values)),
        out_specs=(VMEM,) * len(values),
        compiler_params=ROOM,
        cost_estimate=FREE,
    )(after, *values)


def moved(value, axis, mask):
    count = lax.axis_size(axis)
    return lax.ppermute(value, axis, [(place, place ^ mask) for place in range(count)])


def stage_sent(sends, stage):
    radix, shift = stage
    turns = turns_of(radix)
    zones = lax.axis_size("zone")
    held = [sends[0]]
    for which in range(1, radix):
        pairs = []
        for place in range(zones):
            digit = (place >> shift) & (radix - 1)
            pairs.append((place, place + ((turns[which][digit] - digit) << shift)))
        held.append(lax.ppermute(sends[which], "zone", pairs))
    return held


def regrouped(held, radix):
    lanes = held[0].shape[1]
    cut = [piece.reshape(radix, -1, lanes) for piece in held]
    return [jnp.concatenate([piece[which] for piece in cut], axis=0) for which in range(radix)]


def on_device(
    state,
    source,
    jac_table,
    pattern_col,
    pattern_type,
    pseudo_step,
    zone_count,
    link_src,
    link_owner,
    link_dest,
    link_weight,
    iface_table,
):
    instances = lax.axis_size("inst")
    zones = lax.axis_size("zone")
    state_in = state[0].T
    source_t = source[0].T
    width, clusters = state_in.shape
    links = link_src.shape[1]
    slots_per = 2 * links // zones
    slots = zones * slots_per
    padded = -(-(width + 1) // LANES) * LANES
    table = coefficients(instances)
    block = jax.ShapeDtypeStruct((width, clusters), jnp.float32)

    stages = stages_of(zones)
    first = stages[0][0]
    share = jax.ShapeDtypeStruct((slots // first, padded), jnp.float32)
    state_t, *sends = pl.pallas_call(
        functools.partial(outgoing_kernel, stages, slots_per),
        out_shape=(block, *[share] * first),
        in_specs=[HBM] * 6,
        out_specs=(VMEM,) * (1 + first),
        scratch_shapes=[pltpu.VMEM((1, links), jnp.int32)] * 4
        + [pltpu.VMEM(iface_table.shape, jnp.float32), pltpu.SemaphoreType.DMA((6,))],
        compiler_params=ROOM,
    )(
        in_hbm(state_in),
        in_hbm(link_src),
        in_hbm(link_owner.reshape(1, links)),
        in_hbm(link_dest),
        in_hbm(link_weight),
        in_hbm(iface_table),
    )

    held, held_by = [state_t], [0]
    mask = 1
    while mask < instances // 2:
        arrivals = [moved(piece, "inst", mask) for piece in held]
        held = held + arrivals
        held_by = held_by + [by ^ mask for by in held_by]
        mask *= 2
    others = []
    if instances > 1:
        (combined,) = pl.pallas_call(
            functools.partial(combine_kernel, table, held_by, mask),
            out_shape=(block,),
            in_specs=[VMEM] * len(held),
            out_specs=(VMEM,),
            compiler_params=ROOM,
            cost_estimate=FREE,
        )(*held)
        others = [moved(combined, "inst", mask)]

    kinds = jac_table.shape[0]
    half = pl.pallas_call(
        half_kernel,
        out_shape=jax.ShapeDtypeStruct((width, clusters), jnp.bfloat16),
        in_specs=[VMEM] * 2,
        out_specs=VMEM,
        compiler_params=ROOM,
    )(state_t, combined)
    products = lax.dot_general(
        jac_table.reshape(kinds * width, width),
        half,
        (((1,), (0,)), ((), ())),
        preferred_element_type=jnp.float32,
    )

    pieces = ordered(products, *stage_sent(sends, stages[0]))
    for stage in stages[1:]:
        pieces = stage_sent(regrouped(pieces, stage[0]), stage)
    staying, *incoming = pieces

    column, kind = pattern_col.T, pattern_type.T
    base, rows = pl.pallas_call(
        functools.partial(local_kernel, table),
        out_shape=(block, jax.ShapeDtypeStruct((8, clusters), jnp.float32)),
        in_specs=[HBM] * 4 + [SMEM] + [VMEM] * 3,
        out_specs=(VMEM, VMEM),
        scratch_shapes=[
            pltpu.VMEM(column.shape, jnp.int32),
            pltpu.VMEM(kind.shape, jnp.int32),
            pltpu.VMEM((width, clusters), jnp.float32),
            pltpu.SemaphoreType.DMA((4,)),
        ],
        compiler_params=ROOM,
        cost_estimate=FREE,
    )(
        in_hbm(column),
        in_hbm(kind),
        in_hbm(source_t),
        in_hbm(pseudo_step),
        zone_count,
        state_t,
        products,
        staying,
    )

    updated, residual = pl.pallas_call(
        functools.partial(final_kernel, table, held_by, len(incoming)),
        out_shape=(block, block),
        in_specs=[VMEM] * (2 + len(held) + len(others) + len(incoming)),
        out_specs=(VMEM, VMEM),
        compiler_params=ROOM,
    )(base, rows, *held, *others, *incoming)
    return updated.T[None], residual.T[None]


def solution(mesh):
    placed = (
        P("inst", "zone", None),
        P("inst", "zone", None),
        P("zone", None, None),
        P("zone", None),
        P("zone", None),
        P("inst", "zone"),
        P("zone"),
        P("inst", "zone"),
        P("inst", "zone", None),
        P("inst", "zone"),
        P("inst", "zone"),
        P(),
    )
    return jax.shard_map(
        on_device,
        mesh=mesh,
        in_specs=placed,
        out_specs=(P("inst", "zone", None), P("inst", "zone", None)),
        check_vma=False,
    )
```

```python
import functools
import math

import jax
import jax.numpy as jnp
import numpy as np
from jax import lax
from jax.experimental import pallas as pl
from jax.experimental.pallas import tpu as pltpu
from jax.sharding import PartitionSpec as P

OMEGA = 0.25
NU = 0.1
LANES = 128
VMEM = pl.BlockSpec(memory_space=pltpu.VMEM)
SMEM = pl.BlockSpec(memory_space=pltpu.SMEM)
HBM = pl.BlockSpec(memory_space=pltpu.HBM)
FREE = pl.CostEstimate(flops=1, bytes_accessed=1, transcendentals=0)
ROOM = pltpu.CompilerParams(vmem_limit_bytes=6 << 20)


def in_hbm(value):
    return pltpu.with_memory_space_constraint(value, pltpu.HBM)


def coefficients(period):
    table = [NU * (period * period + 2) / 12.0]
    for shift in range(1, period):
        phase = math.pi * shift / period
        sign = -1.0 if shift % 2 else 1.0
        sine = math.sin(phase)
        table.append(OMEGA * sign * math.cos(phase) / sine + NU * sign / (2.0 * sine * sine))
    return [float(np.float32(entry)) for entry in table]


def chosen(table, index, dtype=jnp.float32):
    value = jnp.asarray(table[0], dtype)
    for position in range(1, len(table)):
        value = jnp.where(index == position, jnp.asarray(table[position], dtype), value)
    return value


def parts_of(value):
    high = value.astype(jnp.bfloat16)
    rest = value - high.astype(jnp.float32)
    middle = rest.astype(jnp.bfloat16)
    low = (rest - middle.astype(jnp.float32)).astype(jnp.bfloat16)
    return high, middle, low


def power_of_two(count):
    return count & (count - 1) == 0


def turns_of(radix, first):
    if radix == 4 and first:
        return ((0, 1, 2, 3), (1, 3, 2, 0), (2, 1, 0, 3), (3, 0, 1, 2), (0, 2, 3, 1))
    return tuple(tuple(digit ^ turn for digit in range(radix)) for turn in range(radix))


def stages_of(zones, instances):
    stages = []
    shift = zones.bit_length() - 1
    while shift:
        bits = 2 if shift > 1 else 1
        shift -= bits
        stages.append((turns_of(1 << bits, not stages and instances > 1), shift))
    return stages


def block_of(owner, me, stages):
    place = jnp.zeros_like(owner)
    for turns, shift in stages:
        radix = len(turns[0])
        mine = (me >> shift) & (radix - 1)
        theirs = (owner >> shift) & (radix - 1)
        turn = jnp.zeros_like(owner)
        for which in range(1, len(turns)):
            target = chosen(turns[which], mine, jnp.int32)
            turn = jnp.where((theirs == target) & (theirs != mine), which, turn)
        place = place * len(turns) + turn
    return place


def as_column(row):
    count = row.shape[1]
    lane = lax.broadcasted_iota(jnp.int32, (count, count), 1)
    sublane = lax.broadcasted_iota(jnp.int32, (count, count), 0)
    return jnp.sum(jnp.where(lane == sublane, row, jnp.zeros_like(row)), axis=1, keepdims=True)


def fetched(pairs, sems):
    copies = []
    for place, (origin, target) in enumerate(pairs):
        copy = pltpu.make_async_copy(origin, target, sems.at[place])
        copy.start()
        copies.append(copy)
    return copies


def outgoing_kernel(
    stages,
    slots_per,
    state_in,
    source_in,
    owner_in,
    dest_in,
    weight_in,
    table_in,
    state,
    *refs,
):
    *sends, source, owner, dest, weight, table, sems = refs
    copies = fetched(
        (
            (owner_in, owner),
            (source_in, source),
            (weight_in, weight),
            (dest_in, dest),
            (state_in, state),
            (table_in, table),
        ),
        sems,
    )
    width, clusters = state.shape
    links = owner.shape[1]
    sets = table.shape[0]
    share, lanes = sends[0].shape
    slots = share * len(sends)
    for copy in copies[:4]:
        copy.wait()
    owners = owner[...].astype(jnp.float32)
    lane = lax.broadcasted_iota(jnp.int32, (links, links), 1)
    sublane = lax.broadcasted_iota(jnp.int32, (links, links), 0)
    earlier = (as_column(owners) == owners) & (sublane < lane)
    rank = jnp.sum(jnp.where(earlier, 1.0, 0.0), axis=0, keepdims=True).astype(jnp.int32)
    slot = block_of(owner[...], lax.axis_index("zone"), stages) * slots_per + rank
    placing = lax.broadcasted_iota(jnp.int32, (slots, links), 0) == slot

    def of_slot(row):
        return jnp.sum(
            jnp.where(placing, row[...].astype(jnp.float32) + 1.0, 0.0), axis=1, keepdims=True
        ) - 1.0

    from_cluster, to_cluster, by_set = of_slot(source), of_slot(dest), of_slot(weight)
    pick = lax.broadcasted_iota(jnp.int32, (slots, clusters), 1) == from_cluster.astype(jnp.int32)
    pick = jnp.where(pick, 1.0, 0.0).astype(jnp.bfloat16)
    choose = lax.broadcasted_iota(jnp.int32, (slots, sets), 1) == by_set.astype(jnp.int32)
    choose = jnp.where(choose, 1.0, 0.0).astype(jnp.bfloat16)
    copies[5].wait()
    scales = jnp.zeros((slots, width), jnp.float32)
    for part in parts_of(table[...]):
        scales = scales + jnp.dot(choose, part, preferred_element_type=jnp.float32)
    copies[4].wait()
    parts = jnp.concatenate(parts_of(state[...]), axis=1)
    picked = lax.dot_general(
        jnp.concatenate([pick, pick, pick], axis=1),
        parts,
        (((1,), (1,)), ((), ())),
        preferred_element_type=jnp.float32,
    )
    blocks = picked * scales
    marks = jnp.broadcast_to(to_cluster, (slots, lanes - width))
    for place, send in enumerate(sends):
        rows = slice(place * share, (place + 1) * share)
        send[:, :width] = blocks[rows]
        send[:, width:] = marks[rows]


def half_kernel(state, _, half):
    half[...] = state[...].astype(jnp.bfloat16)


def landed(pieces, width, clusters):
    arrived = jnp.concatenate([piece[...] for piece in pieces], axis=0)
    target = arrived[:, width : width + 1].astype(jnp.int32)
    landing = lax.broadcasted_iota(jnp.int32, (arrived.shape[0], clusters), 1) == target
    landing = jnp.where(landing, 1.0, 0.0).astype(jnp.bfloat16)
    return lax.dot_general(
        jnp.concatenate(parts_of(arrived), axis=0),
        jnp.concatenate([landing, landing, landing], axis=0),
        (((0,), (0,)), ((), ())),
        preferred_element_type=jnp.float32,
    )[:width]


def local_kernel(
    table,
    column_in,
    kind_in,
    source_in,
    step_in,
    count,
    state,
    products,
    staying,
    base,
    rows,
    column,
    kind,
    source,
    sems,
):
    width, clusters = state.shape
    kinds = products.shape[0] // width
    step = rows.at[pl.ds(0, 1), :]
    copies = fetched(
        [(column_in, column), (kind_in, kind), (source_in, source), (step_in, step)], sems
    )
    total = chosen(table, 0) * state[...] - landed([staying], width, clusters)
    high, low = [], []
    for which in range(kinds):
        full = products[pl.ds(which * width, width), :]
        upper = full.astype(jnp.bfloat16)
        high.append(upper)
        low.append((full - upper.astype(jnp.float32)).astype(jnp.bfloat16))
    copies[0].wait()
    copies[1].wait()
    codes = column[...] + clusters * kind[...]
    row = lax.broadcasted_iota(jnp.int32, (clusters, clusters), 0)
    counts = []
    for which in range(kinds):
        count_of = jnp.zeros((clusters, clusters), jnp.float32)
        for entry in range(codes.shape[0]):
            hit = row == codes[entry : entry + 1, :] - which * clusters
            count_of = count_of + jnp.where(hit, 1.0, 0.0)
        counts.append(count_of.astype(jnp.bfloat16))
    counts = jnp.concatenate(counts, axis=0)
    for part in (high, low):
        total = total + jnp.dot(
            jnp.concatenate(part, axis=1), counts, preferred_element_type=jnp.float32
        )
    copies[2].wait()
    copies[3].wait()
    base[...] = total + source[...]
    active = lax.broadcasted_iota(jnp.int32, (1, clusters), 1) < count[0]
    rows[1:2, :] = jnp.where(active, 1.0, 0.0)


def combine_kernel(table, held_by, mask, *refs):
    period = len(table)
    me = lax.axis_index("inst")
    held, rest = refs[: len(held_by)], refs[len(held_by) :]
    passing = len(rest) // 2
    out = rest[passing]
    for origin, target in zip(rest[:passing], rest[passing + 1 :], strict=True):
        target[...] = origin[...]
    total = None
    for by, ref in zip(held_by, held, strict=True):
        shift = ((me ^ mask) - (me ^ by) + period) & (period - 1)
        term = chosen(table, shift) * ref[...]
        total = term if total is None else total + term
    out[...] = total


def final_kernel(table, held_by, pieces, base, rows, *refs):
    period = len(table)
    held = refs[: len(held_by)]
    others = refs[len(held_by) : len(refs) - pieces - 2]
    incoming = refs[len(refs) - pieces - 2 : len(refs) - 2]
    updated, residual = refs[-2:]
    width, clusters = base.shape
    me = lax.axis_index("inst")
    total = base[...]
    for mask, ref in zip(held_by[1:], held[1:], strict=True):
        shift = (me - (me ^ mask) + period) & (period - 1)
        total = total + chosen(table, shift) * ref[...]
    for ref in others:
        total = total + ref[...]
    total = total - landed(incoming, width, clusters)
    kept = jnp.where(rows[1:2, :] > 0.0, total, 0.0)
    residual[...] = kept
    updated[...] = held[0][...] - rows[0:1, :] * kept


def moved(value, axis, mask):
    count = lax.axis_size(axis)
    return lax.ppermute(value, axis, [(place, place ^ mask) for place in range(count)])


def stage_sent(sends, stage):
    turns, shift = stage
    radix = len(turns[0])
    instances, zones = lax.axis_size("inst"), lax.axis_size("zone")
    held = [sends[0]]
    for which in range(1, len(turns)):
        pairs = []
        for inst in range(instances):
            for zone in range(zones):
                digit = (zone >> shift) & (radix - 1)
                step = turns[which][digit] - digit
                place = inst * zones + zone
                target = place + (step << shift) if step else (inst ^ 1) * zones + zone
                pairs.append((place, target))
        held.append(lax.ppermute(sends[which], ("inst", "zone"), pairs))
    return held


def regroup_kernel(stage, _, *refs):
    turns, shift = stage
    radix = len(turns[0])
    held, outs = refs[: len(turns)], refs[len(turns) :]
    mine = (lax.axis_index("zone") >> shift) & (radix - 1)
    came = [[turn for turn in range(1, len(turns)) if turns[turn][d] != d] for d in range(radix)]
    pieces = [held[0][...]]
    for order in range(radix - 1):
        source = [came[digit][order] for digit in range(radix)]
        piece = held[source[0]][...]
        for digit in range(1, radix):
            if source[digit] != source[0]:
                piece = jnp.where(mine == digit, held[source[digit]][...], piece)
        pieces.append(piece)
    rows = pieces[0].shape[0] // len(outs)
    for which, out in enumerate(outs):
        for place, piece in enumerate(pieces):
            out[pl.ds(place * rows, rows), :] = piece[which * rows : (which + 1) * rows]


def regrouped(held, stage, next_turns, after):
    radix = len(stage[0][0])
    rows, lanes = held[0].shape
    out = jax.ShapeDtypeStruct((radix * rows // next_turns, lanes), jnp.float32)
    return pl.pallas_call(
        functools.partial(regroup_kernel, stage),
        out_shape=(out,) * next_turns,
        in_specs=[VMEM] * (1 + len(held)),
        out_specs=(VMEM,) * next_turns,
        compiler_params=ROOM,
    )(after, *held)


def on_device(
    state,
    source,
    jac_table,
    pattern_col,
    pattern_type,
    pseudo_step,
    zone_count,
    link_src,
    link_owner,
    link_dest,
    link_weight,
    iface_table,
):
    instances = lax.axis_size("inst")
    zones = lax.axis_size("zone")
    state_in = state[0].T
    source_t = source[0].T
    width, clusters = state_in.shape
    links = link_src.shape[1]
    slots_per = 2 * links // zones
    padded = -(-(width + 1) // LANES) * LANES
    table = coefficients(instances)
    block = jax.ShapeDtypeStruct((width, clusters), jnp.float32)

    stages = stages_of(zones, instances)
    turns = [len(stage[0]) for stage in stages] + [1]
    first = turns[0]
    share = jax.ShapeDtypeStruct((math.prod(turns[1:]) * slots_per, padded), jnp.float32)
    state_t, *sends = pl.pallas_call(
        functools.partial(outgoing_kernel, stages, slots_per),
        out_shape=(block, *[share] * first),
        in_specs=[HBM] * 6,
        out_specs=(VMEM,) * (1 + first),
        scratch_shapes=[pltpu.VMEM((1, links), jnp.int32)] * 4
        + [pltpu.VMEM(iface_table.shape, jnp.float32), pltpu.SemaphoreType.DMA((6,))],
        compiler_params=ROOM,
    )(
        in_hbm(state_in),
        in_hbm(link_src),
        in_hbm(link_owner.reshape(1, links)),
        in_hbm(link_dest),
        in_hbm(link_weight),
        in_hbm(iface_table),
    )

    held, held_by = [state_t], [0]
    mask = 1
    while mask < instances // 2:
        arrivals = [moved(piece, "inst", mask) for piece in held]
        held = held + arrivals
        held_by = held_by + [by ^ mask for by in held_by]
        mask *= 2
    others = []
    if instances > 1:
        (combined,) = pl.pallas_call(
            functools.partial(combine_kernel, table, held_by, instances - 1),
            out_shape=(block,),
            in_specs=[VMEM] * len(held),
            out_specs=(VMEM,),
            compiler_params=ROOM,
            cost_estimate=FREE,
        )(*held)
        others = [moved(combined, "inst", instances - 1)]

    pieces = sends
    for place, stage in enumerate(stages):
        if place:
            pieces = regrouped(pieces, stages[place - 1], turns[place], combined)
        pieces = stage_sent(pieces, stage)
    staying, *incoming = pieces

    kinds = jac_table.shape[0]
    half = pl.pallas_call(
        half_kernel,
        out_shape=jax.ShapeDtypeStruct((width, clusters), jnp.bfloat16),
        in_specs=[VMEM] * 2,
        out_specs=VMEM,
        compiler_params=ROOM,
    )(state_t, staying)
    products = lax.dot_general(
        jac_table.reshape(kinds * width, width),
        half,
        (((1,), (0,)), ((), ())),
        preferred_element_type=jnp.float32,
    )

    column, kind = pattern_col.T, pattern_type.T
    base, rows = pl.pallas_call(
        functools.partial(local_kernel, table),
        out_shape=(block, jax.ShapeDtypeStruct((8, clusters), jnp.float32)),
        in_specs=[HBM] * 4 + [SMEM] + [VMEM] * 3,
        out_specs=(VMEM, VMEM),
        scratch_shapes=[
            pltpu.VMEM(column.shape, jnp.int32),
            pltpu.VMEM(kind.shape, jnp.int32),
            pltpu.VMEM((width, clusters), jnp.float32),
            pltpu.SemaphoreType.DMA((4,)),
        ],
        compiler_params=ROOM,
        cost_estimate=FREE,
    )(
        in_hbm(column),
        in_hbm(kind),
        in_hbm(source_t),
        in_hbm(pseudo_step),
        zone_count,
        state_t,
        products,
        staying,
    )

    updated, residual = pl.pallas_call(
        functools.partial(final_kernel, table, held_by, len(incoming)),
        out_shape=(block, block),
        in_specs=[VMEM] * (2 + len(held) + len(others) + len(incoming)),
        out_specs=(VMEM, VMEM),
        compiler_params=ROOM,
    )(base, rows, *held, *others, *incoming)
    return updated.T[None], residual.T[None]


def solution(mesh):
    placed = (
        P("inst", "zone", None),
        P("inst", "zone", None),
        P("zone", None, None),
        P("zone", None),
        P("zone", None),
        P("inst", "zone"),
        P("zone"),
        P("inst", "zone"),
        P("inst", "zone", None),
        P("inst", "zone"),
        P("inst", "zone"),
        P(),
    )
    return jax.shard_map(
        on_device,
        mesh=mesh,
        in_specs=placed,
        out_specs=(P("inst", "zone", None), P("inst", "zone", None)),
        check_vma=False,
    )
```

```python
import functools
import math

import jax
import jax.numpy as jnp
import numpy as np
from jax import lax
from jax.experimental import pallas as pl
from jax.experimental.pallas import tpu as pltpu
from jax.sharding import PartitionSpec as P

OMEGA = 0.25
NU = 0.1
LANES = 128
VMEM = pl.BlockSpec(memory_space=pltpu.VMEM)
SMEM = pl.BlockSpec(memory_space=pltpu.SMEM)
HBM = pl.BlockSpec(memory_space=pltpu.HBM)
FREE = pl.CostEstimate(flops=1, bytes_accessed=1, transcendentals=0)
ROOM = pltpu.CompilerParams(vmem_limit_bytes=6 << 20)


def in_hbm(value):
    return pltpu.with_memory_space_constraint(value, pltpu.HBM)


def coefficients(period):
    table = [NU * (period * period + 2) / 12.0]
    for shift in range(1, period):
        phase = math.pi * shift / period
        sign = -1.0 if shift % 2 else 1.0
        sine = math.sin(phase)
        table.append(OMEGA * sign * math.cos(phase) / sine + NU * sign / (2.0 * sine * sine))
    return [float(np.float32(entry)) for entry in table]


def chosen(table, index, dtype=jnp.float32):
    value = jnp.asarray(table[0], dtype)
    for position in range(1, len(table)):
        value = jnp.where(index == position, jnp.asarray(table[position], dtype), value)
    return value


def parts_of(value):
    high = value.astype(jnp.bfloat16)
    rest = value - high.astype(jnp.float32)
    middle = rest.astype(jnp.bfloat16)
    low = (rest - middle.astype(jnp.float32)).astype(jnp.bfloat16)
    return high, middle, low


def power_of_two(count):
    return count & (count - 1) == 0


def turns_of(radix, last):
    if radix == 4 and last:
        return ((0, 1, 2, 3), (1, 3, 2, 0), (2, 1, 0, 3), (3, 0, 1, 2), (0, 2, 3, 1))
    return tuple(tuple(digit ^ turn for digit in range(radix)) for turn in range(radix))


def stages_of(zones, instances):
    stages = []
    shift, top = 0, zones.bit_length() - 1
    while shift < top:
        bits = 1 if (top - shift) % 2 else 2
        stages.append((turns_of(1 << bits, shift and shift + bits == top and instances > 1), shift))
        shift += bits
    return stages


def used_turns(turns, digit):
    return [turn for turn in range(1, len(turns)) if turns[turn][digit] != digit]


def block_of(owner, me, stages):
    place = jnp.zeros_like(owner)
    for turns, shift in stages:
        radix = len(turns[0])
        mine = (me >> shift) & (radix - 1)
        theirs = (owner >> shift) & (radix - 1)
        order = jnp.zeros_like(owner)
        for target in range(radix):
            orders = [0] * radix
            for digit in range(radix):
                for which, turn in enumerate(used_turns(turns, digit)):
                    if turns[turn][digit] == target:
                        orders[digit] = which + 1
            order = jnp.where(theirs == target, chosen(orders, mine, jnp.int32), order)
        place = place * radix + order
    return place


def as_column(row):
    count = row.shape[1]
    lane = lax.broadcasted_iota(jnp.int32, (count, count), 1)
    sublane = lax.broadcasted_iota(jnp.int32, (count, count), 0)
    return jnp.sum(jnp.where(lane == sublane, row, jnp.zeros_like(row)), axis=1, keepdims=True)


def fetched(pairs, sems):
    copies = []
    for place, (origin, target) in enumerate(pairs):
        copy = pltpu.make_async_copy(origin, target, sems.at[place])
        copy.start()
        copies.append(copy)
    return copies


def outgoing_kernel(
    stages,
    slots_per,
    state_in,
    source_in,
    owner_in,
    dest_in,
    weight_in,
    table_in,
    state,
    *refs,
):
    *sends, source, owner, dest, weight, table, sems = refs
    copies = fetched(
        (
            (owner_in, owner),
            (source_in, source),
            (weight_in, weight),
            (dest_in, dest),
            (state_in, state),
            (table_in, table),
        ),
        sems,
    )
    width, clusters = state.shape
    links = owner.shape[1]
    sets = table.shape[0]
    share, lanes = sends[0].shape
    slots = share * len(sends)
    for copy in copies[:4]:
        copy.wait()
    owners = owner[...].astype(jnp.float32)
    lane = lax.broadcasted_iota(jnp.int32, (links, links), 1)
    sublane = lax.broadcasted_iota(jnp.int32, (links, links), 0)
    earlier = (as_column(owners) == owners) & (sublane < lane)
    rank = jnp.sum(jnp.where(earlier, 1.0, 0.0), axis=0, keepdims=True).astype(jnp.int32)
    slot = block_of(owner[...], lax.axis_index("zone"), stages) * slots_per + rank
    placing = lax.broadcasted_iota(jnp.int32, (slots, links), 0) == slot

    def of_slot(row):
        return jnp.sum(
            jnp.where(placing, row[...].astype(jnp.float32) + 1.0, 0.0), axis=1, keepdims=True
        ) - 1.0

    from_cluster, to_cluster, by_set = of_slot(source), of_slot(dest), of_slot(weight)
    pick = lax.broadcasted_iota(jnp.int32, (slots, clusters), 1) == from_cluster.astype(jnp.int32)
    pick = jnp.where(pick, 1.0, 0.0).astype(jnp.bfloat16)
    choose = lax.broadcasted_iota(jnp.int32, (slots, sets), 1) == by_set.astype(jnp.int32)
    choose = jnp.where(choose, 1.0, 0.0).astype(jnp.bfloat16)
    copies[5].wait()
    scales = jnp.zeros((slots, width), jnp.float32)
    for part in parts_of(table[...]):
        scales = scales + jnp.dot(choose, part, preferred_element_type=jnp.float32)
    copies[4].wait()
    parts = jnp.concatenate(parts_of(state[...]), axis=1)
    picked = lax.dot_general(
        jnp.concatenate([pick, pick, pick], axis=1),
        parts,
        (((1,), (1,)), ((), ())),
        preferred_element_type=jnp.float32,
    )
    blocks = picked * scales
    marks = jnp.broadcast_to(to_cluster, (slots, lanes - width))
    for place, send in enumerate(sends):
        rows = slice(place * share, (place + 1) * share)
        send[:, :width] = blocks[rows]
        send[:, width:] = marks[rows]


def half_kernel(state, _, half):
    half[...] = state[...].astype(jnp.bfloat16)


def landed(pieces, width, clusters):
    arrived = jnp.concatenate([piece[...] for piece in pieces], axis=0)
    target = arrived[:, width : width + 1].astype(jnp.int32)
    landing = lax.broadcasted_iota(jnp.int32, (arrived.shape[0], clusters), 1) == target
    landing = jnp.where(landing, 1.0, 0.0).astype(jnp.bfloat16)
    return lax.dot_general(
        jnp.concatenate(parts_of(arrived), axis=0),
        jnp.concatenate([landing, landing, landing], axis=0),
        (((0,), (0,)), ((), ())),
        preferred_element_type=jnp.float32,
    )[:width]


def local_kernel(
    table,
    column_in,
    kind_in,
    source_in,
    step_in,
    count,
    state,
    products,
    staying,
    base,
    rows,
    column,
    kind,
    source,
    sems,
):
    width, clusters = state.shape
    kinds = products.shape[0] // width
    step = rows.at[pl.ds(0, 1), :]
    copies = fetched(
        [(column_in, column), (kind_in, kind), (source_in, source), (step_in, step)], sems
    )
    total = chosen(table, 0) * state[...] - landed([staying], width, clusters)
    high, low = [], []
    for which in range(kinds):
        full = products[pl.ds(which * width, width), :]
        upper = full.astype(jnp.bfloat16)
        high.append(upper)
        low.append((full - upper.astype(jnp.float32)).astype(jnp.bfloat16))
    copies[0].wait()
    copies[1].wait()
    codes = column[...] + clusters * kind[...]
    row = lax.broadcasted_iota(jnp.int32, (clusters, clusters), 0)
    counts = []
    for which in range(kinds):
        count_of = jnp.zeros((clusters, clusters), jnp.float32)
        for entry in range(codes.shape[0]):
            hit = row == codes[entry : entry + 1, :] - which * clusters
            count_of = count_of + jnp.where(hit, 1.0, 0.0)
        counts.append(count_of.astype(jnp.bfloat16))
    counts = jnp.concatenate(counts, axis=0)
    for part in (high, low):
        total = total + jnp.dot(
            jnp.concatenate(part, axis=1), counts, preferred_element_type=jnp.float32
        )
    copies[2].wait()
    copies[3].wait()
    base[...] = total + source[...]
    active = lax.broadcasted_iota(jnp.int32, (1, clusters), 1) < count[0]
    rows[1:2, :] = jnp.where(active, 1.0, 0.0)


def combine_kernel(table, held_by, mask, *refs):
    period = len(table)
    me = lax.axis_index("inst")
    held, rest = refs[: len(held_by)], refs[len(held_by) :]
    passing = len(rest) // 2
    out = rest[passing]
    for origin, target in zip(rest[:passing], rest[passing + 1 :], strict=True):
        target[...] = origin[...]
    total = None
    for by, ref in zip(held_by, held, strict=True):
        shift = ((me ^ mask) - (me ^ by) + period) & (period - 1)
        term = chosen(table, shift) * ref[...]
        total = term if total is None else total + term
    out[...] = total


def final_kernel(table, held_by, pieces, base, rows, *refs):
    period = len(table)
    held = refs[: len(held_by)]
    others = refs[len(held_by) : len(refs) - pieces - 2]
    incoming = refs[len(refs) - pieces - 2 : len(refs) - 2]
    updated, residual = refs[-2:]
    width, clusters = base.shape
    me = lax.axis_index("inst")
    total = base[...]
    for mask, ref in zip(held_by[1:], held[1:], strict=True):
        shift = (me - (me ^ mask) + period) & (period - 1)
        total = total + chosen(table, shift) * ref[...]
    for ref in others:
        total = total + ref[...]
    total = total - landed(incoming, width, clusters)
    kept = jnp.where(rows[1:2, :] > 0.0, total, 0.0)
    residual[...] = kept
    updated[...] = held[0][...] - rows[0:1, :] * kept


def moved(value, axis, mask):
    count = lax.axis_size(axis)
    return lax.ppermute(value, axis, [(place, place ^ mask) for place in range(count)])


def stage_sent(sends, stage):
    turns, shift = stage
    radix = len(turns[0])
    instances, zones = lax.axis_size("inst"), lax.axis_size("zone")
    held = [sends[0]]
    for which in range(1, len(turns)):
        pairs = []
        for inst in range(instances):
            for zone in range(zones):
                digit = (zone >> shift) & (radix - 1)
                step = turns[which][digit] - digit
                place = inst * zones + zone
                target = place + (step << shift) if step else (inst ^ 1) * zones + zone
                pairs.append((place, target))
        held.append(lax.ppermute(sends[which], ("inst", "zone"), pairs))
    return held


def regroup_kernel(stage, unit, _, *refs):
    turns, shift = stage
    radix = len(turns[0])
    outs = refs[-len(turns) :]
    block = unit // radix
    mine = (lax.axis_index("zone") >> shift) & (radix - 1)
    used = [used_turns(turns, digit) for digit in range(radix)]
    place = 0
    for ref in refs[: -len(turns)]:
        for start in range(0, ref.shape[0], unit):
            blocks = [ref[pl.ds(start + which * block, block), :] for which in range(radix)]
            rows = pl.ds(place * block, block)
            place += 1
            outs[0][rows, :] = blocks[0]
            for turn in range(1, len(turns)):
                value = None
                for which in range(radix - 1):
                    digits = [digit for digit in range(radix) if used[digit][which] == turn]
                    if len(digits) == radix:
                        value = blocks[which + 1]
                    elif digits:
                        here = chosen([int(digit in digits) for digit in range(radix)], mine, jnp.int32)
                        value = jnp.zeros_like(blocks[0]) if value is None else value
                        value = jnp.where(here == 1, blocks[which + 1], value)
                outs[turn][rows, :] = value


def regrouped(held, stage, unit, after):
    turns = stage[0]
    lanes = held[0].shape[1]
    rows = sum(piece.shape[0] for piece in held) // len(turns[0])
    out = jax.ShapeDtypeStruct((rows, lanes), jnp.float32)
    return pl.pallas_call(
        functools.partial(regroup_kernel, stage, unit),
        out_shape=(out,) * len(turns),
        in_specs=[VMEM] * (1 + len(held)),
        out_specs=(VMEM,) * len(turns),
        compiler_params=ROOM,
    )(after, *held)


def on_device(
    state,
    source,
    jac_table,
    pattern_col,
    pattern_type,
    pseudo_step,
    zone_count,
    link_src,
    link_owner,
    link_dest,
    link_weight,
    iface_table,
):
    instances = lax.axis_size("inst")
    zones = lax.axis_size("zone")
    state_in = state[0].T
    source_t = source[0].T
    width, clusters = state_in.shape
    links = link_src.shape[1]
    slots_per = 2 * links // zones
    padded = -(-(width + 1) // LANES) * LANES
    table = coefficients(instances)
    block = jax.ShapeDtypeStruct((width, clusters), jnp.float32)

    stages = stages_of(zones, instances)
    units = [zones * slots_per]
    for turns, _ in stages:
        units.append(units[-1] // len(turns[0]))
    first = len(stages[0][0])
    share = jax.ShapeDtypeStruct((units[1], padded), jnp.float32)
    state_t, *sends = pl.pallas_call(
        functools.partial(outgoing_kernel, stages, slots_per),
        out_shape=(block, *[share] * first),
        in_specs=[HBM] * 6,
        out_specs=(VMEM,) * (1 + first),
        scratch_shapes=[pltpu.VMEM((1, links), jnp.int32)] * 4
        + [pltpu.VMEM(iface_table.shape, jnp.float32), pltpu.SemaphoreType.DMA((6,))],
        compiler_params=ROOM,
    )(
        in_hbm(state_in),
        in_hbm(link_src),
        in_hbm(link_owner.reshape(1, links)),
        in_hbm(link_dest),
        in_hbm(link_weight),
        in_hbm(iface_table),
    )

    held, held_by = [state_t], [0]
    mask = 1
    while mask < instances // 2:
        arrivals = [moved(piece, "inst", mask) for piece in held]
        held = held + arrivals
        held_by = held_by + [by ^ mask for by in held_by]
        mask *= 2
    others = []
    if instances > 1:
        (combined,) = pl.pallas_call(
            functools.partial(combine_kernel, table, held_by, instances - 1),
            out_shape=(block,),
            in_specs=[VMEM] * len(held),
            out_specs=(VMEM,),
            compiler_params=ROOM,
            cost_estimate=FREE,
        )(*held)
        others = [moved(combined, "inst", instances - 1)]

    pieces = sends
    for place, stage in enumerate(stages):
        if place:
            pieces = regrouped(pieces, stage, units[place], combined)
        pieces = stage_sent(pieces, stage)
    staying, *incoming = pieces

    kinds = jac_table.shape[0]
    half = pl.pallas_call(
        half_kernel,
        out_shape=jax.ShapeDtypeStruct((width, clusters), jnp.bfloat16),
        in_specs=[VMEM] * 2,
        out_specs=VMEM,
        compiler_params=ROOM,
    )(state_t, staying)
    products = lax.dot_general(
        jac_table.reshape(kinds * width, width),
        half,
        (((1,), (0,)), ((), ())),
        preferred_element_type=jnp.float32,
    )

    column, kind = pattern_col.T, pattern_type.T
    base, rows = pl.pallas_call(
        functools.partial(local_kernel, table),
        out_shape=(block, jax.ShapeDtypeStruct((8, clusters), jnp.float32)),
        in_specs=[HBM] * 4 + [SMEM] + [VMEM] * 3,
        out_specs=(VMEM, VMEM),
        scratch_shapes=[
            pltpu.VMEM(column.shape, jnp.int32),
            pltpu.VMEM(kind.shape, jnp.int32),
            pltpu.VMEM((width, clusters), jnp.float32),
            pltpu.SemaphoreType.DMA((4,)),
        ],
        compiler_params=ROOM,
        cost_estimate=FREE,
    )(
        in_hbm(column),
        in_hbm(kind),
        in_hbm(source_t),
        in_hbm(pseudo_step),
        zone_count,
        state_t,
        products,
        staying,
    )

    updated, residual = pl.pallas_call(
        functools.partial(final_kernel, table, held_by, len(incoming)),
        out_shape=(block, block),
        in_specs=[VMEM] * (2 + len(held) + len(others) + len(incoming)),
        out_specs=(VMEM, VMEM),
        compiler_params=ROOM,
    )(base, rows, *held, *others, *incoming)
    return updated.T[None], residual.T[None]


def solution(mesh):
    placed = (
        P("inst", "zone", None),
        P("inst", "zone", None),
        P("zone", None, None),
        P("zone", None),
        P("zone", None),
        P("inst", "zone"),
        P("zone"),
        P("inst", "zone"),
        P("inst", "zone", None),
        P("inst", "zone"),
        P("inst", "zone"),
        P(),
    )
    return jax.shard_map(
        on_device,
        mesh=mesh,
        in_specs=placed,
        out_specs=(P("inst", "zone", None), P("inst", "zone", None)),
        check_vma=False,
    )
```

```python
import functools
import math

import jax
import jax.numpy as jnp
import numpy as np
from jax import lax
from jax.experimental import pallas as pl
from jax.experimental.pallas import tpu as pltpu
from jax.sharding import PartitionSpec as P

OMEGA = 0.25
NU = 0.1
LANES = 128
VMEM = pl.BlockSpec(memory_space=pltpu.VMEM)
SMEM = pl.BlockSpec(memory_space=pltpu.SMEM)
HBM = pl.BlockSpec(memory_space=pltpu.HBM)
FREE = pl.CostEstimate(flops=1, bytes_accessed=1, transcendentals=0)
ROOM = pltpu.CompilerParams(vmem_limit_bytes=6 << 20)


def in_hbm(value):
    return pltpu.with_memory_space_constraint(value, pltpu.HBM)


def coefficients(period):
    table = [NU * (period * period + 2) / 12.0]
    for shift in range(1, period):
        phase = math.pi * shift / period
        sign = -1.0 if shift % 2 else 1.0
        sine = math.sin(phase)
        table.append(OMEGA * sign * math.cos(phase) / sine + NU * sign / (2.0 * sine * sine))
    return [float(np.float32(entry)) for entry in table]


def chosen(table, index, dtype=jnp.float32):
    value = jnp.asarray(table[0], dtype)
    for position in range(1, len(table)):
        value = jnp.where(index == position, jnp.asarray(table[position], dtype), value)
    return value


def parts_of(value):
    high = value.astype(jnp.bfloat16)
    rest = value - high.astype(jnp.float32)
    middle = rest.astype(jnp.bfloat16)
    low = (rest - middle.astype(jnp.float32)).astype(jnp.bfloat16)
    return high, middle, low


def power_of_two(count):
    return count & (count - 1) == 0


def turns_of(radix, last):
    if radix == 4 and last:
        return ((0, 1, 2, 3), (1, 3, 2, 0), (2, 1, 0, 3), (3, 0, 1, 2), (0, 2, 3, 1))
    return tuple(tuple(digit ^ turn for digit in range(radix)) for turn in range(radix))


def stages_of(zones, instances):
    stages = []
    shift, top = 0, zones.bit_length() - 1
    while shift < top:
        bits = 1 if (top - shift) % 2 else 2
        stages.append((turns_of(1 << bits, shift and shift + bits == top and instances > 1), shift))
        shift += bits
    return stages


def used_turns(turns, digit):
    return [turn for turn in range(1, len(turns)) if turns[turn][digit] != digit]


def block_of(owner, me, stages):
    place = jnp.zeros_like(owner)
    for turns, shift in stages:
        radix = len(turns[0])
        mine = (me >> shift) & (radix - 1)
        theirs = (owner >> shift) & (radix - 1)
        order = jnp.zeros_like(owner)
        for target in range(radix):
            orders = [0] * radix
            for digit in range(radix):
                for which, turn in enumerate(used_turns(turns, digit)):
                    if turns[turn][digit] == target:
                        orders[digit] = which + 1
            order = jnp.where(theirs == target, chosen(orders, mine, jnp.int32), order)
        place = place * radix + order
    return place


def as_column(row):
    count = row.shape[1]
    lane = lax.broadcasted_iota(jnp.int32, (count, count), 1)
    sublane = lax.broadcasted_iota(jnp.int32, (count, count), 0)
    return jnp.sum(jnp.where(lane == sublane, row, jnp.zeros_like(row)), axis=1, keepdims=True)


def fetched(pairs, sems):
    copies = []
    for place, (origin, target) in enumerate(pairs):
        copy = pltpu.make_async_copy(origin, target, sems.at[place])
        copy.start()
        copies.append(copy)
    return copies


def outgoing_kernel(
    stages,
    slots_per,
    width,
    state_in,
    source_in,
    owner_in,
    dest_in,
    weight_in,
    table_in,
    state,
    *refs,
):
    *sends, source, owner, dest, weight, table, sems = refs
    copies = fetched(
        (
            (owner_in, owner),
            (source_in, source),
            (weight_in, weight),
            (dest_in, dest),
            (state_in, state.at[pl.ds(0, width), :]),
            (table_in, table),
        ),
        sems,
    )
    clusters = state.shape[1]
    links = owner.shape[1]
    sets = table.shape[0]
    share, lanes = sends[-1].shape
    slots = share * len(sends)
    for copy in copies[:4]:
        copy.wait()
    owners = owner[...].astype(jnp.float32)
    lane = lax.broadcasted_iota(jnp.int32, (links, links), 1)
    sublane = lax.broadcasted_iota(jnp.int32, (links, links), 0)
    earlier = (as_column(owners) == owners) & (sublane < lane)
    rank = jnp.sum(jnp.where(earlier, 1.0, 0.0), axis=0, keepdims=True).astype(jnp.int32)
    slot = block_of(owner[...], lax.axis_index("zone"), stages) * slots_per + rank
    placing = lax.broadcasted_iota(jnp.int32, (slots, links), 0) == slot

    def of_slot(row):
        return jnp.sum(
            jnp.where(placing, row[...].astype(jnp.float32) + 1.0, 0.0), axis=1, keepdims=True
        ) - 1.0

    from_cluster, to_cluster, by_set = of_slot(source), of_slot(dest), of_slot(weight)
    pick = lax.broadcasted_iota(jnp.int32, (slots, clusters), 1) == from_cluster.astype(jnp.int32)
    pick = jnp.where(pick, 1.0, 0.0).astype(jnp.bfloat16)
    choose = lax.broadcasted_iota(jnp.int32, (slots, sets), 1) == by_set.astype(jnp.int32)
    choose = jnp.where(choose, 1.0, 0.0).astype(jnp.bfloat16)
    copies[5].wait()
    scales = jnp.zeros((slots, width), jnp.float32)
    for part in parts_of(table[...]):
        scales = scales + jnp.dot(choose, part, preferred_element_type=jnp.float32)
    copies[4].wait()
    parts = jnp.concatenate(parts_of(state[pl.ds(0, width), :]), axis=1)
    picked = lax.dot_general(
        jnp.concatenate([pick, pick, pick], axis=1),
        parts,
        (((1,), (1,)), ((), ())),
        preferred_element_type=jnp.float32,
    )
    marks = jnp.broadcast_to(to_cluster, (slots, lanes - width))
    blocks = jnp.concatenate([picked * scales, marks], axis=1)
    for place, send in enumerate(sends):
        send[...] = blocks[place * share : place * share + send.shape[0]]
    trades = share - sends[0].shape[0]
    if trades:
        for start in range(0, lanes, clusters):
            rows = pl.ds(width + start // clusters * trades, trades)
            state[rows, :] = blocks[share - trades : share, start : start + clusters]


def half_kernel(state, _, half):
    half[...] = state[pl.ds(0, half.shape[0]), :].astype(jnp.bfloat16)


def landed(pieces, width, clusters):
    arrived = jnp.concatenate([piece[...] for piece in pieces], axis=0)
    target = arrived[:, width : width + 1].astype(jnp.int32)
    landing = lax.broadcasted_iota(jnp.int32, (arrived.shape[0], clusters), 1) == target
    landing = jnp.where(landing, 1.0, 0.0).astype(jnp.bfloat16)
    return lax.dot_general(
        jnp.concatenate(parts_of(arrived), axis=0),
        jnp.concatenate([landing, landing, landing], axis=0),
        (((0,), (0,)), ((), ())),
        preferred_element_type=jnp.float32,
    )[:width]


def local_kernel(
    table,
    column_in,
    kind_in,
    source_in,
    step_in,
    count,
    state,
    products,
    staying,
    base,
    rows,
    column,
    kind,
    source,
    sems,
):
    width, clusters = base.shape
    kinds = products.shape[0] // width
    step = rows.at[pl.ds(0, 1), :]
    copies = fetched(
        [(column_in, column), (kind_in, kind), (source_in, source), (step_in, step)], sems
    )
    total = chosen(table, 0) * state[pl.ds(0, width), :] - landed([staying], width, clusters)
    high, low = [], []
    for which in range(kinds):
        full = products[pl.ds(which * width, width), :]
        upper = full.astype(jnp.bfloat16)
        high.append(upper)
        low.append((full - upper.astype(jnp.float32)).astype(jnp.bfloat16))
    copies[0].wait()
    copies[1].wait()
    codes = column[...] + clusters * kind[...]
    row = lax.broadcasted_iota(jnp.int32, (clusters, clusters), 0)
    counts = []
    for which in range(kinds):
        count_of = jnp.zeros((clusters, clusters), jnp.float32)
        for entry in range(codes.shape[0]):
            hit = row == codes[entry : entry + 1, :] - which * clusters
            count_of = count_of + jnp.where(hit, 1.0, 0.0)
        counts.append(count_of.astype(jnp.bfloat16))
    counts = jnp.concatenate(counts, axis=0)
    for part in (high, low):
        total = total + jnp.dot(
            jnp.concatenate(part, axis=1), counts, preferred_element_type=jnp.float32
        )
    copies[2].wait()
    copies[3].wait()
    base[...] = total + source[...]
    active = lax.broadcasted_iota(jnp.int32, (1, clusters), 1) < count[0]
    rows[1:2, :] = jnp.where(active, 1.0, 0.0)


def combine_kernel(table, held_by, mask, *refs):
    period = len(table)
    me = lax.axis_index("inst")
    *held, out = refs
    total = None
    for by, ref in zip(held_by, held, strict=True):
        shift = ((me ^ mask) - (me ^ by) + period) & (period - 1)
        term = chosen(table, shift) * ref[pl.ds(0, out.shape[0]), :]
        total = term if total is None else total + term
    out[...] = total


def final_kernel(table, held_by, pieces, base, rows, *refs):
    period = len(table)
    held = refs[: len(held_by)]
    others = refs[len(held_by) : len(refs) - pieces - 2]
    incoming = refs[len(refs) - pieces - 2 : len(refs) - 2]
    updated, residual = refs[-2:]
    width, clusters = base.shape
    me = lax.axis_index("inst")
    total = base[...]
    for mask, ref in zip(held_by[1:], held[1:], strict=True):
        shift = (me - (me ^ mask) + period) & (period - 1)
        total = total + chosen(table, shift) * ref[pl.ds(0, width), :]
    for ref in others:
        total = total + ref[...]
    total = total - landed(incoming, width, clusters)
    kept = jnp.where(rows[1:2, :] > 0.0, total, 0.0)
    residual[...] = kept
    updated[...] = held[0][pl.ds(0, width), :] - rows[0:1, :] * kept


def moved(value, axis, mask):
    count = lax.axis_size(axis)
    return lax.ppermute(value, axis, [(place, place ^ mask) for place in range(count)])


def stage_sent(sends, stage, crossed=False):
    turns, shift = stage
    radix = len(turns[0])
    instances, zones = lax.axis_size("inst"), lax.axis_size("zone")
    held = [sends[0]]
    for which in range(1, len(turns)):
        pairs = []
        for inst in range(instances):
            for zone in range(zones):
                digit = (zone >> shift) & (radix - 1)
                step = turns[which][digit] - digit
                beside = inst ^ 1 if crossed or not step else inst
                pairs.append((inst * zones + zone, beside * zones + zone + (step << shift)))
        held.append(lax.ppermute(sends[which], ("inst", "zone"), pairs))
    return held


def regroup_kernel(stage, unit, _, *refs):
    turns, shift = stage
    radix = len(turns[0])
    outs = refs[-len(turns) :]
    block = unit // radix
    mine = (lax.axis_index("zone") >> shift) & (radix - 1)
    used = [used_turns(turns, digit) for digit in range(radix)]
    place = 0
    for ref in refs[: -len(turns)]:
        for start in range(0, ref.shape[0], unit):
            blocks = [ref[pl.ds(start + which * block, block), :] for which in range(radix)]
            rows = pl.ds(place * block, block)
            place += 1
            outs[0][rows, :] = blocks[0]
            for turn in range(1, len(turns)):
                value = None
                for which in range(radix - 1):
                    digits = [digit for digit in range(radix) if used[digit][which] == turn]
                    if len(digits) == radix:
                        value = blocks[which + 1]
                    elif digits:
                        here = chosen([int(digit in digits) for digit in range(radix)], mine, jnp.int32)
                        value = jnp.zeros_like(blocks[0]) if value is None else value
                        value = jnp.where(here == 1, blocks[which + 1], value)
                outs[turn][rows, :] = value


def by_digit(values, mine):
    value = values[0]
    for digit in range(1, len(values)):
        if values[digit] is not values[0]:
            value = jnp.where(mine == digit, values[digit], value)
    return value


def crossing_kernel(stage, block, _, beside, came, own, staying, *outs):
    staying[...] = own[...]
    turns, shift = stage
    radix = len(turns[0])
    clusters, lanes = beside.shape[1], came.shape[1]
    mine = (lax.axis_index("zone") >> shift) & (radix - 1)
    trades = (radix - 1) * block
    first = beside.shape[0] - lanes // clusters * trades
    keeps = [jnp.zeros((block, lanes), jnp.float32)]
    for which in range(radix - 1):
        tiles = [
            beside[pl.ds(first + tile * trades + which * block, block), :]
            for tile in range(lanes // clusters)
        ]
        keeps.append(jnp.concatenate(tiles, axis=1))
    comes = [came[pl.ds(which * block, block), :] for which in range(radix)]
    for turn, out in enumerate(outs, 1):
        orders = []
        for digit in range(radix):
            used = used_turns(turns, digit)
            orders.append(used.index(turn) + 1 if turn in used else 0)
        out[pl.ds(0, block), :] = by_digit([keeps[order] for order in orders], mine)
        out[pl.ds(block, block), :] = by_digit([comes[order] for order in orders], mine)


def crossing(stage, block, after, beside, came, own):
    turns = stage[0]
    out = jax.ShapeDtypeStruct((2 * block, came.shape[1]), jnp.float32)
    return pl.pallas_call(
        functools.partial(crossing_kernel, stage, block),
        out_shape=(jax.ShapeDtypeStruct(own.shape, own.dtype), *[out] * (len(turns) - 1)),
        in_specs=[VMEM] * 4,
        out_specs=(VMEM,) * len(turns),
        compiler_params=ROOM,
    )(after, beside, came, own)


def regrouped(held, stage, unit, after):
    turns = stage[0]
    lanes = held[0].shape[1]
    rows = sum(piece.shape[0] for piece in held) // len(turns[0])
    out = jax.ShapeDtypeStruct((rows, lanes), jnp.float32)
    return pl.pallas_call(
        functools.partial(regroup_kernel, stage, unit),
        out_shape=(out,) * len(turns),
        in_specs=[VMEM] * (1 + len(held)),
        out_specs=(VMEM,) * len(turns),
        compiler_params=ROOM,
    )(after, *held)


def on_device(
    state,
    source,
    jac_table,
    pattern_col,
    pattern_type,
    pseudo_step,
    zone_count,
    link_src,
    link_owner,
    link_dest,
    link_weight,
    iface_table,
):
    instances = lax.axis_size("inst")
    zones = lax.axis_size("zone")
    state_in = state[0].T
    source_t = source[0].T
    width, clusters = state_in.shape
    links = link_src.shape[1]
    slots_per = 2 * links // zones
    padded = -(-(width + 1) // LANES) * LANES
    table = coefficients(instances)
    block = jax.ShapeDtypeStruct((width, clusters), jnp.float32)

    stages = stages_of(zones, instances)
    units = [zones * slots_per]
    for turns, _ in stages:
        units.append(units[-1] // len(turns[0]))
    first = len(stages[0][0])
    crossed = len(stages) == 2 and len(stages[1][0]) == len(stages[1][0][0]) + 1
    crossed = crossed and instances >= 4 and clusters == LANES
    share = jax.ShapeDtypeStruct((units[1], padded), jnp.float32)
    shares, bundle = [share] * first, block
    if crossed:
        trades = (units[1] - units[2]) * padded // clusters
        bundle = jax.ShapeDtypeStruct((width + trades, clusters), jnp.float32)
        shares[0] = jax.ShapeDtypeStruct((units[2], padded), jnp.float32)
    state_t, *sends = pl.pallas_call(
        functools.partial(outgoing_kernel, stages, slots_per, width),
        out_shape=(bundle, *shares),
        in_specs=[HBM] * 6,
        out_specs=(VMEM,) * (1 + first),
        scratch_shapes=[pltpu.VMEM((1, links), jnp.int32)] * 4
        + [pltpu.VMEM(iface_table.shape, jnp.float32), pltpu.SemaphoreType.DMA((6,))],
        compiler_params=ROOM,
    )(
        in_hbm(state_in),
        in_hbm(link_src),
        in_hbm(link_owner.reshape(1, links)),
        in_hbm(link_dest),
        in_hbm(link_weight),
        in_hbm(iface_table),
    )

    held, held_by = [state_t], [0]
    mask = 1
    while mask < instances // 2:
        arrivals = [moved(piece, "inst", mask) for piece in held]
        held = held + arrivals
        held_by = held_by + [by ^ mask for by in held_by]
        mask *= 2
    others = []
    if instances > 1:
        (combined,) = pl.pallas_call(
            functools.partial(combine_kernel, table, held_by, instances - 1),
            out_shape=(block,),
            in_specs=[VMEM] * len(held),
            out_specs=(VMEM,),
            compiler_params=ROOM,
            cost_estimate=FREE,
        )(*held)
        others = [moved(combined, "inst", instances - 1)]

    if crossed:
        staying, came = stage_sent(sends, stages[0], True)
        pieces = crossing(stages[1], units[2], combined, held[1], came, staying)
        staying, *incoming = stage_sent(pieces, stages[1], True)
    else:
        pieces = sends
        for place, stage in enumerate(stages):
            if place:
                pieces = regrouped(pieces, stage, units[place], combined)
            pieces = stage_sent(pieces, stage)
        staying, *incoming = pieces

    kinds = jac_table.shape[0]
    half = pl.pallas_call(
        half_kernel,
        out_shape=jax.ShapeDtypeStruct((width, clusters), jnp.bfloat16),
        in_specs=[VMEM] * 2,
        out_specs=VMEM,
        compiler_params=ROOM,
    )(state_t, staying)
    products = lax.dot_general(
        jac_table.reshape(kinds * width, width),
        half,
        (((1,), (0,)), ((), ())),
        preferred_element_type=jnp.float32,
    )

    column, kind = pattern_col.T, pattern_type.T
    base, rows = pl.pallas_call(
        functools.partial(local_kernel, table),
        out_shape=(block, jax.ShapeDtypeStruct((8, clusters), jnp.float32)),
        in_specs=[HBM] * 4 + [SMEM] + [VMEM] * 3,
        out_specs=(VMEM, VMEM),
        scratch_shapes=[
            pltpu.VMEM(column.shape, jnp.int32),
            pltpu.VMEM(kind.shape, jnp.int32),
            pltpu.VMEM((width, clusters), jnp.float32),
            pltpu.SemaphoreType.DMA((4,)),
        ],
        compiler_params=ROOM,
        cost_estimate=FREE,
    )(
        in_hbm(column),
        in_hbm(kind),
        in_hbm(source_t),
        in_hbm(pseudo_step),
        zone_count,
        state_t,
        products,
        staying,
    )

    updated, residual = pl.pallas_call(
        functools.partial(final_kernel, table, held_by, len(incoming)),
        out_shape=(block, block),
        in_specs=[VMEM] * (2 + len(held) + len(others) + len(incoming)),
        out_specs=(VMEM, VMEM),
        compiler_params=ROOM,
    )(base, rows, *held, *others, *incoming)
    return updated.T[None], residual.T[None]


def solution(mesh):
    placed = (
        P("inst", "zone", None),
        P("inst", "zone", None),
        P("zone", None, None),
        P("zone", None),
        P("zone", None),
        P("inst", "zone"),
        P("zone"),
        P("inst", "zone"),
        P("inst", "zone", None),
        P("inst", "zone"),
        P("inst", "zone"),
        P(),
    )
    return jax.shard_map(
        on_device,
        mesh=mesh,
        in_specs=placed,
        out_specs=(P("inst", "zone", None), P("inst", "zone", None)),
        check_vma=False,
    )
```

```python
import functools
import math

import jax
import jax.numpy as jnp
import numpy as np
from jax import lax
from jax.experimental import pallas as pl
from jax.experimental.pallas import tpu as pltpu
from jax.sharding import PartitionSpec as P

OMEGA = 0.25
NU = 0.1
LANES = 128
VMEM = pl.BlockSpec(memory_space=pltpu.VMEM)
SMEM = pl.BlockSpec(memory_space=pltpu.SMEM)
HBM = pl.BlockSpec(memory_space=pltpu.HBM)
FREE = pl.CostEstimate(flops=1, bytes_accessed=1, transcendentals=0)
ROOM = pltpu.CompilerParams(vmem_limit_bytes=6 << 20)


def in_hbm(value):
    return pltpu.with_memory_space_constraint(value, pltpu.HBM)


def coefficients(period):
    table = [NU * (period * period + 2) / 12.0]
    for shift in range(1, period):
        phase = math.pi * shift / period
        sign = -1.0 if shift % 2 else 1.0
        sine = math.sin(phase)
        table.append(OMEGA * sign * math.cos(phase) / sine + NU * sign / (2.0 * sine * sine))
    return [float(np.float32(entry)) for entry in table]


def chosen(table, index, dtype=jnp.float32):
    value = jnp.asarray(table[0], dtype)
    for position in range(1, len(table)):
        value = jnp.where(index == position, jnp.asarray(table[position], dtype), value)
    return value


def parts_of(value):
    high = value.astype(jnp.bfloat16)
    rest = value - high.astype(jnp.float32)
    middle = rest.astype(jnp.bfloat16)
    low = (rest - middle.astype(jnp.float32)).astype(jnp.bfloat16)
    return high, middle, low


def power_of_two(count):
    return count & (count - 1) == 0


def turns_of(radix, last):
    if radix == 4 and last:
        return ((0, 1, 2, 3), (1, 3, 2, 0), (2, 1, 0, 3), (3, 0, 1, 2), (0, 2, 3, 1))
    return tuple(tuple(digit ^ turn for digit in range(radix)) for turn in range(radix))


def stages_of(zones, instances):
    stages = []
    shift, top = 0, zones.bit_length() - 1
    while shift < top:
        bits = 1 if (top - shift) % 2 else 2
        stages.append((turns_of(1 << bits, shift and shift + bits == top and instances > 1), shift))
        shift += bits
    return stages


def used_turns(turns, digit):
    return [turn for turn in range(1, len(turns)) if turns[turn][digit] != digit]


def block_of(owner, me, stages):
    place = jnp.zeros_like(owner)
    for turns, shift in stages:
        radix = len(turns[0])
        mine = (me >> shift) & (radix - 1)
        theirs = (owner >> shift) & (radix - 1)
        order = jnp.zeros_like(owner)
        for target in range(radix):
            orders = [0] * radix
            for digit in range(radix):
                for which, turn in enumerate(used_turns(turns, digit)):
                    if turns[turn][digit] == target:
                        orders[digit] = which + 1
            order = jnp.where(theirs == target, chosen(orders, mine, jnp.int32), order)
        place = place * radix + order
    return place


def as_column(row):
    count = row.shape[1]
    lane = lax.broadcasted_iota(jnp.int32, (count, count), 1)
    sublane = lax.broadcasted_iota(jnp.int32, (count, count), 0)
    return jnp.sum(jnp.where(lane == sublane, row, jnp.zeros_like(row)), axis=1, keepdims=True)


def fetched(pairs, sems):
    copies = []
    for place, (origin, target) in enumerate(pairs):
        copy = pltpu.make_async_copy(origin, target, sems.at[place])
        copy.start()
        copies.append(copy)
    return copies


def outgoing_kernel(
    stages,
    slots_per,
    width,
    state_in,
    source_in,
    owner_in,
    dest_in,
    weight_in,
    table_in,
    state,
    *refs,
):
    *sends, source, owner, dest, weight, table, sems = refs
    copies = fetched(
        (
            (owner_in, owner),
            (source_in, source),
            (weight_in, weight),
            (dest_in, dest),
            (state_in, state.at[pl.ds(0, width), :]),
            (table_in, table),
        ),
        sems,
    )
    clusters = state.shape[1]
    links = owner.shape[1]
    sets = table.shape[0]
    share, lanes = sends[-1].shape
    slots = share * len(sends)
    for copy in copies[:4]:
        copy.wait()
    owners = owner[...].astype(jnp.float32)
    lane = lax.broadcasted_iota(jnp.int32, (links, links), 1)
    sublane = lax.broadcasted_iota(jnp.int32, (links, links), 0)
    earlier = (as_column(owners) == owners) & (sublane < lane)
    rank = jnp.sum(jnp.where(earlier, 1.0, 0.0), axis=0, keepdims=True).astype(jnp.int32)
    slot = block_of(owner[...], lax.axis_index("zone"), stages) * slots_per + rank
    placing = lax.broadcasted_iota(jnp.int32, (slots, links), 0) == slot

    def of_slot(row):
        return jnp.sum(
            jnp.where(placing, row[...].astype(jnp.float32) + 1.0, 0.0), axis=1, keepdims=True
        ) - 1.0

    from_cluster, to_cluster, by_set = of_slot(source), of_slot(dest), of_slot(weight)
    pick = lax.broadcasted_iota(jnp.int32, (slots, clusters), 1) == from_cluster.astype(jnp.int32)
    pick = jnp.where(pick, 1.0, 0.0).astype(jnp.bfloat16)
    choose = lax.broadcasted_iota(jnp.int32, (slots, sets), 1) == by_set.astype(jnp.int32)
    choose = jnp.where(choose, 1.0, 0.0).astype(jnp.bfloat16)
    copies[5].wait()
    scales = jnp.zeros((slots, width), jnp.float32)
    for part in parts_of(table[...]):
        scales = scales + jnp.dot(choose, part, preferred_element_type=jnp.float32)
    copies[4].wait()
    parts = jnp.concatenate(parts_of(state[pl.ds(0, width), :]), axis=1)
    picked = lax.dot_general(
        jnp.concatenate([pick, pick, pick], axis=1),
        parts,
        (((1,), (1,)), ((), ())),
        preferred_element_type=jnp.float32,
    )
    marks = jnp.broadcast_to(to_cluster, (slots, lanes - width))
    blocks = jnp.concatenate([picked * scales, marks], axis=1)
    for place, send in enumerate(sends):
        send[...] = blocks[place * share : place * share + send.shape[0]]
    trades = share - sends[0].shape[0]
    if trades:
        for start in range(0, lanes, clusters):
            rows = pl.ds(width + start // clusters * trades, trades)
            state[rows, :] = blocks[share - trades : share, start : start + clusters]


def share_kernel(weight, state, _, half, share, none):
    value = state[pl.ds(0, half.shape[0]), :]
    half[...] = value.astype(jnp.bfloat16)
    share[...] = weight * value
    none[...] = jnp.zeros_like(none)


def landed(pieces, width, clusters):
    arrived = jnp.concatenate([piece[...] for piece in pieces], axis=0)
    target = arrived[:, width : width + 1].astype(jnp.int32)
    landing = lax.broadcasted_iota(jnp.int32, (arrived.shape[0], clusters), 1) == target
    landing = jnp.where(landing, 1.0, 0.0).astype(jnp.bfloat16)
    return lax.dot_general(
        jnp.concatenate(parts_of(arrived), axis=0),
        jnp.concatenate([landing, landing, landing], axis=0),
        (((0,), (0,)), ((), ())),
        preferred_element_type=jnp.float32,
    )[:width]


def local_kernel(codes, own, products, staying, base):
    width, clusters = base.shape
    kinds = products.shape[0] // width
    row = lax.broadcasted_iota(jnp.int32, (clusters, clusters), 0)
    high, low, counts = [], [], []
    for which in range(kinds):
        full = products[pl.ds(which * width, width), :]
        upper = full.astype(jnp.bfloat16)
        high.append(upper)
        low.append((full - upper.astype(jnp.float32)).astype(jnp.bfloat16))
        count = jnp.zeros((clusters, clusters), jnp.float32)
        for entry in range(codes.shape[0]):
            hit = row == codes[entry : entry + 1, :] - which * clusters
            count = count + jnp.where(hit, 1.0, 0.0)
        counts.append(count.astype(jnp.bfloat16))
    counts = jnp.concatenate(counts, axis=0)
    total = own[...] - landed([staying], width, clusters)
    for part in (high, low):
        total = total + jnp.dot(
            jnp.concatenate(part, axis=1), counts, preferred_element_type=jnp.float32
        )
    base[...] = total


def early_kernel(before, *refs):
    *pieces, base = refs
    base[...] = before[...] - landed(pieces, *base.shape)


def combine_kernel(table, held_by, mask, *refs):
    period = len(table)
    me = lax.axis_index("inst")
    *held, out = refs
    total = None
    for by, ref in zip(held_by, held, strict=True):
        shift = ((me ^ mask) - (me ^ by) + period) & (period - 1)
        term = chosen(table, shift) * ref[pl.ds(0, out.shape[0]), :]
        total = term if total is None else total + term
    out[...] = total


def final_kernel(table, held_by, pieces, base, rows, *refs):
    period = len(table)
    held = refs[: len(held_by)]
    others = refs[len(held_by) : len(refs) - pieces - 2]
    incoming = refs[len(refs) - pieces - 2 : len(refs) - 2]
    updated, residual = refs[-2:]
    width, clusters = base.shape
    me = lax.axis_index("inst")
    total = base[...]
    for mask, ref in zip(held_by[1:], held[1:], strict=True):
        shift = (me - (me ^ mask) + period) & (period - 1)
        total = total + chosen(table, shift) * ref[pl.ds(0, width), :]
    for ref in others:
        total = total + ref[...]
    total = total - landed(incoming, width, clusters)
    kept = jnp.where(rows[1:2, :] > 0.0, total, 0.0)
    residual[...] = kept
    updated[...] = held[0][pl.ds(0, width), :] - rows[0:1, :] * kept


def moved(value, axis, mask):
    count = lax.axis_size(axis)
    return lax.ppermute(value, axis, [(place, place ^ mask) for place in range(count)])


def stage_sent(sends, stage, crossed=False):
    turns, shift = stage
    radix = len(turns[0])
    instances, zones = lax.axis_size("inst"), lax.axis_size("zone")
    held = [sends[0]]
    for which in range(1, len(turns)):
        pairs = []
        for inst in range(instances):
            for zone in range(zones):
                digit = (zone >> shift) & (radix - 1)
                step = turns[which][digit] - digit
                beside = inst ^ 1 if crossed or not step else inst
                pairs.append((inst * zones + zone, beside * zones + zone + (step << shift)))
        held.append(lax.ppermute(sends[which], ("inst", "zone"), pairs))
    return held


def regroup_kernel(stage, unit, _, *refs):
    turns, shift = stage
    radix = len(turns[0])
    outs = refs[-len(turns) :]
    block = unit // radix
    mine = (lax.axis_index("zone") >> shift) & (radix - 1)
    used = [used_turns(turns, digit) for digit in range(radix)]
    place = 0
    for ref in refs[: -len(turns)]:
        for start in range(0, ref.shape[0], unit):
            blocks = [ref[pl.ds(start + which * block, block), :] for which in range(radix)]
            rows = pl.ds(place * block, block)
            place += 1
            outs[0][rows, :] = blocks[0]
            for turn in range(1, len(turns)):
                value = None
                for which in range(radix - 1):
                    digits = [digit for digit in range(radix) if used[digit][which] == turn]
                    if len(digits) == radix:
                        value = blocks[which + 1]
                    elif digits:
                        here = chosen([int(digit in digits) for digit in range(radix)], mine, jnp.int32)
                        value = jnp.zeros_like(blocks[0]) if value is None else value
                        value = jnp.where(here == 1, blocks[which + 1], value)
                outs[turn][rows, :] = value


def by_digit(values, mine):
    value = values[0]
    for digit in range(1, len(values)):
        if values[digit] is not values[0]:
            value = jnp.where(mine == digit, values[digit], value)
    return value


def crossing_kernel(stage, block, _, beside, came, own, staying, *outs):
    staying[...] = own[...]
    turns, shift = stage
    radix = len(turns[0])
    clusters, lanes = beside.shape[1], came.shape[1]
    mine = (lax.axis_index("zone") >> shift) & (radix - 1)
    trades = (radix - 1) * block
    first = beside.shape[0] - lanes // clusters * trades
    keeps = [jnp.zeros((block, lanes), jnp.float32)]
    for which in range(radix - 1):
        tiles = [
            beside[pl.ds(first + tile * trades + which * block, block), :]
            for tile in range(lanes // clusters)
        ]
        keeps.append(jnp.concatenate(tiles, axis=1))
    comes = [came[pl.ds(which * block, block), :] for which in range(radix)]
    for turn, out in enumerate(outs, 1):
        orders = []
        for digit in range(radix):
            used = used_turns(turns, digit)
            orders.append(used.index(turn) + 1 if turn in used else 0)
        out[pl.ds(0, block), :] = by_digit([keeps[order] for order in orders], mine)
        out[pl.ds(block, block), :] = by_digit([comes[order] for order in orders], mine)


def crossing(stage, block, after, beside, came, own):
    turns = stage[0]
    out = jax.ShapeDtypeStruct((2 * block, came.shape[1]), jnp.float32)
    return pl.pallas_call(
        functools.partial(crossing_kernel, stage, block),
        out_shape=(jax.ShapeDtypeStruct(own.shape, own.dtype), *[out] * (len(turns) - 1)),
        in_specs=[VMEM] * 4,
        out_specs=(VMEM,) * len(turns),
        compiler_params=ROOM,
    )(after, beside, came, own)


def regrouped(held, stage, unit, after):
    turns = stage[0]
    lanes = held[0].shape[1]
    rows = sum(piece.shape[0] for piece in held) // len(turns[0])
    out = jax.ShapeDtypeStruct((rows, lanes), jnp.float32)
    return pl.pallas_call(
        functools.partial(regroup_kernel, stage, unit),
        out_shape=(out,) * len(turns),
        in_specs=[VMEM] * (1 + len(held)),
        out_specs=(VMEM,) * len(turns),
        compiler_params=ROOM,
    )(after, *held)


def on_device(
    state,
    source,
    jac_table,
    pattern_col,
    pattern_type,
    pseudo_step,
    zone_count,
    link_src,
    link_owner,
    link_dest,
    link_weight,
    iface_table,
):
    instances = lax.axis_size("inst")
    zones = lax.axis_size("zone")
    state_in = state[0].T
    source_t = source[0].T
    width, clusters = state_in.shape
    links = link_src.shape[1]
    slots_per = 2 * links // zones
    padded = -(-(width + 1) // LANES) * LANES
    table = coefficients(instances)
    block = jax.ShapeDtypeStruct((width, clusters), jnp.float32)

    stages = stages_of(zones, instances)
    units = [zones * slots_per]
    for turns, _ in stages:
        units.append(units[-1] // len(turns[0]))
    first = len(stages[0][0])
    crossed = len(stages) == 2 and len(stages[1][0]) == len(stages[1][0][0]) + 1
    crossed = crossed and instances >= 4 and clusters == LANES
    share = jax.ShapeDtypeStruct((units[1], padded), jnp.float32)
    shares, bundle = [share] * first, block
    if crossed:
        trades = (units[1] - units[2]) * padded // clusters
        bundle = jax.ShapeDtypeStruct((width + trades, clusters), jnp.float32)
        shares[0] = jax.ShapeDtypeStruct((units[2], padded), jnp.float32)
    state_t, *sends = pl.pallas_call(
        functools.partial(outgoing_kernel, stages, slots_per, width),
        out_shape=(bundle, *shares),
        in_specs=[HBM] * 6,
        out_specs=(VMEM,) * (1 + first),
        scratch_shapes=[pltpu.VMEM((1, links), jnp.int32)] * 4
        + [pltpu.VMEM(iface_table.shape, jnp.float32), pltpu.SemaphoreType.DMA((6,))],
        compiler_params=ROOM,
    )(
        in_hbm(state_in),
        in_hbm(link_src),
        in_hbm(link_owner.reshape(1, links)),
        in_hbm(link_dest),
        in_hbm(link_weight),
        in_hbm(iface_table),
    )

    held, held_by = [state_t], [0]
    mask = 1
    while mask < instances // 2:
        arrivals = [moved(piece, "inst", mask) for piece in held]
        held = held + arrivals
        held_by = held_by + [by ^ mask for by in held_by]
        mask *= 2
    others = []
    if instances > 1:
        (combined,) = pl.pallas_call(
            functools.partial(combine_kernel, table, held_by, instances - 1),
            out_shape=(block,),
            in_specs=[VMEM] * len(held),
            out_specs=(VMEM,),
            compiler_params=ROOM,
            cost_estimate=FREE,
        )(*held)
        others = [moved(combined, "inst", instances - 1)]

    if crossed:
        staying, came = stage_sent(sends, stages[0], True)
        pieces = crossing(stages[1], units[2], combined, held[1], came, staying)
        staying, *incoming = stage_sent(pieces, stages[1], True)
    else:
        pieces = sends
        for place, stage in enumerate(stages):
            if place:
                pieces = regrouped(pieces, stage, units[place], combined)
            pieces = stage_sent(pieces, stage)
        staying, *incoming = pieces

    kinds = jac_table.shape[0]
    codes = pattern_col.T, pattern_type.T
    half, own, none = pl.pallas_call(
        functools.partial(share_kernel, table[0]),
        out_shape=(
            jax.ShapeDtypeStruct((width, clusters), jnp.bfloat16),
            block,
            jax.ShapeDtypeStruct(codes[0].shape, jnp.int32),
        ),
        in_specs=[VMEM] * 2,
        out_specs=(VMEM,) * 3,
        compiler_params=ROOM,
    )(state_t, staying)
    products = lax.dot_general(
        jac_table.reshape(kinds * width, width),
        half,
        (((1,), (0,)), ((), ())),
        preferred_element_type=jnp.float32,
    )

    codes = codes[0] + clusters * codes[1] + none
    active = lax.broadcasted_iota(jnp.int32, (1, clusters), 1) + none[:1] < zone_count[0]
    rows = jnp.concatenate([pseudo_step, active.astype(jnp.float32)], axis=0)
    base = pl.pallas_call(
        local_kernel,
        out_shape=block,
        in_specs=[VMEM] * 4,
        out_specs=VMEM,
        compiler_params=ROOM,
        cost_estimate=FREE,
    )(codes, own, products, staying)
    base = base + source_t
    early = len(incoming) // 2
    if early:
        base = pl.pallas_call(
            early_kernel,
            out_shape=block,
            in_specs=[VMEM] * (1 + early),
            out_specs=VMEM,
            compiler_params=ROOM,
            cost_estimate=FREE,
        )(base, *incoming[:early])
        incoming = incoming[early:]

    updated, residual = pl.pallas_call(
        functools.partial(final_kernel, table, held_by, len(incoming)),
        out_shape=(block, block),
        in_specs=[VMEM] * (2 + len(held) + len(others) + len(incoming)),
        out_specs=(VMEM, VMEM),
        compiler_params=ROOM,
    )(base, rows, *held, *others, *incoming)
    return updated.T[None], residual.T[None]


def solution(mesh):
    placed = (
        P("inst", "zone", None),
        P("inst", "zone", None),
        P("zone", None, None),
        P("zone", None),
        P("zone", None),
        P("inst", "zone"),
        P("zone"),
        P("inst", "zone"),
        P("inst", "zone", None),
        P("inst", "zone"),
        P("inst", "zone"),
        P(),
    )
    return jax.shard_map(
        on_device,
        mesh=mesh,
        in_specs=placed,
        out_specs=(P("inst", "zone", None), P("inst", "zone", None)),
        check_vma=False,
    )
```

```python
import functools
import math

import jax
import jax.numpy as jnp
import numpy as np
from jax import lax
from jax.experimental import pallas as pl
from jax.experimental.pallas import tpu as pltpu
from jax.sharding import PartitionSpec as P

OMEGA = 0.25
NU = 0.1
LANES = 128
VMEM = pl.BlockSpec(memory_space=pltpu.VMEM)
SMEM = pl.BlockSpec(memory_space=pltpu.SMEM)
HBM = pl.BlockSpec(memory_space=pltpu.HBM)
FREE = pl.CostEstimate(flops=1, bytes_accessed=1, transcendentals=0)
ROOM = pltpu.CompilerParams(vmem_limit_bytes=6 << 20)


def in_hbm(value):
    return pltpu.with_memory_space_constraint(value, pltpu.HBM)


def coefficients(period):
    table = [NU * (period * period + 2) / 12.0]
    for shift in range(1, period):
        phase = math.pi * shift / period
        sign = -1.0 if shift % 2 else 1.0
        sine = math.sin(phase)
        table.append(OMEGA * sign * math.cos(phase) / sine + NU * sign / (2.0 * sine * sine))
    return [float(np.float32(entry)) for entry in table]


def chosen(table, index, dtype=jnp.float32):
    value = jnp.asarray(table[0], dtype)
    for position in range(1, len(table)):
        value = jnp.where(index == position, jnp.asarray(table[position], dtype), value)
    return value


def parts_of(value):
    high = value.astype(jnp.bfloat16)
    rest = value - high.astype(jnp.float32)
    middle = rest.astype(jnp.bfloat16)
    low = (rest - middle.astype(jnp.float32)).astype(jnp.bfloat16)
    return high, middle, low


def power_of_two(count):
    return count & (count - 1) == 0


def turns_of(radix, last):
    if radix == 4 and last:
        return ((0, 1, 2, 3), (1, 3, 2, 0), (2, 1, 0, 3), (3, 0, 1, 2), (0, 2, 3, 1))
    return tuple(tuple(digit ^ turn for digit in range(radix)) for turn in range(radix))


def stages_of(zones, instances):
    stages = []
    shift, top = 0, zones.bit_length() - 1
    while shift < top:
        bits = 1 if (top - shift) % 2 else 2
        stages.append((turns_of(1 << bits, shift and shift + bits == top and instances > 1), shift))
        shift += bits
    return stages


def used_turns(turns, digit):
    return [turn for turn in range(1, len(turns)) if turns[turn][digit] != digit]


def block_of(owner, me, stages):
    place = jnp.zeros_like(owner)
    for turns, shift in stages:
        radix = len(turns[0])
        mine = (me >> shift) & (radix - 1)
        theirs = (owner >> shift) & (radix - 1)
        order = jnp.zeros_like(owner)
        for target in range(radix):
            orders = [0] * radix
            for digit in range(radix):
                for which, turn in enumerate(used_turns(turns, digit)):
                    if turns[turn][digit] == target:
                        orders[digit] = which + 1
            order = jnp.where(theirs == target, chosen(orders, mine, jnp.int32), order)
        place = place * radix + order
    return place


def as_column(row):
    count = row.shape[1]
    lane = lax.broadcasted_iota(jnp.int32, (count, count), 1)
    sublane = lax.broadcasted_iota(jnp.int32, (count, count), 0)
    return jnp.sum(jnp.where(lane == sublane, row, jnp.zeros_like(row)), axis=1, keepdims=True)


def fetched(pairs, sems):
    copies = []
    for place, (origin, target) in enumerate(pairs):
        copy = pltpu.make_async_copy(origin, target, sems.at[place])
        copy.start()
        copies.append(copy)
    return copies


def outgoing_kernel(
    stages,
    slots_per,
    width,
    state_in,
    source_in,
    owner_in,
    dest_in,
    weight_in,
    table_in,
    state,
    *refs,
):
    *sends, source, owner, dest, weight, table, sems = refs
    copies = fetched(
        (
            (owner_in, owner),
            (source_in, source),
            (weight_in, weight),
            (dest_in, dest),
            (state_in, state.at[pl.ds(0, width), :]),
            (table_in, table),
        ),
        sems,
    )
    clusters = state.shape[1]
    links = owner.shape[1]
    sets = table.shape[0]
    share, lanes = sends[-1].shape
    slots = share * len(sends)
    for copy in copies[:4]:
        copy.wait()
    owners = owner[...].astype(jnp.float32)
    lane = lax.broadcasted_iota(jnp.int32, (links, links), 1)
    sublane = lax.broadcasted_iota(jnp.int32, (links, links), 0)
    earlier = (as_column(owners) == owners) & (sublane < lane)
    rank = jnp.sum(jnp.where(earlier, 1.0, 0.0), axis=0, keepdims=True).astype(jnp.int32)
    slot = block_of(owner[...], lax.axis_index("zone"), stages) * slots_per + rank
    placing = lax.broadcasted_iota(jnp.int32, (slots, links), 0) == slot

    def of_slot(row):
        return jnp.sum(
            jnp.where(placing, row[...].astype(jnp.float32) + 1.0, 0.0), axis=1, keepdims=True
        ) - 1.0

    from_cluster, to_cluster, by_set = of_slot(source), of_slot(dest), of_slot(weight)
    pick = lax.broadcasted_iota(jnp.int32, (slots, clusters), 1) == from_cluster.astype(jnp.int32)
    pick = jnp.where(pick, 1.0, 0.0).astype(jnp.bfloat16)
    choose = lax.broadcasted_iota(jnp.int32, (slots, sets), 1) == by_set.astype(jnp.int32)
    choose = jnp.where(choose, 1.0, 0.0).astype(jnp.bfloat16)
    copies[5].wait()
    scales = jnp.zeros((slots, width), jnp.float32)
    for part in parts_of(table[...]):
        scales = scales + jnp.dot(choose, part, preferred_element_type=jnp.float32)
    copies[4].wait()
    parts = jnp.concatenate(parts_of(state[pl.ds(0, width), :]), axis=1)
    picked = lax.dot_general(
        jnp.concatenate([pick, pick, pick], axis=1),
        parts,
        (((1,), (1,)), ((), ())),
        preferred_element_type=jnp.float32,
    )
    marks = jnp.broadcast_to(to_cluster, (slots, lanes - width))
    blocks = jnp.concatenate([picked * scales, marks], axis=1)
    for place, send in enumerate(sends):
        send[...] = blocks[place * share : place * share + send.shape[0]]
    trades = share - sends[0].shape[0]
    if trades:
        for start in range(0, lanes, clusters):
            rows = pl.ds(width + start // clusters * trades, trades)
            state[rows, :] = blocks[share - trades : share, start : start + clusters]


def share_kernel(weight, state, _, half, share, none):
    value = state[pl.ds(0, half.shape[0]), :]
    half[...] = value.astype(jnp.bfloat16)
    share[...] = weight * value
    none[...] = jnp.zeros_like(none)


def landed(pieces, width, clusters):
    arrived = [piece[...] for piece in pieces]
    short = -sum(piece.shape[0] for piece in arrived) % 16
    if short:
        arrived.append(jnp.zeros((short, arrived[0].shape[1]), jnp.float32))
    arrived = jnp.concatenate(arrived, axis=0)
    target = arrived[:, width : width + 1].astype(jnp.int32)
    landing = lax.broadcasted_iota(jnp.int32, (arrived.shape[0], clusters), 1) == target
    landing = jnp.where(landing, 1.0, 0.0).astype(jnp.bfloat16)
    return lax.dot_general(
        jnp.concatenate(parts_of(arrived), axis=0),
        jnp.concatenate([landing, landing, landing], axis=0),
        (((0,), (0,)), ((), ())),
        preferred_element_type=jnp.float32,
    )[:width]


def local_kernel(codes, own, products, staying, base):
    width, clusters = base.shape
    kinds = products.shape[0] // width
    row = lax.broadcasted_iota(jnp.int32, (clusters, clusters), 0)
    high, low, counts = [], [], []
    for which in range(kinds):
        full = products[pl.ds(which * width, width), :]
        upper = full.astype(jnp.bfloat16)
        high.append(upper)
        low.append((full - upper.astype(jnp.float32)).astype(jnp.bfloat16))
        count = jnp.zeros((clusters, clusters), jnp.float32)
        for entry in range(codes.shape[0]):
            hit = row == codes[entry : entry + 1, :] - which * clusters
            count = count + jnp.where(hit, 1.0, 0.0)
        counts.append(count.astype(jnp.bfloat16))
    counts = jnp.concatenate(counts, axis=0)
    total = own[...] - landed([staying], width, clusters)
    for part in (high, low):
        total = total + jnp.dot(
            jnp.concatenate(part, axis=1), counts, preferred_element_type=jnp.float32
        )
    base[...] = total


def early_kernel(table, held_by, pieces, before, *refs):
    period = len(table)
    held = refs[: len(held_by)]
    others = refs[len(held_by) : len(refs) - pieces - 1]
    base = refs[-1]
    width, clusters = base.shape
    me = lax.axis_index("inst")
    total = before[...]
    for mask, ref in zip(held_by, held, strict=True):
        shift = (me - (me ^ mask) + period) & (period - 1)
        total = total + chosen(table, shift) * ref[pl.ds(0, width), :]
    for ref in others:
        total = total + ref[...]
    if pieces:
        total = total - landed(refs[len(refs) - pieces - 1 : -1], width, clusters)
    base[...] = total


def combine_kernel(table, held_by, mask, *refs):
    period = len(table)
    me = lax.axis_index("inst")
    *held, out = refs
    total = None
    for by, ref in zip(held_by, held, strict=True):
        shift = ((me ^ mask) - (me ^ by) + period) & (period - 1)
        term = chosen(table, shift) * ref[pl.ds(0, out.shape[0]), :]
        total = term if total is None else total + term
    out[...] = total


def final_kernel(base, rows, state, *refs):
    *incoming, updated, residual = refs
    width, clusters = base.shape
    total = base[...] - landed(incoming, width, clusters)
    kept = jnp.where(rows[1:2, :] > 0.0, total, 0.0)
    residual[...] = kept
    updated[...] = state[pl.ds(0, width), :] - rows[0:1, :] * kept


def moved(value, axis, mask):
    count = lax.axis_size(axis)
    return lax.ppermute(value, axis, [(place, place ^ mask) for place in range(count)])


def stage_sent(sends, stage, crossed=False):
    turns, shift = stage
    radix = len(turns[0])
    instances, zones = lax.axis_size("inst"), lax.axis_size("zone")
    held = [sends[0]]
    for which in range(1, len(turns)):
        pairs = []
        for inst in range(instances):
            for zone in range(zones):
                digit = (zone >> shift) & (radix - 1)
                step = turns[which][digit] - digit
                beside = inst ^ 1 if crossed or not step else inst
                pairs.append((inst * zones + zone, beside * zones + zone + (step << shift)))
        held.append(lax.ppermute(sends[which], ("inst", "zone"), pairs))
    return held


def regroup_kernel(stage, unit, _, *refs):
    turns, shift = stage
    radix = len(turns[0])
    outs = refs[-len(turns) :]
    block = unit // radix
    mine = (lax.axis_index("zone") >> shift) & (radix - 1)
    used = [used_turns(turns, digit) for digit in range(radix)]
    place = 0
    for ref in refs[: -len(turns)]:
        for start in range(0, ref.shape[0], unit):
            blocks = [ref[pl.ds(start + which * block, block), :] for which in range(radix)]
            rows = pl.ds(place * block, block)
            place += 1
            outs[0][rows, :] = blocks[0]
            for turn in range(1, len(turns)):
                value = None
                for which in range(radix - 1):
                    digits = [digit for digit in range(radix) if used[digit][which] == turn]
                    if len(digits) == radix:
                        value = blocks[which + 1]
                    elif digits:
                        here = chosen([int(digit in digits) for digit in range(radix)], mine, jnp.int32)
                        value = jnp.zeros_like(blocks[0]) if value is None else value
                        value = jnp.where(here == 1, blocks[which + 1], value)
                outs[turn][rows, :] = value


def by_digit(values, mine):
    value = values[0]
    for digit in range(1, len(values)):
        if values[digit] is not values[0]:
            value = jnp.where(mine == digit, values[digit], value)
    return value


def crossing_kernel(stage, block, _, beside, came, own, staying, *outs):
    staying[...] = own[...]
    turns, shift = stage
    radix = len(turns[0])
    clusters, lanes = beside.shape[1], came.shape[1]
    mine = (lax.axis_index("zone") >> shift) & (radix - 1)
    trades = (radix - 1) * block
    first = beside.shape[0] - lanes // clusters * trades
    keeps = [jnp.zeros((block, lanes), jnp.float32)]
    for which in range(radix - 1):
        tiles = [
            beside[pl.ds(first + tile * trades + which * block, block), :]
            for tile in range(lanes // clusters)
        ]
        keeps.append(jnp.concatenate(tiles, axis=1))
    comes = [came[pl.ds(which * block, block), :] for which in range(radix)]
    for turn, out in enumerate(outs, 1):
        orders = []
        for digit in range(radix):
            used = used_turns(turns, digit)
            orders.append(used.index(turn) + 1 if turn in used else 0)
        out[pl.ds(0, block), :] = by_digit([keeps[order] for order in orders], mine)
        out[pl.ds(block, block), :] = by_digit([comes[order] for order in orders], mine)


def crossing(stage, block, after, beside, came, own):
    turns = stage[0]
    out = jax.ShapeDtypeStruct((2 * block, came.shape[1]), jnp.float32)
    return pl.pallas_call(
        functools.partial(crossing_kernel, stage, block),
        out_shape=(jax.ShapeDtypeStruct(own.shape, own.dtype), *[out] * (len(turns) - 1)),
        in_specs=[VMEM] * 4,
        out_specs=(VMEM,) * len(turns),
        compiler_params=ROOM,
    )(after, beside, came, own)


def regrouped(held, stage, unit, after):
    turns = stage[0]
    lanes = held[0].shape[1]
    rows = sum(piece.shape[0] for piece in held) // len(turns[0])
    out = jax.ShapeDtypeStruct((rows, lanes), jnp.float32)
    return pl.pallas_call(
        functools.partial(regroup_kernel, stage, unit),
        out_shape=(out,) * len(turns),
        in_specs=[VMEM] * (1 + len(held)),
        out_specs=(VMEM,) * len(turns),
        compiler_params=ROOM,
    )(after, *held)


def on_device(
    state,
    source,
    jac_table,
    pattern_col,
    pattern_type,
    pseudo_step,
    zone_count,
    link_src,
    link_owner,
    link_dest,
    link_weight,
    iface_table,
):
    instances = lax.axis_size("inst")
    zones = lax.axis_size("zone")
    state_in = state[0].T
    source_t = source[0].T
    width, clusters = state_in.shape
    links = link_src.shape[1]
    slots_per = 2 * links // zones
    padded = -(-(width + 1) // LANES) * LANES
    table = coefficients(instances)
    block = jax.ShapeDtypeStruct((width, clusters), jnp.float32)

    stages = stages_of(zones, instances)
    units = [zones * slots_per]
    for turns, _ in stages:
        units.append(units[-1] // len(turns[0]))
    first = len(stages[0][0])
    crossed = len(stages) == 2 and len(stages[1][0]) == len(stages[1][0][0]) + 1
    crossed = crossed and instances >= 4 and clusters == LANES
    share = jax.ShapeDtypeStruct((units[1], padded), jnp.float32)
    shares, bundle = [share] * first, block
    if crossed:
        trades = (units[1] - units[2]) * padded // clusters
        bundle = jax.ShapeDtypeStruct((width + trades, clusters), jnp.float32)
        shares[0] = jax.ShapeDtypeStruct((units[2], padded), jnp.float32)
    state_t, *sends = pl.pallas_call(
        functools.partial(outgoing_kernel, stages, slots_per, width),
        out_shape=(bundle, *shares),
        in_specs=[HBM] * 6,
        out_specs=(VMEM,) * (1 + first),
        scratch_shapes=[pltpu.VMEM((1, links), jnp.int32)] * 4
        + [pltpu.VMEM(iface_table.shape, jnp.float32), pltpu.SemaphoreType.DMA((6,))],
        compiler_params=ROOM,
    )(
        in_hbm(state_in),
        in_hbm(link_src),
        in_hbm(link_owner.reshape(1, links)),
        in_hbm(link_dest),
        in_hbm(link_weight),
        in_hbm(iface_table),
    )

    held, held_by = [state_t], [0]
    mask = 1
    while mask < instances // 2:
        arrivals = [moved(piece, "inst", mask) for piece in held]
        held = held + arrivals
        held_by = held_by + [by ^ mask for by in held_by]
        mask *= 2
    others = []
    if instances > 1:
        (combined,) = pl.pallas_call(
            functools.partial(combine_kernel, table, held_by, instances - 1),
            out_shape=(block,),
            in_specs=[VMEM] * len(held),
            out_specs=(VMEM,),
            compiler_params=ROOM,
            cost_estimate=FREE,
        )(*held)
        others = [moved(combined, "inst", instances - 1)]

    if crossed:
        staying, came = stage_sent(sends, stages[0], True)
        pieces = crossing(stages[1], units[2], combined, held[1], came, staying)
        staying, *incoming = stage_sent(pieces, stages[1], True)
    else:
        pieces = sends
        for place, stage in enumerate(stages):
            if place:
                pieces = regrouped(pieces, stage, units[place], combined)
            pieces = stage_sent(pieces, stage)
        staying, *incoming = pieces

    kinds = jac_table.shape[0]
    codes = pattern_col.T, pattern_type.T
    half, own, none = pl.pallas_call(
        functools.partial(share_kernel, table[0]),
        out_shape=(
            jax.ShapeDtypeStruct((width, clusters), jnp.bfloat16),
            block,
            jax.ShapeDtypeStruct(codes[0].shape, jnp.int32),
        ),
        in_specs=[VMEM] * 2,
        out_specs=(VMEM,) * 3,
        compiler_params=ROOM,
    )(state_t, staying)
    products = lax.dot_general(
        jac_table.reshape(kinds * width, width),
        half,
        (((1,), (0,)), ((), ())),
        preferred_element_type=jnp.float32,
    )

    codes = codes[0] + clusters * codes[1] + none
    active = lax.broadcasted_iota(jnp.int32, (1, clusters), 1) + none[:1] < zone_count[0]
    rows = jnp.concatenate([pseudo_step, active.astype(jnp.float32)], axis=0)
    base = pl.pallas_call(
        local_kernel,
        out_shape=block,
        in_specs=[VMEM] * 4,
        out_specs=VMEM,
        compiler_params=ROOM,
        cost_estimate=FREE,
    )(codes, own, products, staying)
    base = base + source_t
    early = len(incoming) // 2
    sooner = [*held[1:], *others, *incoming[:early]]
    base = pl.pallas_call(
        functools.partial(early_kernel, table, held_by[1:], early),
        out_shape=block,
        in_specs=[VMEM] * (1 + len(sooner)),
        out_specs=VMEM,
        compiler_params=ROOM,
        cost_estimate=FREE,
    )(base, *sooner)
    incoming = incoming[early:]
    updated, residual = pl.pallas_call(
        final_kernel,
        out_shape=(block, block),
        in_specs=[VMEM] * (3 + len(incoming)),
        out_specs=(VMEM, VMEM),
        compiler_params=ROOM,
    )(base, rows, state_t, *incoming)
    return updated.T[None], residual.T[None]


def solution(mesh):
    placed = (
        P("inst", "zone", None),
        P("inst", "zone", None),
        P("zone", None, None),
        P("zone", None),
        P("zone", None),
        P("inst", "zone"),
        P("zone"),
        P("inst", "zone"),
        P("inst", "zone", None),
        P("inst", "zone"),
        P("inst", "zone"),
        P(),
    )
    return jax.shard_map(
        on_device,
        mesh=mesh,
        in_specs=placed,
        out_specs=(P("inst", "zone", None), P("inst", "zone", None)),
        check_vma=False,
    )
```

```python
import functools
import math

import jax
import jax.numpy as jnp
import numpy as np
from jax import lax
from jax.experimental import pallas as pl
from jax.experimental.pallas import tpu as pltpu
from jax.sharding import PartitionSpec as P

OMEGA = 0.25
NU = 0.1
LANES = 128
VMEM = pl.BlockSpec(memory_space=pltpu.VMEM)
SMEM = pl.BlockSpec(memory_space=pltpu.SMEM)
HBM = pl.BlockSpec(memory_space=pltpu.HBM)
FREE = pl.CostEstimate(flops=1, bytes_accessed=1, transcendentals=0)
ROOM = pltpu.CompilerParams(vmem_limit_bytes=6 << 20)


def in_hbm(value):
    return pltpu.with_memory_space_constraint(value, pltpu.HBM)


def coefficients(period):
    table = [NU * (period * period + 2) / 12.0]
    for shift in range(1, period):
        phase = math.pi * shift / period
        sign = -1.0 if shift % 2 else 1.0
        sine = math.sin(phase)
        table.append(OMEGA * sign * math.cos(phase) / sine + NU * sign / (2.0 * sine * sine))
    return [float(np.float32(entry)) for entry in table]


def chosen(table, index, dtype=jnp.float32):
    value = jnp.asarray(table[0], dtype)
    for position in range(1, len(table)):
        value = jnp.where(index == position, jnp.asarray(table[position], dtype), value)
    return value


def parts_of(value):
    high = value.astype(jnp.bfloat16)
    rest = value - high.astype(jnp.float32)
    middle = rest.astype(jnp.bfloat16)
    low = (rest - middle.astype(jnp.float32)).astype(jnp.bfloat16)
    return high, middle, low


def power_of_two(count):
    return count & (count - 1) == 0


def turns_of(radix, last):
    if radix == 4 and last:
        return ((0, 1, 2, 3), (1, 3, 2, 0), (2, 1, 0, 3), (3, 0, 1, 2), (0, 2, 3, 1))
    return tuple(tuple(digit ^ turn for digit in range(radix)) for turn in range(radix))


def stages_of(zones, instances):
    stages = []
    shift, top = 0, zones.bit_length() - 1
    while shift < top:
        bits = 1 if (top - shift) % 2 else 2
        stages.append((turns_of(1 << bits, shift and shift + bits == top and instances > 1), shift))
        shift += bits
    return stages


def used_turns(turns, digit):
    return [turn for turn in range(1, len(turns)) if turns[turn][digit] != digit]


def block_of(owner, me, stages):
    place = jnp.zeros_like(owner)
    for turns, shift in stages:
        radix = len(turns[0])
        mine = (me >> shift) & (radix - 1)
        theirs = (owner >> shift) & (radix - 1)
        order = jnp.zeros_like(owner)
        for target in range(radix):
            orders = [0] * radix
            for digit in range(radix):
                for which, turn in enumerate(used_turns(turns, digit)):
                    if turns[turn][digit] == target:
                        orders[digit] = which + 1
            order = jnp.where(theirs == target, chosen(orders, mine, jnp.int32), order)
        place = place * radix + order
    return place


def as_column(row):
    count = row.shape[1]
    lane = lax.broadcasted_iota(jnp.int32, (count, count), 1)
    sublane = lax.broadcasted_iota(jnp.int32, (count, count), 0)
    return jnp.sum(jnp.where(lane == sublane, row, jnp.zeros_like(row)), axis=1, keepdims=True)


def fetched(pairs, sems):
    copies = []
    for place, (origin, target) in enumerate(pairs):
        copy = pltpu.make_async_copy(origin, target, sems.at[place])
        copy.start()
        copies.append(copy)
    return copies


def outgoing_kernel(
    stages,
    slots_per,
    width,
    state_in,
    source_in,
    owner_in,
    dest_in,
    weight_in,
    table_in,
    state,
    *refs,
):
    *sends, source, owner, dest, weight, table, sems = refs
    cuts = sems.shape[0] - 5
    spans = [pl.ds(cut * (width // cuts), width // cuts) for cut in range(cuts)]
    copies = fetched(
        [(owner_in, owner), (source_in, source), (weight_in, weight), (dest_in, dest)]
        + [(state_in.at[span, :], state.at[span, :]) for span in spans]
        + [(table_in, table)],
        sems,
    )
    clusters = state.shape[1]
    links = owner.shape[1]
    sets = table.shape[0]
    share, lanes = sends[-1].shape
    slots = share * len(sends)
    for copy in copies[:4]:
        copy.wait()
    owners = owner[...].astype(jnp.float32)
    lane = lax.broadcasted_iota(jnp.int32, (links, links), 1)
    sublane = lax.broadcasted_iota(jnp.int32, (links, links), 0)
    earlier = (as_column(owners) == owners) & (sublane < lane)
    rank = jnp.sum(jnp.where(earlier, 1.0, 0.0), axis=0, keepdims=True).astype(jnp.int32)
    slot = block_of(owner[...], lax.axis_index("zone"), stages) * slots_per + rank
    placing = lax.broadcasted_iota(jnp.int32, (slots, links), 0) == slot

    def of_slot(row):
        return jnp.sum(
            jnp.where(placing, row[...].astype(jnp.float32) + 1.0, 0.0), axis=1, keepdims=True
        ) - 1.0

    from_cluster, to_cluster, by_set = of_slot(source), of_slot(dest), of_slot(weight)
    pick = lax.broadcasted_iota(jnp.int32, (slots, clusters), 1) == from_cluster.astype(jnp.int32)
    pick = jnp.where(pick, 1.0, 0.0).astype(jnp.bfloat16)
    choose = lax.broadcasted_iota(jnp.int32, (slots, sets), 1) == by_set.astype(jnp.int32)
    choose = jnp.where(choose, 1.0, 0.0).astype(jnp.bfloat16)
    for copy in copies[4:]:
        copy.wait()
    scales = jnp.zeros((slots, width), jnp.float32)
    for part in parts_of(table[...]):
        scales = scales + jnp.dot(choose, part, preferred_element_type=jnp.float32)
    parts = jnp.concatenate(parts_of(state[pl.ds(0, width), :]), axis=1)
    picked = lax.dot_general(
        jnp.concatenate([pick, pick, pick], axis=1),
        parts,
        (((1,), (1,)), ((), ())),
        preferred_element_type=jnp.float32,
    )
    marks = jnp.broadcast_to(to_cluster, (slots, lanes - width))
    blocks = jnp.concatenate([picked * scales, marks], axis=1)
    for place, send in enumerate(sends):
        send[...] = blocks[place * share : place * share + send.shape[0]]
    trades = share - sends[0].shape[0]
    if trades:
        for start in range(0, lanes, clusters):
            rows = pl.ds(width + start // clusters * trades, trades)
            state[rows, :] = blocks[share - trades : share, start : start + clusters]


def share_kernel(weight, state, _, half, share, none):
    value = state[pl.ds(0, half.shape[0]), :]
    half[...] = value.astype(jnp.bfloat16)
    share[...] = weight * value
    none[...] = jnp.zeros_like(none)


def landed(pieces, width, clusters):
    arrived = [piece[...] for piece in pieces]
    short = -sum(piece.shape[0] for piece in arrived) % 16
    if short:
        arrived.append(jnp.zeros((short, arrived[0].shape[1]), jnp.float32))
    arrived = jnp.concatenate(arrived, axis=0)
    target = arrived[:, width : width + 1].astype(jnp.int32)
    landing = lax.broadcasted_iota(jnp.int32, (arrived.shape[0], clusters), 1) == target
    landing = jnp.where(landing, 1.0, 0.0).astype(jnp.bfloat16)
    return lax.dot_general(
        jnp.concatenate(parts_of(arrived), axis=0),
        jnp.concatenate([landing, landing, landing], axis=0),
        (((0,), (0,)), ((), ())),
        preferred_element_type=jnp.float32,
    )[:width]


def local_kernel(codes, own, products, staying, base):
    width, clusters = base.shape
    kinds = products.shape[0] // width
    row = lax.broadcasted_iota(jnp.int32, (clusters, clusters), 0)
    high, low, counts = [], [], []
    for which in range(kinds):
        full = products[pl.ds(which * width, width), :]
        upper = full.astype(jnp.bfloat16)
        high.append(upper)
        low.append((full - upper.astype(jnp.float32)).astype(jnp.bfloat16))
        count = jnp.zeros((clusters, clusters), jnp.float32)
        for entry in range(codes.shape[0]):
            hit = row == codes[entry : entry + 1, :] - which * clusters
            count = count + jnp.where(hit, 1.0, 0.0)
        counts.append(count.astype(jnp.bfloat16))
    counts = jnp.concatenate(counts, axis=0)
    total = own[...] - landed([staying], width, clusters)
    for part in (high, low):
        total = total + jnp.dot(
            jnp.concatenate(part, axis=1), counts, preferred_element_type=jnp.float32
        )
    base[...] = total


def early_kernel(table, held_by, pieces, before, *refs):
    period = len(table)
    held = refs[: len(held_by)]
    others = refs[len(held_by) : len(refs) - pieces - 1]
    base = refs[-1]
    width, clusters = base.shape
    me = lax.axis_index("inst")
    total = before[...]
    for mask, ref in zip(held_by, held, strict=True):
        shift = (me - (me ^ mask) + period) & (period - 1)
        total = total + chosen(table, shift) * ref[pl.ds(0, width), :]
    for ref in others:
        total = total + ref[...]
    if pieces:
        total = total - landed(refs[len(refs) - pieces - 1 : -1], width, clusters)
    base[...] = total


def combine_kernel(table, held_by, mask, *refs):
    period = len(table)
    me = lax.axis_index("inst")
    *held, out = refs
    total = None
    for by, ref in zip(held_by, held, strict=True):
        shift = ((me ^ mask) - (me ^ by) + period) & (period - 1)
        term = chosen(table, shift) * ref[pl.ds(0, out.shape[0]), :]
        total = term if total is None else total + term
    out[...] = total


def final_kernel(base, rows, state, *refs):
    *incoming, updated, residual = refs
    width, clusters = base.shape
    total = base[...] - landed(incoming, width, clusters)
    kept = jnp.where(rows[1:2, :] > 0.0, total, 0.0)
    residual[...] = kept
    updated[...] = state[pl.ds(0, width), :] - rows[0:1, :] * kept


def moved(value, axis, mask):
    count = lax.axis_size(axis)
    return lax.ppermute(value, axis, [(place, place ^ mask) for place in range(count)])


def stage_sent(sends, stage, crossed=False):
    turns, shift = stage
    radix = len(turns[0])
    instances, zones = lax.axis_size("inst"), lax.axis_size("zone")
    held = [sends[0]]
    for which in range(1, len(turns)):
        pairs = []
        for inst in range(instances):
            for zone in range(zones):
                digit = (zone >> shift) & (radix - 1)
                step = turns[which][digit] - digit
                beside = inst ^ 1 if crossed or not step else inst
                pairs.append((inst * zones + zone, beside * zones + zone + (step << shift)))
        held.append(lax.ppermute(sends[which], ("inst", "zone"), pairs))
    return held


def regroup_kernel(stage, unit, _, *refs):
    turns, shift = stage
    radix = len(turns[0])
    outs = refs[-len(turns) :]
    block = unit // radix
    mine = (lax.axis_index("zone") >> shift) & (radix - 1)
    used = [used_turns(turns, digit) for digit in range(radix)]
    place = 0
    for ref in refs[: -len(turns)]:
        for start in range(0, ref.shape[0], unit):
            blocks = [ref[pl.ds(start + which * block, block), :] for which in range(radix)]
            rows = pl.ds(place * block, block)
            place += 1
            outs[0][rows, :] = blocks[0]
            for turn in range(1, len(turns)):
                value = None
                for which in range(radix - 1):
                    digits = [digit for digit in range(radix) if used[digit][which] == turn]
                    if len(digits) == radix:
                        value = blocks[which + 1]
                    elif digits:
                        here = chosen([int(digit in digits) for digit in range(radix)], mine, jnp.int32)
                        value = jnp.zeros_like(blocks[0]) if value is None else value
                        value = jnp.where(here == 1, blocks[which + 1], value)
                outs[turn][rows, :] = value


def by_digit(values, mine):
    value = values[0]
    for digit in range(1, len(values)):
        if values[digit] is not values[0]:
            value = jnp.where(mine == digit, values[digit], value)
    return value


def crossing_kernel(stage, block, _, beside, came, own, staying, *outs):
    staying[...] = own[...]
    turns, shift = stage
    radix = len(turns[0])
    clusters, lanes = beside.shape[1], came.shape[1]
    mine = (lax.axis_index("zone") >> shift) & (radix - 1)
    trades = (radix - 1) * block
    first = beside.shape[0] - lanes // clusters * trades
    keeps = [jnp.zeros((block, lanes), jnp.float32)]
    for which in range(radix - 1):
        tiles = [
            beside[pl.ds(first + tile * trades + which * block, block), :]
            for tile in range(lanes // clusters)
        ]
        keeps.append(jnp.concatenate(tiles, axis=1))
    comes = [came[pl.ds(which * block, block), :] for which in range(radix)]
    for turn, out in enumerate(outs, 1):
        orders = []
        for digit in range(radix):
            used = used_turns(turns, digit)
            orders.append(used.index(turn) + 1 if turn in used else 0)
        out[pl.ds(0, block), :] = by_digit([keeps[order] for order in orders], mine)
        out[pl.ds(block, block), :] = by_digit([comes[order] for order in orders], mine)


def crossing(stage, block, after, beside, came, own):
    turns = stage[0]
    out = jax.ShapeDtypeStruct((2 * block, came.shape[1]), jnp.float32)
    return pl.pallas_call(
        functools.partial(crossing_kernel, stage, block),
        out_shape=(jax.ShapeDtypeStruct(own.shape, own.dtype), *[out] * (len(turns) - 1)),
        in_specs=[VMEM] * 4,
        out_specs=(VMEM,) * len(turns),
        compiler_params=ROOM,
    )(after, beside, came, own)


def regrouped(held, stage, unit, after):
    turns = stage[0]
    lanes = held[0].shape[1]
    rows = sum(piece.shape[0] for piece in held) // len(turns[0])
    out = jax.ShapeDtypeStruct((rows, lanes), jnp.float32)
    return pl.pallas_call(
        functools.partial(regroup_kernel, stage, unit),
        out_shape=(out,) * len(turns),
        in_specs=[VMEM] * (1 + len(held)),
        out_specs=(VMEM,) * len(turns),
        compiler_params=ROOM,
    )(after, *held)


def on_device(
    state,
    source,
    jac_table,
    pattern_col,
    pattern_type,
    pseudo_step,
    zone_count,
    link_src,
    link_owner,
    link_dest,
    link_weight,
    iface_table,
):
    instances = lax.axis_size("inst")
    zones = lax.axis_size("zone")
    state_in = state[0].T
    source_t = source[0].T
    width, clusters = state_in.shape
    links = link_src.shape[1]
    slots_per = 2 * links // zones
    padded = -(-(width + 1) // LANES) * LANES
    table = coefficients(instances)
    block = jax.ShapeDtypeStruct((width, clusters), jnp.float32)

    stages = stages_of(zones, instances)
    units = [zones * slots_per]
    for turns, _ in stages:
        units.append(units[-1] // len(turns[0]))
    first = len(stages[0][0])
    crossed = len(stages) == 2 and len(stages[1][0]) == len(stages[1][0][0]) + 1
    crossed = crossed and instances >= 4 and clusters == LANES
    share = jax.ShapeDtypeStruct((units[1], padded), jnp.float32)
    shares, bundle = [share] * first, block
    cuts = 5 if width % 40 == 0 else 1
    if crossed:
        trades = (units[1] - units[2]) * padded // clusters
        bundle = jax.ShapeDtypeStruct((width + trades, clusters), jnp.float32)
        shares[0] = jax.ShapeDtypeStruct((units[2], padded), jnp.float32)
    state_t, *sends = pl.pallas_call(
        functools.partial(outgoing_kernel, stages, slots_per, width),
        out_shape=(bundle, *shares),
        in_specs=[HBM] * 6,
        out_specs=(VMEM,) * (1 + first),
        scratch_shapes=[pltpu.VMEM((1, links), jnp.int32)] * 4
        + [pltpu.VMEM(iface_table.shape, jnp.float32), pltpu.SemaphoreType.DMA((5 + cuts,))],
        compiler_params=ROOM,
    )(
        in_hbm(state_in),
        in_hbm(link_src),
        in_hbm(link_owner.reshape(1, links)),
        in_hbm(link_dest),
        in_hbm(link_weight),
        in_hbm(iface_table),
    )

    held, held_by = [state_t], [0]
    mask = 1
    while mask < instances // 2:
        arrivals = [moved(piece, "inst", mask) for piece in held]
        held = held + arrivals
        held_by = held_by + [by ^ mask for by in held_by]
        mask *= 2
    others = []
    if instances > 1:
        (combined,) = pl.pallas_call(
            functools.partial(combine_kernel, table, held_by, instances - 1),
            out_shape=(block,),
            in_specs=[VMEM] * len(held),
            out_specs=(VMEM,),
            compiler_params=ROOM,
            cost_estimate=FREE,
        )(*held)
        others = [moved(combined, "inst", instances - 1)]

    if crossed:
        staying, came = stage_sent(sends, stages[0], True)
        pieces = crossing(stages[1], units[2], combined, held[1], came, staying)
        staying, *incoming = stage_sent(pieces, stages[1], True)
    else:
        pieces = sends
        for place, stage in enumerate(stages):
            if place:
                pieces = regrouped(pieces, stage, units[place], combined)
            pieces = stage_sent(pieces, stage)
        staying, *incoming = pieces

    kinds = jac_table.shape[0]
    codes = pattern_col.T, pattern_type.T
    half, own, none = pl.pallas_call(
        functools.partial(share_kernel, table[0]),
        out_shape=(
            jax.ShapeDtypeStruct((width, clusters), jnp.bfloat16),
            block,
            jax.ShapeDtypeStruct(codes[0].shape, jnp.int32),
        ),
        in_specs=[VMEM] * 2,
        out_specs=(VMEM,) * 3,
        compiler_params=ROOM,
    )(state_t, staying)
    products = lax.dot_general(
        jac_table.reshape(kinds * width, width),
        half,
        (((1,), (0,)), ((), ())),
        preferred_element_type=jnp.float32,
    )

    codes = codes[0] + clusters * codes[1] + none
    active = lax.broadcasted_iota(jnp.int32, (1, clusters), 1) + none[:1] < zone_count[0]
    rows = jnp.concatenate([pseudo_step, active.astype(jnp.float32)], axis=0)
    base = pl.pallas_call(
        local_kernel,
        out_shape=block,
        in_specs=[VMEM] * 4,
        out_specs=VMEM,
        compiler_params=ROOM,
        cost_estimate=FREE,
    )(codes, own, products, staying)
    base = base + source_t
    early = len(incoming) // 2
    sooner = [*held[1:], *others, *incoming[:early]]
    base = pl.pallas_call(
        functools.partial(early_kernel, table, held_by[1:], early),
        out_shape=block,
        in_specs=[VMEM] * (1 + len(sooner)),
        out_specs=VMEM,
        compiler_params=ROOM,
        cost_estimate=FREE,
    )(base, *sooner)
    incoming = incoming[early:]
    updated, residual = pl.pallas_call(
        final_kernel,
        out_shape=(block, block),
        in_specs=[VMEM] * (3 + len(incoming)),
        out_specs=(VMEM, VMEM),
        compiler_params=ROOM,
    )(base, rows, state_t, *incoming)
    return updated.T[None], residual.T[None]


def solution(mesh):
    placed = (
        P("inst", "zone", None),
        P("inst", "zone", None),
        P("zone", None, None),
        P("zone", None),
        P("zone", None),
        P("inst", "zone"),
        P("zone"),
        P("inst", "zone"),
        P("inst", "zone", None),
        P("inst", "zone"),
        P("inst", "zone"),
        P(),
    )
    return jax.shard_map(
        on_device,
        mesh=mesh,
        in_specs=placed,
        out_specs=(P("inst", "zone", None), P("inst", "zone", None)),
        check_vma=False,
    )
```

```python
import functools
import math

import jax
import jax.numpy as jnp
import numpy as np
from jax import lax
from jax.experimental import pallas as pl
from jax.experimental.pallas import tpu as pltpu
from jax.sharding import PartitionSpec as P

OMEGA = 0.25
NU = 0.1
LANES = 128
VMEM = pl.BlockSpec(memory_space=pltpu.VMEM)
SMEM = pl.BlockSpec(memory_space=pltpu.SMEM)
HBM = pl.BlockSpec(memory_space=pltpu.HBM)
FREE = pl.CostEstimate(flops=1, bytes_accessed=1, transcendentals=0)
ROOM = pltpu.CompilerParams(vmem_limit_bytes=6 << 20)


def in_hbm(value):
    return pltpu.with_memory_space_constraint(value, pltpu.HBM)


def coefficients(period):
    table = [NU * (period * period + 2) / 12.0]
    for shift in range(1, period):
        phase = math.pi * shift / period
        sign = -1.0 if shift % 2 else 1.0
        sine = math.sin(phase)
        table.append(OMEGA * sign * math.cos(phase) / sine + NU * sign / (2.0 * sine * sine))
    return [float(np.float32(entry)) for entry in table]


def chosen(table, index, dtype=jnp.float32):
    value = jnp.asarray(table[0], dtype)
    for position in range(1, len(table)):
        value = jnp.where(index == position, jnp.asarray(table[position], dtype), value)
    return value


def parts_of(value):
    high = value.astype(jnp.bfloat16)
    return high, (value - high.astype(jnp.float32)).astype(jnp.bfloat16)


def power_of_two(count):
    return count & (count - 1) == 0


def turns_of(radix, last):
    if radix == 4 and last:
        return ((0, 1, 2, 3), (1, 3, 2, 0), (2, 1, 0, 3), (3, 0, 1, 2), (0, 2, 3, 1))
    return tuple(tuple(digit ^ turn for digit in range(radix)) for turn in range(radix))


def stages_of(zones, instances):
    stages = []
    shift, top = 0, zones.bit_length() - 1
    while shift < top:
        bits = 1 if (top - shift) % 2 else 2
        stages.append((turns_of(1 << bits, shift and shift + bits == top and instances > 1), shift))
        shift += bits
    return stages


def used_turns(turns, digit):
    return [turn for turn in range(1, len(turns)) if turns[turn][digit] != digit]


def block_of(owner, me, stages):
    place = jnp.zeros_like(owner)
    for turns, shift in stages:
        radix = len(turns[0])
        mine = (me >> shift) & (radix - 1)
        theirs = (owner >> shift) & (radix - 1)
        order = jnp.zeros_like(owner)
        for target in range(radix):
            orders = [0] * radix
            for digit in range(radix):
                for which, turn in enumerate(used_turns(turns, digit)):
                    if turns[turn][digit] == target:
                        orders[digit] = which + 1
            order = jnp.where(theirs == target, chosen(orders, mine, jnp.int32), order)
        place = place * radix + order
    return place


def as_column(row):
    count = row.shape[1]
    lane = lax.broadcasted_iota(jnp.int32, (count, count), 1)
    sublane = lax.broadcasted_iota(jnp.int32, (count, count), 0)
    return jnp.sum(jnp.where(lane == sublane, row, jnp.zeros_like(row)), axis=1, keepdims=True)


def fetched(pairs, sems):
    copies = []
    for place, (origin, target) in enumerate(pairs):
        copy = pltpu.make_async_copy(origin, target, sems.at[place])
        copy.start()
        copies.append(copy)
    return copies


def outgoing_kernel(
    stages,
    slots_per,
    width,
    state_in,
    source_in,
    owner_in,
    dest_in,
    weight_in,
    table_in,
    state,
    *refs,
):
    *sends, source, owner, dest, weight, table, sems = refs
    cuts = sems.shape[0] - 5
    spans = [pl.ds(cut * (width // cuts), width // cuts) for cut in range(cuts)]
    copies = fetched(
        [(owner_in, owner), (source_in, source), (weight_in, weight), (dest_in, dest)]
        + [(state_in.at[span, :], state.at[span, :]) for span in spans]
        + [(table_in, table)],
        sems,
    )
    clusters = state.shape[1]
    links = owner.shape[1]
    sets = table.shape[0]
    share, lanes = sends[-1].shape
    slots = share * len(sends)
    for copy in copies[:4]:
        copy.wait()
    owners = owner[...].astype(jnp.float32)
    lane = lax.broadcasted_iota(jnp.int32, (links, links), 1)
    sublane = lax.broadcasted_iota(jnp.int32, (links, links), 0)
    earlier = (as_column(owners) == owners) & (sublane < lane)
    rank = jnp.sum(jnp.where(earlier, 1.0, 0.0), axis=0, keepdims=True).astype(jnp.int32)
    slot = block_of(owner[...], lax.axis_index("zone"), stages) * slots_per + rank
    placing = lax.broadcasted_iota(jnp.int32, (slots, links), 0) == slot

    def of_slot(row):
        return jnp.sum(
            jnp.where(placing, row[...].astype(jnp.float32) + 1.0, 0.0), axis=1, keepdims=True
        ) - 1.0

    from_cluster, to_cluster, by_set = of_slot(source), of_slot(dest), of_slot(weight)
    pick = lax.broadcasted_iota(jnp.int32, (slots, clusters), 1) == from_cluster.astype(jnp.int32)
    pick = jnp.where(pick, 1.0, 0.0).astype(jnp.bfloat16)
    choose = lax.broadcasted_iota(jnp.int32, (slots, sets), 1) == by_set.astype(jnp.int32)
    choose = jnp.where(choose, 1.0, 0.0).astype(jnp.bfloat16)
    for copy in copies[4:]:
        copy.wait()
    scales = jnp.zeros((slots, width), jnp.float32)
    for part in parts_of(table[...]):
        scales = scales + jnp.dot(choose, part, preferred_element_type=jnp.float32)
    parts = jnp.concatenate(parts_of(state[pl.ds(0, width), :]), axis=1)
    picked = lax.dot_general(
        jnp.concatenate([pick, pick], axis=1),
        parts,
        (((1,), (1,)), ((), ())),
        preferred_element_type=jnp.float32,
    )
    marks = jnp.broadcast_to(to_cluster, (slots, lanes - width))
    blocks = jnp.concatenate([picked * scales, marks], axis=1)
    for place, send in enumerate(sends):
        send[...] = blocks[place * share : place * share + send.shape[0]]
    trades = share - sends[0].shape[0]
    if trades:
        for start in range(0, lanes, clusters):
            rows = pl.ds(width + start // clusters * trades, trades)
            state[rows, :] = blocks[share - trades : share, start : start + clusters]


def share_kernel(weight, state, _, half, share, none):
    value = state[pl.ds(0, half.shape[0]), :]
    half[...] = value.astype(jnp.bfloat16)
    share[...] = weight * value
    none[...] = jnp.zeros_like(none)


def landed(pieces, width, clusters):
    arrived = [piece[...] for piece in pieces]
    short = -sum(piece.shape[0] for piece in arrived) % 16
    if short:
        arrived.append(jnp.zeros((short, arrived[0].shape[1]), jnp.float32))
    arrived = jnp.concatenate(arrived, axis=0)
    target = arrived[:, width : width + 1].astype(jnp.int32)
    landing = lax.broadcasted_iota(jnp.int32, (arrived.shape[0], clusters), 1) == target
    landing = jnp.where(landing, 1.0, 0.0).astype(jnp.bfloat16)
    return lax.dot_general(
        jnp.concatenate(parts_of(arrived), axis=0),
        jnp.concatenate([landing, landing], axis=0),
        (((0,), (0,)), ((), ())),
        preferred_element_type=jnp.float32,
    )[:width]


def local_kernel(codes, own, products, staying, base):
    width, clusters = base.shape
    kinds = products.shape[0] // width
    row = lax.broadcasted_iota(jnp.int32, (clusters, clusters), 0)
    high, low, counts = [], [], []
    for which in range(kinds):
        full = products[pl.ds(which * width, width), :]
        upper = full.astype(jnp.bfloat16)
        high.append(upper)
        low.append((full - upper.astype(jnp.float32)).astype(jnp.bfloat16))
        count = jnp.zeros((clusters, clusters), jnp.float32)
        for entry in range(codes.shape[0]):
            hit = row == codes[entry : entry + 1, :] - which * clusters
            count = count + jnp.where(hit, 1.0, 0.0)
        counts.append(count.astype(jnp.bfloat16))
    counts = jnp.concatenate(counts, axis=0)
    total = own[...] - landed([staying], width, clusters)
    for part in (high, low):
        total = total + jnp.dot(
            jnp.concatenate(part, axis=1), counts, preferred_element_type=jnp.float32
        )
    base[...] = total


def early_kernel(table, held_by, pieces, before, *refs):
    period = len(table)
    held = refs[: len(held_by)]
    others = refs[len(held_by) : len(refs) - pieces - 1]
    base = refs[-1]
    width, clusters = base.shape
    me = lax.axis_index("inst")
    total = before[...]
    for mask, ref in zip(held_by, held, strict=True):
        shift = (me - (me ^ mask) + period) & (period - 1)
        total = total + chosen(table, shift) * ref[pl.ds(0, width), :]
    for ref in others:
        total = total + ref[...]
    if pieces:
        total = total - landed(refs[len(refs) - pieces - 1 : -1], width, clusters)
    base[...] = total


def combine_kernel(table, held_by, mask, *refs):
    period = len(table)
    me = lax.axis_index("inst")
    *held, out = refs
    total = None
    for by, ref in zip(held_by, held, strict=True):
        shift = ((me ^ mask) - (me ^ by) + period) & (period - 1)
        term = chosen(table, shift) * ref[pl.ds(0, out.shape[0]), :]
        total = term if total is None else total + term
    out[...] = total


def final_kernel(base, rows, state, *refs):
    *incoming, updated, residual = refs
    width, clusters = base.shape
    total = base[...] - landed(incoming, width, clusters)
    kept = jnp.where(rows[1:2, :] > 0.0, total, 0.0)
    residual[...] = kept
    updated[...] = state[pl.ds(0, width), :] - rows[0:1, :] * kept


def moved(value, axis, mask):
    count = lax.axis_size(axis)
    return lax.ppermute(value, axis, [(place, place ^ mask) for place in range(count)])


def stage_sent(sends, stage, crossed=False):
    turns, shift = stage
    radix = len(turns[0])
    instances, zones = lax.axis_size("inst"), lax.axis_size("zone")
    held = [sends[0]]
    for which in range(1, len(turns)):
        pairs = []
        for inst in range(instances):
            for zone in range(zones):
                digit = (zone >> shift) & (radix - 1)
                step = turns[which][digit] - digit
                beside = inst ^ 1 if crossed or not step else inst
                pairs.append((inst * zones + zone, beside * zones + zone + (step << shift)))
        held.append(lax.ppermute(sends[which], ("inst", "zone"), pairs))
    return held


def regroup_kernel(stage, unit, _, *refs):
    turns, shift = stage
    radix = len(turns[0])
    outs = refs[-len(turns) :]
    block = unit // radix
    mine = (lax.axis_index("zone") >> shift) & (radix - 1)
    used = [used_turns(turns, digit) for digit in range(radix)]
    place = 0
    for ref in refs[: -len(turns)]:
        for start in range(0, ref.shape[0], unit):
            blocks = [ref[pl.ds(start + which * block, block), :] for which in range(radix)]
            rows = pl.ds(place * block, block)
            place += 1
            outs[0][rows, :] = blocks[0]
            for turn in range(1, len(turns)):
                value = None
                for which in range(radix - 1):
                    digits = [digit for digit in range(radix) if used[digit][which] == turn]
                    if len(digits) == radix:
                        value = blocks[which + 1]
                    elif digits:
                        here = chosen([int(digit in digits) for digit in range(radix)], mine, jnp.int32)
                        value = jnp.zeros_like(blocks[0]) if value is None else value
                        value = jnp.where(here == 1, blocks[which + 1], value)
                outs[turn][rows, :] = value


def by_digit(values, mine):
    value = values[0]
    for digit in range(1, len(values)):
        if values[digit] is not values[0]:
            value = jnp.where(mine == digit, values[digit], value)
    return value


def crossing_kernel(stage, block, _, beside, came, own, staying, *outs):
    staying[...] = own[...]
    turns, shift = stage
    radix = len(turns[0])
    clusters, lanes = beside.shape[1], came.shape[1]
    mine = (lax.axis_index("zone") >> shift) & (radix - 1)
    trades = (radix - 1) * block
    first = beside.shape[0] - lanes // clusters * trades
    keeps = [jnp.zeros((block, lanes), jnp.float32)]
    for which in range(radix - 1):
        tiles = [
            beside[pl.ds(first + tile * trades + which * block, block), :]
            for tile in range(lanes // clusters)
        ]
        keeps.append(jnp.concatenate(tiles, axis=1))
    comes = [came[pl.ds(which * block, block), :] for which in range(radix)]
    for turn, out in enumerate(outs, 1):
        orders = []
        for digit in range(radix):
            used = used_turns(turns, digit)
            orders.append(used.index(turn) + 1 if turn in used else 0)
        out[pl.ds(0, block), :] = by_digit([keeps[order] for order in orders], mine)
        out[pl.ds(block, block), :] = by_digit([comes[order] for order in orders], mine)


def crossing(stage, block, after, beside, came, own):
    turns = stage[0]
    out = jax.ShapeDtypeStruct((2 * block, came.shape[1]), jnp.float32)
    return pl.pallas_call(
        functools.partial(crossing_kernel, stage, block),
        out_shape=(jax.ShapeDtypeStruct(own.shape, own.dtype), *[out] * (len(turns) - 1)),
        in_specs=[VMEM] * 4,
        out_specs=(VMEM,) * len(turns),
        compiler_params=ROOM,
    )(after, beside, came, own)


def regrouped(held, stage, unit, after):
    turns = stage[0]
    lanes = held[0].shape[1]
    rows = sum(piece.shape[0] for piece in held) // len(turns[0])
    out = jax.ShapeDtypeStruct((rows, lanes), jnp.float32)
    return pl.pallas_call(
        functools.partial(regroup_kernel, stage, unit),
        out_shape=(out,) * len(turns),
        in_specs=[VMEM] * (1 + len(held)),
        out_specs=(VMEM,) * len(turns),
        compiler_params=ROOM,
    )(after, *held)


def on_device(
    state,
    source,
    jac_table,
    pattern_col,
    pattern_type,
    pseudo_step,
    zone_count,
    link_src,
    link_owner,
    link_dest,
    link_weight,
    iface_table,
):
    instances = lax.axis_size("inst")
    zones = lax.axis_size("zone")
    state_in = state[0].T
    source_t = source[0].T
    width, clusters = state_in.shape
    links = link_src.shape[1]
    slots_per = 2 * links // zones
    padded = -(-(width + 1) // LANES) * LANES
    table = coefficients(instances)
    block = jax.ShapeDtypeStruct((width, clusters), jnp.float32)

    stages = stages_of(zones, instances)
    units = [zones * slots_per]
    for turns, _ in stages:
        units.append(units[-1] // len(turns[0]))
    first = len(stages[0][0])
    crossed = len(stages) == 2 and len(stages[1][0]) == len(stages[1][0][0]) + 1
    crossed = crossed and instances >= 4 and clusters == LANES
    share = jax.ShapeDtypeStruct((units[1], padded), jnp.float32)
    shares, bundle = [share] * first, block
    cuts = 5 if width % 40 == 0 else 1
    if crossed:
        trades = (units[1] - units[2]) * padded // clusters
        bundle = jax.ShapeDtypeStruct((width + trades, clusters), jnp.float32)
        shares[0] = jax.ShapeDtypeStruct((units[2], padded), jnp.float32)
    state_t, *sends = pl.pallas_call(
        functools.partial(outgoing_kernel, stages, slots_per, width),
        out_shape=(bundle, *shares),
        in_specs=[HBM] * 6,
        out_specs=(VMEM,) * (1 + first),
        scratch_shapes=[pltpu.VMEM((1, links), jnp.int32)] * 4
        + [pltpu.VMEM(iface_table.shape, jnp.float32), pltpu.SemaphoreType.DMA((5 + cuts,))],
        compiler_params=ROOM,
    )(
        in_hbm(state_in),
        in_hbm(link_src),
        in_hbm(link_owner.reshape(1, links)),
        in_hbm(link_dest),
        in_hbm(link_weight),
        in_hbm(iface_table),
    )

    held, held_by = [state_t], [0]
    mask = 1
    while mask < instances // 2:
        arrivals = [moved(piece, "inst", mask) for piece in held]
        held = held + arrivals
        held_by = held_by + [by ^ mask for by in held_by]
        mask *= 2
    others = []
    if instances > 1:
        (combined,) = pl.pallas_call(
            functools.partial(combine_kernel, table, held_by, instances - 1),
            out_shape=(block,),
            in_specs=[VMEM] * len(held),
            out_specs=(VMEM,),
            compiler_params=ROOM,
            cost_estimate=FREE,
        )(*held)
        others = [moved(combined, "inst", instances - 1)]

    if crossed:
        staying, came = stage_sent(sends, stages[0], True)
        pieces = crossing(stages[1], units[2], combined, held[1], came, staying)
        staying, *incoming = stage_sent(pieces, stages[1], True)
    else:
        pieces = sends
        for place, stage in enumerate(stages):
            if place:
                pieces = regrouped(pieces, stage, units[place], combined)
            pieces = stage_sent(pieces, stage)
        staying, *incoming = pieces

    kinds = jac_table.shape[0]
    codes = pattern_col.T, pattern_type.T
    half, own, none = pl.pallas_call(
        functools.partial(share_kernel, table[0]),
        out_shape=(
            jax.ShapeDtypeStruct((width, clusters), jnp.bfloat16),
            block,
            jax.ShapeDtypeStruct(codes[0].shape, jnp.int32),
        ),
        in_specs=[VMEM] * 2,
        out_specs=(VMEM,) * 3,
        compiler_params=ROOM,
    )(state_t, staying)
    products = lax.dot_general(
        jac_table.reshape(kinds * width, width),
        half,
        (((1,), (0,)), ((), ())),
        preferred_element_type=jnp.float32,
    )

    codes = codes[0] + clusters * codes[1] + none
    active = lax.broadcasted_iota(jnp.int32, (1, clusters), 1) + none[:1] < zone_count[0]
    rows = jnp.concatenate([pseudo_step, active.astype(jnp.float32)], axis=0)
    base = pl.pallas_call(
        local_kernel,
        out_shape=block,
        in_specs=[VMEM] * 4,
        out_specs=VMEM,
        compiler_params=ROOM,
        cost_estimate=FREE,
    )(codes, own, products, staying)
    base = base + source_t
    early = len(incoming) // 2
    sooner = [*held[1:], *others, *incoming[:early]]
    base = pl.pallas_call(
        functools.partial(early_kernel, table, held_by[1:], early),
        out_shape=block,
        in_specs=[VMEM] * (1 + len(sooner)),
        out_specs=VMEM,
        compiler_params=ROOM,
        cost_estimate=FREE,
    )(base, *sooner)
    incoming = incoming[early:]
    updated, residual = pl.pallas_call(
        final_kernel,
        out_shape=(block, block),
        in_specs=[VMEM] * (3 + len(incoming)),
        out_specs=(VMEM, VMEM),
        compiler_params=ROOM,
    )(base, rows, state_t, *incoming)
    return updated.T[None], residual.T[None]


def solution(mesh):
    placed = (
        P("inst", "zone", None),
        P("inst", "zone", None),
        P("zone", None, None),
        P("zone", None),
        P("zone", None),
        P("inst", "zone"),
        P("zone"),
        P("inst", "zone"),
        P("inst", "zone", None),
        P("inst", "zone"),
        P("inst", "zone"),
        P(),
    )
    return jax.shard_map(
        on_device,
        mesh=mesh,
        in_specs=placed,
        out_specs=(P("inst", "zone", None), P("inst", "zone", None)),
        check_vma=False,
    )
```

```python
import functools
import math

import jax
import jax.numpy as jnp
import numpy as np
from jax import lax
from jax.experimental import pallas as pl
from jax.experimental.pallas import tpu as pltpu
from jax.sharding import PartitionSpec as P

OMEGA = 0.25
NU = 0.1
LANES = 128
VMEM = pl.BlockSpec(memory_space=pltpu.VMEM)
SMEM = pl.BlockSpec(memory_space=pltpu.SMEM)
HBM = pl.BlockSpec(memory_space=pltpu.HBM)
FREE = pl.CostEstimate(flops=1, bytes_accessed=1, transcendentals=0)
ROOM = pltpu.CompilerParams(vmem_limit_bytes=6 << 20)


def in_hbm(value):
    return pltpu.with_memory_space_constraint(value, pltpu.HBM)


def coefficients(period):
    table = [NU * (period * period + 2) / 12.0]
    for shift in range(1, period):
        phase = math.pi * shift / period
        sign = -1.0 if shift % 2 else 1.0
        sine = math.sin(phase)
        table.append(OMEGA * sign * math.cos(phase) / sine + NU * sign / (2.0 * sine * sine))
    return [float(np.float32(entry)) for entry in table]


def chosen(table, index, dtype=jnp.float32):
    value = jnp.asarray(table[0], dtype)
    for position in range(1, len(table)):
        value = jnp.where(index == position, jnp.asarray(table[position], dtype), value)
    return value


def parts_of(value):
    high = value.astype(jnp.bfloat16)
    return high, (value - high.astype(jnp.float32)).astype(jnp.bfloat16)


def power_of_two(count):
    return count & (count - 1) == 0


def turns_of(radix, last):
    if radix == 4 and last:
        return ((0, 1, 2, 3), (1, 3, 2, 0), (2, 1, 0, 3), (3, 0, 1, 2), (0, 2, 3, 1))
    return tuple(tuple(digit ^ turn for digit in range(radix)) for turn in range(radix))


def stages_of(zones, instances):
    stages = []
    shift, top = 0, zones.bit_length() - 1
    while shift < top:
        bits = 1 if (top - shift) % 2 else 2
        stages.append((turns_of(1 << bits, shift and shift + bits == top and instances > 1), shift))
        shift += bits
    return stages


def used_turns(turns, digit):
    return [turn for turn in range(1, len(turns)) if turns[turn][digit] != digit]


def block_of(owner, me, stages):
    place = jnp.zeros_like(owner)
    for turns, shift in stages:
        radix = len(turns[0])
        mine = (me >> shift) & (radix - 1)
        theirs = (owner >> shift) & (radix - 1)
        order = jnp.zeros_like(owner)
        for target in range(radix):
            orders = [0] * radix
            for digit in range(radix):
                for which, turn in enumerate(used_turns(turns, digit)):
                    if turns[turn][digit] == target:
                        orders[digit] = which + 1
            order = jnp.where(theirs == target, chosen(orders, mine, jnp.int32), order)
        place = place * radix + order
    return place


def as_column(row):
    count = row.shape[1]
    lane = lax.broadcasted_iota(jnp.int32, (count, count), 1)
    sublane = lax.broadcasted_iota(jnp.int32, (count, count), 0)
    return jnp.sum(jnp.where(lane == sublane, row, jnp.zeros_like(row)), axis=1, keepdims=True)


def fetched(pairs, sems):
    copies = []
    for place, (origin, target) in enumerate(pairs):
        copy = pltpu.make_async_copy(origin, target, sems.at[place])
        copy.start()
        copies.append(copy)
    return copies


def outgoing_kernel(
    stages,
    slots_per,
    width,
    state_in,
    source_in,
    owner_in,
    dest_in,
    weight_in,
    table_in,
    state,
    *refs,
):
    *sends, source, owner, dest, weight, table, sems = refs
    cuts = sems.shape[0] - 5
    spans = [pl.ds(cut * (width // cuts), width // cuts) for cut in range(cuts)]
    copies = fetched(
        [(owner_in, owner), (source_in, source), (weight_in, weight), (dest_in, dest)]
        + [(state_in.at[span, :], state.at[span, :]) for span in spans]
        + [(table_in, table)],
        sems,
    )
    clusters = state.shape[1]
    links = owner.shape[1]
    sets = table.shape[0]
    share, lanes = sends[-1].shape
    slots = share * len(sends)
    for copy in copies[:4]:
        copy.wait()
    owners = owner[...].astype(jnp.float32)
    lane = lax.broadcasted_iota(jnp.int32, (links, links), 1)
    sublane = lax.broadcasted_iota(jnp.int32, (links, links), 0)
    earlier = (as_column(owners) == owners) & (sublane < lane)
    rank = jnp.sum(jnp.where(earlier, 1.0, 0.0), axis=0, keepdims=True).astype(jnp.int32)
    slot = block_of(owner[...], lax.axis_index("zone"), stages) * slots_per + rank
    placing = lax.broadcasted_iota(jnp.int32, (slots, links), 0) == slot

    def of_slot(row):
        return jnp.sum(
            jnp.where(placing, row[...].astype(jnp.float32) + 1.0, 0.0), axis=1, keepdims=True
        ) - 1.0

    from_cluster, to_cluster, by_set = of_slot(source), of_slot(dest), of_slot(weight)
    pick = lax.broadcasted_iota(jnp.int32, (slots, clusters), 1) == from_cluster.astype(jnp.int32)
    pick = jnp.where(pick, 1.0, 0.0).astype(jnp.bfloat16)
    choose = lax.broadcasted_iota(jnp.int32, (slots, sets), 1) == by_set.astype(jnp.int32)
    choose = jnp.where(choose, 1.0, 0.0).astype(jnp.bfloat16)
    for copy in copies[4:]:
        copy.wait()
    scales = jnp.zeros((slots, width), jnp.float32)
    for part in parts_of(table[...]):
        scales = scales + jnp.dot(choose, part, preferred_element_type=jnp.float32)
    parts = jnp.concatenate(parts_of(state[pl.ds(0, width), :]), axis=1)
    picked = lax.dot_general(
        jnp.concatenate([pick, pick], axis=1),
        parts,
        (((1,), (1,)), ((), ())),
        preferred_element_type=jnp.float32,
    )
    marks = jnp.broadcast_to(to_cluster, (slots, lanes - width))
    blocks = jnp.concatenate([picked * scales, marks], axis=1)
    for place, send in enumerate(sends):
        send[...] = blocks[place * share : place * share + send.shape[0]]
    trades = share - sends[0].shape[0]
    if trades:
        for start in range(0, lanes, clusters):
            rows = pl.ds(width + start // clusters * trades, trades)
            state[rows, :] = blocks[share - trades : share, start : start + clusters]


def share_kernel(weight, state, _, half, share, none):
    value = state[pl.ds(0, half.shape[0]), :]
    half[...] = value.astype(jnp.bfloat16)
    share[...] = weight * value
    none[...] = jnp.zeros_like(none)


def landed(pieces, width, clusters):
    arrived = [piece[...] for piece in pieces]
    short = -sum(piece.shape[0] for piece in arrived) % 16
    if short:
        arrived.append(jnp.zeros((short, arrived[0].shape[1]), jnp.float32))
    arrived = jnp.concatenate(arrived, axis=0)
    target = arrived[:, width : width + 1]
    cluster = lax.broadcasted_iota(jnp.int32, (arrived.shape[0], clusters), 1)
    landing = cluster.astype(jnp.float32) == target
    landing = jnp.where(landing, 1.0, 0.0).astype(jnp.bfloat16)
    return lax.dot_general(
        jnp.concatenate(parts_of(arrived), axis=0),
        jnp.concatenate([landing, landing], axis=0),
        (((0,), (0,)), ((), ())),
        preferred_element_type=jnp.float32,
    )[:width]


def local_kernel(codes, own, products, staying, base):
    width, clusters = base.shape
    kinds = products.shape[0] // width
    row = lax.broadcasted_iota(jnp.int32, (clusters, clusters), 0)
    high, low, counts = [], [], []
    for which in range(kinds):
        full = products[pl.ds(which * width, width), :]
        upper = full.astype(jnp.bfloat16)
        high.append(upper)
        low.append((full - upper.astype(jnp.float32)).astype(jnp.bfloat16))
        count = jnp.zeros((clusters, clusters), jnp.float32)
        for entry in range(codes.shape[0]):
            hit = row == codes[entry : entry + 1, :] - which * clusters
            count = count + jnp.where(hit, 1.0, 0.0)
        counts.append(count.astype(jnp.bfloat16))
    counts = jnp.concatenate(counts, axis=0)
    total = own[...] - landed([staying], width, clusters)
    for part in (high, low):
        total = total + jnp.dot(
            jnp.concatenate(part, axis=1), counts, preferred_element_type=jnp.float32
        )
    base[...] = total


def early_kernel(table, held_by, pieces, before, *refs):
    period = len(table)
    held = refs[: len(held_by)]
    others = refs[len(held_by) : len(refs) - pieces - 1]
    base = refs[-1]
    width, clusters = base.shape
    me = lax.axis_index("inst")
    total = before[...]
    for mask, ref in zip(held_by, held, strict=True):
        shift = (me - (me ^ mask) + period) & (period - 1)
        total = total + chosen(table, shift) * ref[pl.ds(0, width), :]
    for ref in others:
        total = total + ref[...]
    if pieces:
        total = total - landed(refs[len(refs) - pieces - 1 : -1], width, clusters)
    base[...] = total


def combine_kernel(table, held_by, mask, *refs):
    period = len(table)
    me = lax.axis_index("inst")
    *held, out = refs
    total = None
    for by, ref in zip(held_by, held, strict=True):
        shift = ((me ^ mask) - (me ^ by) + period) & (period - 1)
        term = chosen(table, shift) * ref[pl.ds(0, out.shape[0]), :]
        total = term if total is None else total + term
    out[...] = total


def final_kernel(base, rows, state, *refs):
    *incoming, updated, residual = refs
    width, clusters = base.shape
    total = base[...] - landed(incoming, width, clusters)
    kept = jnp.where(rows[1:2, :] > 0.0, total, 0.0)
    residual[...] = kept
    updated[...] = state[pl.ds(0, width), :] - rows[0:1, :] * kept


def moved(value, axis, mask):
    count = lax.axis_size(axis)
    return lax.ppermute(value, axis, [(place, place ^ mask) for place in range(count)])


def stage_sent(sends, stage, crossed=False):
    turns, shift = stage
    radix = len(turns[0])
    instances, zones = lax.axis_size("inst"), lax.axis_size("zone")
    held = [sends[0]]
    for which in range(1, len(turns)):
        pairs = []
        for inst in range(instances):
            for zone in range(zones):
                digit = (zone >> shift) & (radix - 1)
                step = turns[which][digit] - digit
                beside = inst ^ 1 if crossed or not step else inst
                pairs.append((inst * zones + zone, beside * zones + zone + (step << shift)))
        held.append(lax.ppermute(sends[which], ("inst", "zone"), pairs))
    return held


def regroup_kernel(stage, unit, _, *refs):
    turns, shift = stage
    radix = len(turns[0])
    outs = refs[-len(turns) :]
    block = unit // radix
    mine = (lax.axis_index("zone") >> shift) & (radix - 1)
    used = [used_turns(turns, digit) for digit in range(radix)]
    place = 0
    for ref in refs[: -len(turns)]:
        for start in range(0, ref.shape[0], unit):
            blocks = [ref[pl.ds(start + which * block, block), :] for which in range(radix)]
            rows = pl.ds(place * block, block)
            place += 1
            outs[0][rows, :] = blocks[0]
            for turn in range(1, len(turns)):
                value = None
                for which in range(radix - 1):
                    digits = [digit for digit in range(radix) if used[digit][which] == turn]
                    if len(digits) == radix:
                        value = blocks[which + 1]
                    elif digits:
                        here = chosen([int(digit in digits) for digit in range(radix)], mine, jnp.int32)
                        value = jnp.zeros_like(blocks[0]) if value is None else value
                        value = jnp.where(here == 1, blocks[which + 1], value)
                outs[turn][rows, :] = value


def by_digit(values, mine):
    value = values[0]
    for digit in range(1, len(values)):
        if values[digit] is not values[0]:
            value = jnp.where(mine == digit, values[digit], value)
    return value


def crossing_kernel(stage, block, _, beside, came, own, staying, *outs):
    staying[...] = own[...]
    turns, shift = stage
    radix = len(turns[0])
    clusters, lanes = beside.shape[1], came.shape[1]
    mine = (lax.axis_index("zone") >> shift) & (radix - 1)
    trades = (radix - 1) * block
    first = beside.shape[0] - lanes // clusters * trades
    keeps = [jnp.zeros((block, lanes), jnp.float32)]
    for which in range(radix - 1):
        tiles = [
            beside[pl.ds(first + tile * trades + which * block, block), :]
            for tile in range(lanes // clusters)
        ]
        keeps.append(jnp.concatenate(tiles, axis=1))
    comes = [came[pl.ds(which * block, block), :] for which in range(radix)]
    for turn, out in enumerate(outs, 1):
        orders = []
        for digit in range(radix):
            used = used_turns(turns, digit)
            orders.append(used.index(turn) + 1 if turn in used else 0)
        out[pl.ds(0, block), :] = by_digit([keeps[order] for order in orders], mine)
        out[pl.ds(block, block), :] = by_digit([comes[order] for order in orders], mine)


def crossing(stage, block, after, beside, came, own):
    turns = stage[0]
    out = jax.ShapeDtypeStruct((2 * block, came.shape[1]), jnp.float32)
    return pl.pallas_call(
        functools.partial(crossing_kernel, stage, block),
        out_shape=(jax.ShapeDtypeStruct(own.shape, own.dtype), *[out] * (len(turns) - 1)),
        in_specs=[VMEM] * 4,
        out_specs=(VMEM,) * len(turns),
        compiler_params=ROOM,
    )(after, beside, came, own)


def regrouped(held, stage, unit, after):
    turns = stage[0]
    lanes = held[0].shape[1]
    rows = sum(piece.shape[0] for piece in held) // len(turns[0])
    out = jax.ShapeDtypeStruct((rows, lanes), jnp.float32)
    return pl.pallas_call(
        functools.partial(regroup_kernel, stage, unit),
        out_shape=(out,) * len(turns),
        in_specs=[VMEM] * (1 + len(held)),
        out_specs=(VMEM,) * len(turns),
        compiler_params=ROOM,
    )(after, *held)


def on_device(
    state,
    source,
    jac_table,
    pattern_col,
    pattern_type,
    pseudo_step,
    zone_count,
    link_src,
    link_owner,
    link_dest,
    link_weight,
    iface_table,
):
    instances = lax.axis_size("inst")
    zones = lax.axis_size("zone")
    state_in = state[0].T
    source_t = source[0].T
    width, clusters = state_in.shape
    links = link_src.shape[1]
    slots_per = 2 * links // zones
    padded = -(-(width + 1) // LANES) * LANES
    table = coefficients(instances)
    block = jax.ShapeDtypeStruct((width, clusters), jnp.float32)

    stages = stages_of(zones, instances)
    units = [zones * slots_per]
    for turns, _ in stages:
        units.append(units[-1] // len(turns[0]))
    first = len(stages[0][0])
    crossed = len(stages) == 2 and len(stages[1][0]) == len(stages[1][0][0]) + 1
    crossed = crossed and instances >= 4 and clusters == LANES
    share = jax.ShapeDtypeStruct((units[1], padded), jnp.float32)
    shares, bundle = [share] * first, block
    cuts = 5 if width % 40 == 0 else 1
    if crossed:
        trades = (units[1] - units[2]) * padded // clusters
        bundle = jax.ShapeDtypeStruct((width + trades, clusters), jnp.float32)
        shares[0] = jax.ShapeDtypeStruct((units[2], padded), jnp.float32)
    state_t, *sends = pl.pallas_call(
        functools.partial(outgoing_kernel, stages, slots_per, width),
        out_shape=(bundle, *shares),
        in_specs=[HBM] * 6,
        out_specs=(VMEM,) * (1 + first),
        scratch_shapes=[pltpu.VMEM((1, links), jnp.int32)] * 4
        + [pltpu.VMEM(iface_table.shape, jnp.float32), pltpu.SemaphoreType.DMA((5 + cuts,))],
        compiler_params=ROOM,
    )(
        in_hbm(state_in),
        in_hbm(link_src),
        in_hbm(link_owner.reshape(1, links)),
        in_hbm(link_dest),
        in_hbm(link_weight),
        in_hbm(iface_table),
    )

    held, held_by = [state_t], [0]
    mask = 1
    while mask < instances // 2:
        arrivals = [moved(piece, "inst", mask) for piece in held]
        held = held + arrivals
        held_by = held_by + [by ^ mask for by in held_by]
        mask *= 2
    others = []
    if instances > 1:
        (combined,) = pl.pallas_call(
            functools.partial(combine_kernel, table, held_by, instances - 1),
            out_shape=(block,),
            in_specs=[VMEM] * len(held),
            out_specs=(VMEM,),
            compiler_params=ROOM,
            cost_estimate=FREE,
        )(*held)
        others = [moved(combined, "inst", instances - 1)]

    if crossed:
        staying, came = stage_sent(sends, stages[0], True)
        pieces = crossing(stages[1], units[2], combined, held[1], came, staying)
        staying, *incoming = stage_sent(pieces, stages[1], True)
    else:
        pieces = sends
        for place, stage in enumerate(stages):
            if place:
                pieces = regrouped(pieces, stage, units[place], combined)
            pieces = stage_sent(pieces, stage)
        staying, *incoming = pieces

    kinds = jac_table.shape[0]
    codes = pattern_col.T, pattern_type.T
    half, own, none = pl.pallas_call(
        functools.partial(share_kernel, table[0]),
        out_shape=(
            jax.ShapeDtypeStruct((width, clusters), jnp.bfloat16),
            block,
            jax.ShapeDtypeStruct(codes[0].shape, jnp.int32),
        ),
        in_specs=[VMEM] * 2,
        out_specs=(VMEM,) * 3,
        compiler_params=ROOM,
    )(state_t, staying)
    products = lax.dot_general(
        jac_table.reshape(kinds * width, width),
        half,
        (((1,), (0,)), ((), ())),
        preferred_element_type=jnp.float32,
    )

    codes = codes[0] + clusters * codes[1] + none
    active = lax.broadcasted_iota(jnp.int32, (1, clusters), 1) + none[:1] < zone_count[0]
    rows = jnp.concatenate([pseudo_step, active.astype(jnp.float32)], axis=0)
    base = pl.pallas_call(
        local_kernel,
        out_shape=block,
        in_specs=[VMEM] * 4,
        out_specs=VMEM,
        compiler_params=ROOM,
        cost_estimate=FREE,
    )(codes, own, products, staying)
    base = base + source_t
    early = len(incoming) // 2
    sooner = [*held[1:], *others, *incoming[:early]]
    base = pl.pallas_call(
        functools.partial(early_kernel, table, held_by[1:], early),
        out_shape=block,
        in_specs=[VMEM] * (1 + len(sooner)),
        out_specs=VMEM,
        compiler_params=ROOM,
        cost_estimate=FREE,
    )(base, *sooner)
    incoming = incoming[early:]
    updated, residual = pl.pallas_call(
        final_kernel,
        out_shape=(block, block),
        in_specs=[VMEM] * (3 + len(incoming)),
        out_specs=(VMEM, VMEM),
        compiler_params=ROOM,
    )(base, rows, state_t, *incoming)
    return updated.T[None], residual.T[None]


def solution(mesh):
    placed = (
        P("inst", "zone", None),
        P("inst", "zone", None),
        P("zone", None, None),
        P("zone", None),
        P("zone", None),
        P("inst", "zone"),
        P("zone"),
        P("inst", "zone"),
        P("inst", "zone", None),
        P("inst", "zone"),
        P("inst", "zone"),
        P(),
    )
    return jax.shard_map(
        on_device,
        mesh=mesh,
        in_specs=placed,
        out_specs=(P("inst", "zone", None), P("inst", "zone", None)),
        check_vma=False,
    )
```
